32 devices in a mesh: band: 4 (over x, core), dp: 8 (over z, y).
Axes of the slice: x: 2, y: 2, z: 4, core: 2. Of those that a mesh axis runs over, the one named last changes fastest.
Arguments:
- pixels: bfloat16 [8, 32768, 64], P('band', 'dp'), may hold values from -6 to 6
- band_ids: int32 [8, 8], P('dp'), may hold values from 0 to 31
- band_mask: int32 [8, 8], P('dp'), may hold values 0 or 1
- sensor_tags: int32 [8], P('dp'), may hold values from 0 to 5
- segment_ids: int32 [32, 1024], P(('dp', 'band')), may hold values from 0 to 3, never falling along the last dimension, each value on 1 to 512 neighbouring positions
- wave_table: bfloat16 [32, 128], replicated, may hold values from -6 to 6
- gen_w1: bfloat16 [128, 128], replicated, may hold values from -0.5 to 0.5
- gen_w2: bfloat16 [128, 49152], replicated, may hold values from -0.0234375 to 0.0234375
- sensor_table: bfloat16 [6, 768], replicated, may hold values from -3 to 3
- ln1_gain: float32 [768], replicated, may hold values from 0.5 to 1.5
- qkv_weight: bfloat16 [768, 2304], replicated, may hold values from -0.21875 to 0.21875
- proj_weight: bfloat16 [768, 768], replicated, may hold values from -0.875 to 0.875
- ln2_gain: float32 [768], replicated, may hold values from 0.5 to 1.5
- fc1_weight: bfloat16 [768, 3072], replicated, may hold values from -0.21875 to 0.21875
- fc2_weight: bfloat16 [3072, 768], replicated, may hold values from -0.109375 to 0.109375
- out_grad: bfloat16 [32768, 768], P(('dp', 'band')), may hold values from -6 to 6
Outputs:
- encoded: float32 [32768, 768], P(('dp', 'band'))
- pixel_grad: float32 [8, 32768, 64], P('band', 'dp')
- wave_table_grad: float32 [32, 128], replicated
- gen_w1_grad: float32 [128, 128], replicated
- gen_w2_grad: float32 [128, 49152], P(None, ('band', 'dp'))
- sensor_grad: float32 [6, 768], replicated
- ln1_gain_grad: float32 [768], replicated
- qkv_grad: float32 [768, 2304], P(None, ('band', 'dp'))
- proj_grad: float32 [768, 768], P(None, ('band', 'dp'))
- ln2_gain_grad: float32 [768], replicated
- fc1_grad: float32 [768, 3072], P(None, ('band', 'dp'))
- fc2_grad: float32 [3072, 768], P(('band', 'dp'))
The draws below stay inside these ranges and needn't reach their ends.
Inputs may be any that keep to these rules, and one draw needn't show every extreme that they name: `segment_ids`: chip numbers never fall along a sequence; a chip holds 1 to 512 patches, one exactly 512.
All inputs are finite; a program needn't handle non-finite values. No bound on the sum of `band_mask` on one device may be relied on, other than what follows from the above.
Results may differ from the reference program's by a relative error of at most 0.019.
Values may be sent and summed in bfloat16 or wider, within the bound.
No kernel may reach another device: no remote copies, remote signals or barrier semaphores. Data moves between devices by JAX's collectives and lax.ppermute only.
A program may use at most 320 MiB of HBM per device.

```python
import math
import jax
import jax.numpy as jnp
import numpy as np
from jax import lax

D = 768
HEADS = 12
HD = 64
FF = 3072
PIX = 64
WG = 128
WAVES = 32
SENSORS = 6
LEN = 1024
SEGS = 4
MOST = 512
GROUP_TOK = 4096
BANDS = 8
GROUPS = 8
TOKENS = 32768
SEQS = 32


def plant(values, rng, low, top_value):
    dims = values.shape
    index_at = [jax.random.randint(jax.random.fold_in(rng, axis), (), 0, dims[axis]) for axis in range(len(dims))]
    values = values.at[tuple(index_at)].set(low)
    longest = dims.index(max(dims))
    index_at[longest] = (index_at[longest] + 1) % dims[longest]
    return values.at[tuple(index_at)].set(top_value)


def steps_of(key, shape, split, smallest, top_value):
    level, own = 1.0, jax.random.fold_in(key, 6)
    for dim, blocks in split:
        heights = jnp.exp(jax.random.uniform(jax.random.fold_in(own, dim), (blocks,), jnp.float32, smallest / len(split), top_value / len(split)))
        level = level * jnp.repeat(heights, shape[dim] // blocks).reshape([-1 if axis == dim else 1 for axis in range(len(shape))])
    return level


def length_profile(count, total, reach, skew):
    portions = [(1 << 20) // math.isqrt(rank ** skew) + 1 for rank in range(2, count + 1)]
    spare, given = total - reach - (count - 1), [1] * (count - 1)
    while spare > 0:
        candidates = [i for i in range(count - 1) if given[i] < reach]
        whole, remaining = sum([portions[i] for i in candidates]), spare
        for i in candidates:
            more = min(reach - given[i], max(1, remaining * portions[i] // whole), spare)
            given[i] = given[i] + more
            spare = spare - more
    return np.array([reach] + given)


def uneven(key, number_of, total, reach, skew):
    if number_of == 2:
        one = jax.random.randint(key, (), max(1, total - reach), min(reach, total - 1) + 1)
        return jnp.stack([one, total - one])
    tallies = jnp.asarray(length_profile(number_of, total, reach, skew), jnp.int32)
    twos = (number_of - 1) // 2
    donor, sink = tallies[1:1 + 2 * twos:2], tallies[2:2 + 2 * twos:2]
    margin = jnp.minimum(donor - 1, reach - sink)
    shifted = jax.random.randint(jax.random.fold_in(key, 1), (twos,), 0, 1 << 20) % (margin + 1)
    tallies = tallies.at[1:1 + 2 * twos:2].set(donor - shifted).at[2:2 + 2 * twos:2].set(sink + shifted)
    return tallies[jax.random.permutation(jax.random.fold_in(key, 2), number_of)]


def centred(stream_key, extent, scale, bound, shards=(), held_as=jnp.bfloat16):
    entries = scale * jax.random.normal(stream_key, extent, jnp.float32)
    if shards:
        entries = entries * steps_of(stream_key, extent, shards, -0.22, 0.18)
    return jnp.clip(entries, -bound, bound).astype(held_as)


def setup_inputs(seed: int = 0) -> dict:
    arg_keys = jax.random.split(jax.random.key(seed), 17)
    pixels = centred(arg_keys[0], (BANDS, TOKENS, PIX), 1.0, 6.0, ((0, 4), (1, 8)))
    band_ids = plant(jax.random.randint(arg_keys[1], (GROUPS, BANDS), 0, WAVES), jax.random.fold_in(arg_keys[1], 1), 0, WAVES - 1).astype(jnp.int32)
    band_mask = plant((jax.random.randint(arg_keys[2], (GROUPS, BANDS), 0, 4) < 3).astype(jnp.int32), jax.random.fold_in(arg_keys[2], 1), 0, 1)
    sensor_tags = plant(jax.random.randint(arg_keys[3], (GROUPS,), 0, SENSORS), jax.random.fold_in(arg_keys[3], 1), 0, SENSORS - 1).astype(jnp.int32)
    segment_ids = jax.vmap(lambda own: jnp.searchsorted(jnp.cumsum(uneven(own, SEGS, LEN, MOST, 2)), jnp.arange(LEN), side="right"))(jax.random.split(arg_keys[4], SEQS)).reshape((SEQS, LEN)).astype(jnp.int32)
    wave_table = centred(arg_keys[5], (WAVES, WG), 1.0, 6.0)
    gen_w1 = centred(arg_keys[6], (WG, WG), WG ** -0.5, 0.5)
    gen_w2 = centred(arg_keys[7], (WG, PIX * D), (WG * PIX * BANDS) ** -0.5, 0.0234375)
    sensor_table = centred(arg_keys[8], (SENSORS, D), 0.5, 3.0)
    ln1_gain = jnp.clip(1.0 + 0.1 * jax.random.normal(arg_keys[9], (D,), jnp.float32), 0.5, 1.5)
    qkv_weight = centred(arg_keys[10], (D, 3 * D), D ** -0.5, 0.21875)
    proj_weight = centred(arg_keys[11], (D, D), (D // 16) ** -0.5, 0.875)
    ln2_gain = jnp.clip(1.0 + 0.1 * jax.random.normal(arg_keys[12], (D,), jnp.float32), 0.5, 1.5)
    fc1_weight = centred(arg_keys[13], (D, FF), D ** -0.5, 0.21875)
    fc2_weight = centred(arg_keys[14], (FF, D), FF ** -0.5, 0.109375)
    out_grad = centred(arg_keys[15], (TOKENS, D), 1.0, 6.0, ((0, 32),))
    return {"pixels": pixels, "band_ids": band_ids, "band_mask": band_mask, "sensor_tags": sensor_tags, "segment_ids": segment_ids, "wave_table": wave_table, "gen_w1": gen_w1, "gen_w2": gen_w2, "sensor_table": sensor_table, "ln1_gain": ln1_gain, "qkv_weight": qkv_weight, "proj_weight": proj_weight, "ln2_gain": ln2_gain, "fc1_weight": fc1_weight, "fc2_weight": fc2_weight, "out_grad": out_grad}


@jax.custom_vjp
def low(v):
    return lax.optimization_barrier(v.astype(jnp.bfloat16)).astype(jnp.float32)

@jax.custom_vjp
def low_back(v):
    return v

def low_keep(v):
    return (low(v), None)

def low_pass(kept, grad):
    return (grad,)

def back_keep(v):
    return (v, None)

def back_low(kept, grad):
    return (low(grad),)
low.defvjp(low_keep, low_pass)
low_back.defvjp(back_keep, back_low)
highest = lax.Precision.HIGHEST

def matmul(left, right):
    return jnp.dot(left, right, precision=highest, preferred_element_type=jnp.float32)

def layer_norm(inputs, gain):
    center = inputs - lax.optimization_barrier(jnp.mean(inputs, axis=-1, keepdims=True))
    return center * lax.rsqrt(lax.optimization_barrier(jnp.mean(center * center, axis=-1, keepdims=True)) + 1e-05) * gain

def attend(packed):
    queries, keys, values, segment = packed
    query_heads = queries.reshape(LEN, HEADS, HD)
    key_heads = keys.reshape(LEN, HEADS, HD)
    value_heads = values.reshape(LEN, HEADS, HD)
    scores = low_back(jnp.einsum('qhd,khd->hqk', query_heads, key_heads, precision=highest) * HD ** (-0.5))
    same_segment = segment[:, None] == segment[None, :]
    scores = jnp.where(same_segment[None], scores, -1000000000.0)
    row_peak = lax.optimization_barrier(jnp.max(scores, axis=-1, keepdims=True))
    weights = jnp.exp(scores - row_peak)
    probs = low(weights / lax.optimization_barrier(jnp.sum(weights, axis=-1, keepdims=True)))
    mixed_rows = jnp.einsum('hqk,khd->qhd', probs, value_heads, precision=highest).reshape(LEN, D)
    return low_back(low(mixed_rows))

def forward(pixels, wave_table, gen_w1, gen_w2, sensor_table, ln1_gain, qkv_weight, proj_weight, ln2_gain, fc1_weight, fc2_weight, band_ids, band_mask, sensor_tags, segment_ids):
    select = (band_ids[:, :, None] == jnp.arange(WAVES, dtype=jnp.int32)[None, None, :]).astype(jnp.float32)
    wave_rows = jnp.einsum('gbw,wc->gbc', select, wave_table, precision=highest)
    hidden = wave_rows + jax.nn.gelu(jnp.einsum('gbc,ce->gbe', wave_rows, gen_w1, precision=highest))
    kernels = low(low_back(jnp.einsum('gbe,ef->gbf', low(hidden), gen_w2, precision=highest)))
    kernels = kernels * band_mask.astype(jnp.float32)[:, :, None]
    kernels = kernels.reshape(GROUPS, BANDS, PIX, D)
    grouped = pixels.reshape(BANDS, GROUPS, GROUP_TOK, PIX)
    embedded = low_back(jnp.einsum('bgtp,gbpd->gtd', grouped, kernels, precision=highest))
    sensor_pick = (sensor_tags[:, None] == jnp.arange(SENSORS, dtype=jnp.int32)[None, :]).astype(jnp.float32)
    sensor_rows = matmul(sensor_pick, sensor_table)
    start = (embedded + sensor_rows[:, None, :]).reshape(TOKENS, D)
    normed1 = low(layer_norm(start, ln1_gain))
    projected = low(low_back(matmul(normed1, qkv_weight)))
    queries = projected[:, :D].reshape(SEQS, LEN, D)
    keys = projected[:, D:2 * D].reshape(SEQS, LEN, D)
    values = projected[:, 2 * D:].reshape(SEQS, LEN, D)
    attended = lax.map(jax.checkpoint(attend), (queries, keys, values, segment_ids)).reshape(TOKENS, D)
    after = start + low_back(matmul(attended, proj_weight))
    normed2 = low(layer_norm(after, ln2_gain))
    up = low_back(matmul(normed2, fc1_weight))
    act = low(jax.nn.gelu(up))
    return after + matmul(act, fc2_weight)

def reference(pixels, band_ids, band_mask, sensor_tags, segment_ids, wave_table, gen_w1, gen_w2, sensor_table, ln1_gain, qkv_weight, proj_weight, ln2_gain, fc1_weight, fc2_weight, out_grad):
    floats = (pixels, wave_table, gen_w1, gen_w2, sensor_table, ln1_gain, qkv_weight, proj_weight, ln2_gain, fc1_weight, fc2_weight)
    floats = tuple((item.astype(jnp.float32) for item in floats))

    def run(*inputs):
        return forward(*inputs, band_ids, band_mask, sensor_tags, segment_ids)
    encoded, pull = jax.vjp(run, *floats)
    grads = pull(out_grad.astype(jnp.float32))
    return (encoded, grads[0], grads[1], grads[2], grads[3], grads[4], grads[5], grads[6], grads[7], grads[8], grads[9], grads[10])
```

```python
import jax
import jax.numpy as jnp
from jax import lax
from jax.sharding import PartitionSpec as P

HEADS = 12


highest = lax.Precision.HIGHEST


def layer_norm(inputs, gain):
    center = inputs - jnp.mean(inputs, axis=-1, keepdims=True)
    inverse = lax.rsqrt(jnp.mean(center * center, axis=-1, keepdims=True) + 1e-05)
    unit_rows = center * inverse
    return (unit_rows * gain, unit_rows, inverse)


def norm_back(grad_rows, unit_rows, inverse, gain):
    scaled = grad_rows * gain
    inner = jnp.mean(scaled * unit_rows, axis=-1, keepdims=True)
    result = inverse * (scaled - jnp.mean(scaled, axis=-1, keepdims=True) - unit_rows * inner)
    return (result, jnp.sum(grad_rows * unit_rows, axis=0))


def generate(wave_rows, gen_w1):
    return wave_rows + jax.nn.gelu(
        jnp.dot(wave_rows.astype(jnp.bfloat16), gen_w1, preferred_element_type=jnp.float32)
    )


def generate_exact(wave_rows, weight):
    return wave_rows + jax.nn.gelu(jnp.dot(wave_rows, weight, precision=highest))


def score_block(query_heads, key_heads, seg_rows, seg_all, score_scale):
    scores = (
        jnp.einsum("qhd,khd->hqk", query_heads, key_heads, preferred_element_type=jnp.float32)
        * score_scale
    )
    same_segment = seg_rows[:, None] == seg_all[None, :]
    return jnp.where(same_segment[None], scores, -1000000000.0)


def attend_forward(queries, keys, values, segment, head_count):
    length, model_width = queries.shape
    head_size = model_width // head_count
    score_scale = head_size ** (-0.5)
    block_rows = min(512, length)
    query_heads = queries.reshape(length, head_count, head_size)
    key_heads = keys.reshape(length, head_count, head_size)
    value_heads = values.reshape(length, head_count, head_size)
    outputs = []
    totals = []
    for first_row in range(0, length, block_rows):
        rows_end = first_row + block_rows
        scores = score_block(
            query_heads[first_row:rows_end],
            key_heads,
            segment[first_row:rows_end],
            segment,
            score_scale,
        )
        row_peak = jnp.max(scores, axis=-1, keepdims=True)
        log_total = row_peak + jnp.log(jnp.sum(jnp.exp(scores - row_peak), axis=-1, keepdims=True))
        weights_low = jnp.exp(scores - log_total).astype(jnp.bfloat16)
        mixed_rows = jnp.einsum(
            "hqk,khd->qhd", weights_low, value_heads, preferred_element_type=jnp.float32
        )
        outputs.append(mixed_rows.reshape(-1, model_width))
        totals.append(log_total)
    return (jnp.concatenate(outputs, axis=0).astype(jnp.bfloat16), jnp.concatenate(totals, axis=1))


def attend_back(queries, keys, values, segment, totals, grad_mixed, head_count):
    length, model_width = queries.shape
    head_size = model_width // head_count
    score_scale = head_size ** (-0.5)
    block_rows = min(512, length)
    query_heads = queries.reshape(length, head_count, head_size)
    key_heads = keys.reshape(length, head_count, head_size)
    value_heads = values.reshape(length, head_count, head_size)
    grad_heads = grad_mixed.reshape(length, head_count, head_size)
    grad_keys = jnp.zeros((length, head_count, head_size), jnp.float32)
    grad_values = jnp.zeros((length, head_count, head_size), jnp.float32)
    grad_queries = []
    for first_row in range(0, length, block_rows):
        rows_end = first_row + block_rows
        scores = score_block(
            query_heads[first_row:rows_end],
            key_heads,
            segment[first_row:rows_end],
            segment,
            score_scale,
        )
        weights = jnp.exp(scores - totals[:, first_row:rows_end])
        weights_low = weights.astype(jnp.bfloat16)
        grad_weights = jnp.einsum(
            "qhd,khd->hqk",
            grad_heads[first_row:rows_end],
            value_heads,
            preferred_element_type=jnp.float32,
        )
        grad_scores = (
            weights * (grad_weights - jnp.sum(weights * grad_weights, axis=-1, keepdims=True))
        ).astype(jnp.bfloat16)
        grad_queries.append(
            jnp.einsum(
                "hqk,khd->qhd", grad_scores, key_heads, preferred_element_type=jnp.float32
            ).reshape(-1, model_width)
            * score_scale
        )
        grad_keys = (
            grad_keys
            + jnp.einsum(
                "hqk,qhd->khd",
                grad_scores,
                query_heads[first_row:rows_end],
                preferred_element_type=jnp.float32,
            )
            * score_scale
        )
        grad_values = grad_values + jnp.einsum(
            "hqk,qhd->khd",
            weights_low,
            grad_heads[first_row:rows_end],
            preferred_element_type=jnp.float32,
        )
    return jnp.concatenate(
        [
            jnp.concatenate(grad_queries, axis=0),
            grad_keys.reshape(length, model_width),
            grad_values.reshape(length, model_width),
        ],
        axis=1,
    )


def swap(piece, axis, mask):
    count = lax.axis_size(axis)
    return lax.ppermute(piece, axis, [(i, i ^ mask) for i in range(count)])


def bits_of(axis):
    return lax.axis_size(axis).bit_length() - 1


def all_bits():
    return [("band", bit) for bit in reversed(range(bits_of("band")))] + [
        ("dp", bit) for bit in reversed(range(bits_of("dp")))
    ]


def scatter_sum(term, order):
    dims = all_bits()
    rows = term.shape[0] // (2 ** len(dims))
    parts = [term.reshape((2,) * len(dims) + (rows,) + term.shape[1:])]
    for axis, bit in order:
        dim = dims.index((axis, bit))
        dims.pop(dim)
        mine = (lax.axis_index(axis) >> bit) & 1
        send = sum(
            lax.dynamic_index_in_dim(part, 1 - mine, dim, False).astype(jnp.float32)
            for part in parts
        ).astype(jnp.bfloat16)
        parts = [lax.dynamic_index_in_dim(part, mine, dim, False) for part in parts]
        parts.append(swap(send, axis, 1 << bit))
    return sum(part.astype(jnp.float32) for part in parts)


def exchange(pieces, axis):
    count = lax.axis_size(axis)
    shape = pieces.shape
    held = pieces
    for bit in range(bits_of(axis)):
        view = held.reshape((count >> (bit + 1), 2, 1 << bit) + shape[1:])
        got = swap(view[:, 1], axis, 1 << bit)
        held = jnp.stack([view[:, 0], got], axis=1).reshape(shape)
    return held


def gather_xor(piece, axis):
    held = piece[None]
    for bit in range(bits_of(axis)):
        held = jnp.concatenate([held, swap(held, axis, 1 << bit)], axis=0)
    return held


def in_order(held, axis):
    place = lax.axis_index(axis)
    return jnp.stack(
        [
            lax.dynamic_index_in_dim(held, place ^ i, 0, False)
            for i in range(held.shape[0])
        ]
    )


def shards(
    pixels,
    band_ids,
    band_mask,
    sensor_tags,
    segment_ids,
    wave_table,
    gen_w1,
    gen_w2,
    sensor_table,
    ln1_gain,
    qkv_weight,
    proj_weight,
    ln2_gain,
    fc1_weight,
    fc2_weight,
    out_grad,
):
    band_place = lax.axis_index("band")
    dp_place = lax.axis_index("dp")
    band_count = lax.axis_size("band")
    dp_count = lax.axis_size("dp")
    slots_dev = pixels.shape[0]
    slots = band_ids.shape[1]
    tok_dev = out_grad.shape[0]
    model_width = qkv_weight.shape[0]
    patch_pixels = pixels.shape[2]
    wave_count = wave_table.shape[0]
    seq_count = segment_ids.shape[0]
    length = segment_ids.shape[1]
    sensors = sensor_table.shape[0]
    code_width = wave_table.shape[1]
    part_rows = slots_dev * patch_pixels

    own_pixels = pixels.transpose(0, 2, 1).reshape(part_rows, -1)
    token_pixels = jnp.zeros((band_count * part_rows, tok_dev), pixels.dtype)
    for mask in range(band_count):
        other = band_place ^ mask
        piece = lax.dynamic_slice_in_dim(own_pixels, other * tok_dev, tok_dev, 1)
        if mask:
            piece = swap(piece, "band", mask)
        token_pixels = lax.dynamic_update_slice_in_dim(
            token_pixels, piece, other * part_rows, 0
        )

    numbers = jnp.concatenate([band_ids[0], band_mask[0], sensor_tags])
    all_numbers = in_order(gather_xor(numbers, "dp"), "dp")
    all_ids = all_numbers[:, :slots].reshape(-1)
    all_masks = all_numbers[:, slots : 2 * slots].reshape(-1)
    all_tags = all_numbers[:, 2 * slots]

    select = (all_ids[:, None] == jnp.arange(wave_count, dtype=jnp.int32)[None, :]).astype(
        jnp.float32
    )
    table_exact = wave_table.astype(jnp.float32)
    gen_w1_exact = gen_w1.astype(jnp.float32)

    def lookup_generate(table, weight):
        return generate_exact(jnp.dot(select, table, precision=highest), weight)

    hidden_all, gen_pull = jax.vjp(lookup_generate, table_exact, gen_w1_exact)
    hidden_all_low = hidden_all.astype(jnp.bfloat16)

    select_own = (band_ids[0][:, None] == jnp.arange(wave_count, dtype=jnp.int32)[None, :]).astype(
        jnp.bfloat16
    )
    wave_rows = jnp.dot(select_own, wave_table, preferred_element_type=jnp.float32)
    hidden_low = generate(wave_rows, gen_w1).astype(jnp.bfloat16)
    kernel_flat = jnp.dot(hidden_low, gen_w2, preferred_element_type=jnp.float32).astype(
        jnp.bfloat16
    )
    mask_low = band_mask[0].astype(jnp.bfloat16)
    kernel = (kernel_flat * mask_low[:, None]).reshape(slots * patch_pixels, model_width)
    sensor_pick = (sensor_tags[0] == jnp.arange(sensors, dtype=jnp.int32)).astype(jnp.float32)
    sensor_row = jnp.dot(sensor_pick, sensor_table.astype(jnp.float32), precision=highest)
    start_rows = (
        jnp.einsum("st,sd->td", token_pixels, kernel, preferred_element_type=jnp.float32)
        + sensor_row[None, :]
    )
    normed1, unit1, inverse1 = layer_norm(start_rows, ln1_gain)
    normed1_low = normed1.astype(jnp.bfloat16)
    projected = jnp.dot(normed1_low, qkv_weight, preferred_element_type=jnp.float32).astype(
        jnp.bfloat16
    )
    queries = projected[:, :model_width].reshape(seq_count, length, model_width)
    keys = projected[:, model_width : 2 * model_width].reshape(seq_count, length, model_width)
    values = projected[:, 2 * model_width :].reshape(seq_count, length, model_width)

    def forward_one(packed):
        return attend_forward(packed[0], packed[1], packed[2], packed[3], HEADS)

    attended, totals = lax.map(forward_one, (queries, keys, values, segment_ids))
    attended = attended.reshape(tok_dev, model_width)
    after = start_rows + jnp.dot(attended, proj_weight, preferred_element_type=jnp.float32)
    normed2, unit2, inverse2 = layer_norm(after, ln2_gain)
    normed2_low = normed2.astype(jnp.bfloat16)
    up_rows = jnp.dot(normed2_low, fc1_weight, preferred_element_type=jnp.float32)
    act_low = jax.nn.gelu(up_rows).astype(jnp.bfloat16)
    encoded = after + jnp.dot(act_low, fc2_weight, preferred_element_type=jnp.float32)
    grad_act = jnp.dot(out_grad, fc2_weight.T, preferred_element_type=jnp.float32)
    fc2_term = jnp.dot(act_low.T, out_grad, preferred_element_type=jnp.float32).astype(jnp.bfloat16)
    gelu_out, gelu_pull = jax.vjp(jax.nn.gelu, up_rows)
    grad_up = gelu_pull(grad_act)[0].astype(jnp.bfloat16)
    fc1_term = jnp.dot(grad_up.T, normed2_low, preferred_element_type=jnp.float32).astype(
        jnp.bfloat16
    )
    grad_normed2 = jnp.dot(grad_up, fc1_weight.T, preferred_element_type=jnp.float32)
    grad_after_norm, ln2_term = norm_back(grad_normed2, unit2, inverse2, ln2_gain)
    grad_after = out_grad.astype(jnp.float32) + grad_after_norm
    grad_attn = grad_after.astype(jnp.bfloat16)
    proj_term = jnp.dot(grad_attn.T, attended, preferred_element_type=jnp.float32).astype(
        jnp.bfloat16
    )
    grad_attended = jnp.dot(grad_attn, proj_weight.T, preferred_element_type=jnp.float32).astype(
        jnp.bfloat16
    )

    def back_one(packed):
        return attend_back(packed[0], packed[1], packed[2], packed[3], packed[4], packed[5], HEADS)

    grad_projected = lax.map(
        back_one,
        (
            queries,
            keys,
            values,
            segment_ids,
            totals,
            grad_attended.reshape(seq_count, length, model_width),
        ),
    )
    grad_projected = grad_projected.reshape(tok_dev, 3 * model_width).astype(jnp.bfloat16)
    qkv_term = jnp.dot(grad_projected.T, normed1_low, preferred_element_type=jnp.float32).astype(
        jnp.bfloat16
    )
    grad_normed1 = jnp.dot(grad_projected, qkv_weight.T, preferred_element_type=jnp.float32)
    grad_start_norm, ln1_term = norm_back(grad_normed1, unit1, inverse1, ln1_gain)
    grad_start = grad_after + grad_start_norm
    sensor_term = jnp.sum(grad_start, axis=0)
    grad_embed = grad_start.astype(jnp.bfloat16)

    kernel_term = jnp.dot(token_pixels, grad_embed, preferred_element_type=jnp.float32)
    kernel_parts = [
        kernel_term.astype(jnp.bfloat16).reshape(
            (slots,) + (2,) * bits_of("band") + (patch_pixels // band_count, model_width)
        )
    ]
    for bit in range(bits_of("band")):
        mine = (band_place >> bit) & 1
        dim = bits_of("band") - bit
        send = sum(
            lax.dynamic_index_in_dim(part, 1 - mine, dim, False).astype(jnp.float32)
            for part in kernel_parts
        ).astype(jnp.bfloat16)
        kernel_parts = [lax.dynamic_index_in_dim(part, mine, dim, False) for part in kernel_parts]
        kernel_parts.append(swap(send, "band", 1 << bit))
    kernel_sum = sum(part.astype(jnp.float32) for part in kernel_parts).reshape(slots, -1)
    grad_kernel_low = (kernel_sum * band_mask[0].astype(jnp.float32)[:, None]).astype(jnp.bfloat16)
    range_width = grad_kernel_low.shape[1]
    hidden_term = lax.dot_general(
        grad_kernel_low,
        lax.dynamic_slice_in_dim(gen_w2, band_place * range_width, range_width, 1),
        (((1,), (1,)), ((), ())),
        preferred_element_type=jnp.float32,
    )
    share = range_width // dp_count
    kernel_shares = jnp.stack(
        [
            lax.dynamic_slice_in_dim(grad_kernel_low, (dp_place ^ i) * share, share, 1)
            for i in range(dp_count)
        ]
    )
    kernel_rows = in_order(exchange(kernel_shares, "dp"), "dp").reshape(-1, share)
    gen_w2_grad = lax.dot_general(
        hidden_all_low,
        kernel_rows,
        (((0,), (0,)), ((), ())),
        preferred_element_type=jnp.float32,
    )

    small = jnp.concatenate([hidden_term.reshape(-1), ln1_term, ln2_term, sensor_term])
    for bit in range(bits_of("band")):
        small = small + swap(small, "band", 1 << bit)
    all_small = in_order(gather_xor(small, "dp"), "dp")
    hidden_size = slots * code_width
    grad_hidden = all_small[:, :hidden_size].reshape(-1, code_width)
    sums = jnp.sum(all_small[:, hidden_size:], axis=0)
    ln1_gain_grad = sums[:model_width]
    ln2_gain_grad = sums[model_width : 2 * model_width]
    sensor_each = all_small[:, hidden_size + 2 * model_width :]
    all_pick = (all_tags[None, :] == jnp.arange(sensors, dtype=jnp.int32)[:, None]).astype(
        jnp.float32
    )
    sensor_grad = jnp.dot(all_pick, sensor_each, precision=highest)
    wave_table_grad, gen_w1_grad = gen_pull(grad_hidden)

    pixel_terms = lax.dot_general(
        kernel,
        grad_embed,
        (((1,), (1,)), ((), ())),
        preferred_element_type=jnp.float32,
    )
    grad_pixels = jnp.zeros((part_rows, band_count * tok_dev), jnp.float32)
    for mask in range(band_count):
        other = band_place ^ mask
        piece = lax.dynamic_slice_in_dim(pixel_terms, other * part_rows, part_rows, 0)
        if mask:
            piece = swap(piece.astype(jnp.bfloat16), "band", mask).astype(jnp.float32)
        grad_pixels = lax.dynamic_update_slice_in_dim(grad_pixels, piece, other * tok_dev, 1)
    grad_pixels = grad_pixels.reshape(slots_dev, patch_pixels, -1).transpose(0, 2, 1)

    dims = all_bits()
    core_first = [("band", 0)]
    rest = [item for item in dims if item not in core_first]
    fc2_grad = scatter_sum(fc2_term, core_first + rest)
    turned = core_first + rest[len(rest) // 2 :] + rest[: len(rest) // 2]
    fc1_grad = scatter_sum(fc1_term, turned).T
    proj_grad = scatter_sum(proj_term, core_first + rest).T
    qkv_grad = scatter_sum(qkv_term, core_first + rest).T
    return (
        encoded,
        grad_pixels,
        wave_table_grad,
        gen_w1_grad,
        gen_w2_grad,
        sensor_grad,
        ln1_gain_grad,
        qkv_grad,
        proj_grad,
        ln2_gain_grad,
        fc1_grad,
        fc2_grad,
    )


def solution(mesh):
    return jax.shard_map(
        shards,
        mesh=mesh,
        in_specs=(
            P("band", "dp", None),
            P("dp", None),
            P("dp", None),
            P("dp"),
            P(("dp", "band"), None),
            P(),
            P(),
            P(),
            P(),
            P(),
            P(),
            P(),
            P(),
            P(),
            P(),
            P(("dp", "band"), None),
        ),
        out_specs=(
            P(("dp", "band"), None),
            P("band", "dp", None),
            P(),
            P(),
            P(None, ("band", "dp")),
            P(),
            P(),
            P(None, ("band", "dp")),
            P(None, ("band", "dp")),
            P(),
            P(None, ("band", "dp")),
            P(("band", "dp"), None),
        ),
        check_vma=False,
    )
```

```python
import functools

import jax
import jax.numpy as jnp
from jax import lax
from jax.experimental import pallas as pl
from jax.experimental.pallas import tpu as pltpu
from jax.sharding import PartitionSpec as P


highest = lax.Precision.HIGHEST


def layer_norm(inputs, gain):
    center = inputs - jnp.mean(inputs, axis=-1, keepdims=True)
    inverse = lax.rsqrt(jnp.mean(center * center, axis=-1, keepdims=True) + 1e-05)
    unit_rows = center * inverse
    return (unit_rows * gain, unit_rows, inverse)


def norm_back(grad_rows, unit_rows, inverse, gain):
    scaled = grad_rows * gain
    inner = jnp.mean(scaled * unit_rows, axis=-1, keepdims=True)
    result = inverse * (scaled - jnp.mean(scaled, axis=-1, keepdims=True) - unit_rows * inner)
    return (result, jnp.sum(grad_rows * unit_rows, axis=0))


def generate(wave_rows, gen_w1):
    return wave_rows + jax.nn.gelu(
        jnp.dot(wave_rows.astype(jnp.bfloat16), gen_w1, preferred_element_type=jnp.float32)
    )


def generate_exact(wave_rows, weight):
    return wave_rows + jax.nn.gelu(jnp.dot(wave_rows, weight, precision=highest))


BLOCK = 256
STEP = 128
FAR = 2.0**30
LANES = (((1,), (1,)), ((), ()))
ROWS = (((0,), (0,)), ((), ()))


def dot32(left, right, dims):
    return lax.dot_general(left, right, dims, preferred_element_type=jnp.float32)


def windows(segment_ids):
    length = segment_ids.shape[1]
    first = segment_ids[:, ::BLOCK]
    last = segment_ids[:, BLOCK - 1 :: BLOCK]
    begin = jnp.sum(segment_ids[:, None, :] < first[:, :, None], axis=-1)
    end = jnp.sum(segment_ids[:, None, :] <= last[:, :, None], axis=-1)
    low = begin // STEP
    count = (end + STEP - 1) // STEP - low
    return jnp.stack([low, count - 1], axis=-1).astype(jnp.int32).reshape(-1)


def features(segment_ids):
    lane = jnp.arange(128, dtype=jnp.int32)
    code = segment_ids.reshape(-1, 1)
    same = (code == (lane % 64)[None, :])
    used = (lane % 64 < 4)[None, :]
    query_side = jnp.where(same & used, 1.0, 0.0)
    key_side = jnp.where(used & ~same, -FAR, 0.0)
    return query_side.astype(jnp.bfloat16), key_side.astype(jnp.bfloat16)


def head_masks():
    lane = lax.broadcasted_iota(jnp.int32, (1, 128), 1)
    low = jnp.where(lane < 64, 1.0, 0.0)
    return low.astype(jnp.bfloat16), (1.0 - low).astype(jnp.bfloat16)


def forward_kernel(win, q_ref, k_ref, v_ref, qf_ref, kf_ref, o_ref, lse_ref, qa, ka, va):
    length = q_ref.shape[0]
    blocks = length // BLOCK
    base = pl.program_id(0) * blocks * 2
    for h, mask in enumerate(head_masks()):
        other = jnp.bfloat16(1.0) - mask
        qa[h] = q_ref[...] * (mask * jnp.bfloat16(0.125)) + qf_ref[...] * other
        ka[h] = k_ref[...] * mask + kf_ref[...] * other
        va[h] = v_ref[...] * mask + other

    def one_block(block, carry):
        rows = pl.ds(pl.multiple_of(block * BLOCK, BLOCK), BLOCK)
        low = pl.multiple_of(win[base + 2 * block] * STEP, STEP)

        def run(width):
            keys = pl.ds(low, width)
            mixes, peaks = [], []
            for h in range(2):
                scores = dot32(qa[h, rows, :], ka[h, keys, :], LANES)
                peak = jnp.max(scores, axis=1, keepdims=True)
                probs = jnp.exp(scores - peak).astype(jnp.bfloat16)
                mixes.append(jnp.dot(probs, va[h, keys, :], preferred_element_type=jnp.float32))
                peaks.append(peak)
            low_lanes = lax.broadcasted_iota(jnp.int32, (1, 128), 1) < 64
            mixed = jnp.where(low_lanes, mixes[0], mixes[1])
            total = pltpu.roll(jnp.where(low_lanes, mixes[1], mixes[0]), 64, 1)
            o_ref[rows, :] = (mixed / total).astype(jnp.bfloat16)
            both = (jnp.where(low_lanes, peaks[0], peaks[1]) + jnp.log(total)).T
            lse_ref[0, 0, 0:1, rows] = both[0:1]
            lse_ref[0, 0, 1:2, rows] = both[64:65]

        count = win[base + 2 * block + 1]
        for size in range(length // STEP):
            pl.when(count == size)(functools.partial(run, (size + 1) * STEP))
        return carry

    lax.fori_loop(0, blocks, one_block, 0)


def back_kernel(win, q_ref, k_ref, v_ref, qf_ref, kf_ref, g_ref, o_ref, lse_ref, out_ref, qa, ka, qh, kh, vh, gh, delta, dk, dv):
    length = q_ref.shape[0]
    blocks = length // BLOCK
    base = pl.program_id(0) * blocks * 2
    masks = head_masks()
    for h, mask in enumerate(masks):
        other = jnp.bfloat16(1.0) - mask
        scaled = q_ref[...] * (mask * jnp.bfloat16(0.125))
        qh[h] = scaled
        qa[h] = scaled + qf_ref[...] * other
        own = k_ref[...] * mask
        kh[h] = own
        ka[h] = own + kf_ref[...] * other
        vh[h] = v_ref[...] * mask
        gh[h] = g_ref[...] * mask
    product = g_ref[...].astype(jnp.float32) * o_ref[...].astype(jnp.float32)
    turned = product.T
    delta[0:1, :] = jnp.sum(turned[:64], axis=0, keepdims=True)
    delta[1:2, :] = jnp.sum(turned[64:], axis=0, keepdims=True)
    dk[...] = jnp.zeros_like(dk)
    dv[...] = jnp.zeros_like(dv)

    def one_block(block, carry):
        rows = pl.ds(pl.multiple_of(block * BLOCK, BLOCK), BLOCK)
        low = pl.multiple_of(win[base + 2 * block] * STEP, STEP)

        def run(width):
            keys = pl.ds(low, width)
            turned_grad = None
            for h in range(2):
                scores = dot32(ka[h, keys, :], qa[h, rows, :], LANES)
                probs = jnp.exp(scores - lse_ref[0, 0, h : h + 1, rows])
                grad_probs = dot32(vh[h, keys, :], gh[h, rows, :], LANES)
                grad_scores = (probs * (grad_probs - delta[h : h + 1, rows])).astype(jnp.bfloat16)
                dv[keys, :] += jnp.dot(probs.astype(jnp.bfloat16), gh[h, rows, :], preferred_element_type=jnp.float32)
                dk[keys, :] += jnp.dot(grad_scores, qh[h, rows, :], preferred_element_type=jnp.float32)
                term = dot32(grad_scores, kh[h, keys, :], ROWS)
                turned_grad = term if h == 0 else turned_grad + term
            out_ref[0, rows, :] = (turned_grad * 0.125).astype(jnp.bfloat16)

        count = win[base + 2 * block + 1]
        for size in range(length // STEP):
            pl.when(count == size)(functools.partial(run, (size + 1) * STEP))
        return carry

    lax.fori_loop(0, blocks, one_block, 0)
    out_ref[1] = dk[...].astype(jnp.bfloat16)
    out_ref[2] = dv[...].astype(jnp.bfloat16)


def attend_forward(projected, segment_ids, win, query_side, key_side):
    seqs, length = segment_ids.shape
    width = projected.shape[1] // 3
    pairs = width // 128

    def columns(offset):
        return pl.BlockSpec((length, 128), lambda s, p, w: (s, p + offset))

    fixed = pl.BlockSpec((length, 128), lambda s, p, w: (s, 0))
    return pl.pallas_call(
        forward_kernel,
        grid_spec=pltpu.PrefetchScalarGridSpec(
            num_scalar_prefetch=1,
            grid=(seqs, pairs),
            in_specs=[columns(0), columns(pairs), columns(2 * pairs), fixed, fixed],
            out_specs=[
                columns(0),
                pl.BlockSpec((1, 1, 8, length), lambda s, p, w: (s, p, 0, 0)),
            ],
            scratch_shapes=[pltpu.VMEM((2, length, 128), jnp.bfloat16)] * 3,
        ),
        out_shape=[
            jax.ShapeDtypeStruct((seqs * length, width), jnp.bfloat16),
            jax.ShapeDtypeStruct((seqs, pairs, 8, length), jnp.float32),
        ],
        compiler_params=pltpu.CompilerParams(vmem_limit_bytes=48 << 20),
        cost_estimate=pl.CostEstimate(flops=4 * seqs * length * length * width, bytes_accessed=8 * seqs * length * width, transcendentals=0),
        name="attend_forward",
    )(win, projected, projected, projected, query_side, key_side)


def attend_back(projected, segment_ids, win, query_side, key_side, grad, mixed, lse):
    seqs, length = segment_ids.shape
    width = projected.shape[1] // 3
    pairs = width // 128

    def columns(offset):
        return pl.BlockSpec((length, 128), lambda s, p, w: (s, p + offset))

    fixed = pl.BlockSpec((length, 128), lambda s, p, w: (s, 0))
    low = pltpu.VMEM((2, length, 128), jnp.bfloat16)
    return pl.pallas_call(
        back_kernel,
        grid_spec=pltpu.PrefetchScalarGridSpec(
            num_scalar_prefetch=1,
            grid=(seqs, pairs),
            in_specs=[
                columns(0),
                columns(pairs),
                columns(2 * pairs),
                fixed,
                fixed,
                columns(0),
                columns(0),
                pl.BlockSpec((1, 1, 8, length), lambda s, p, w: (s, p, 0, 0)),
            ],
            out_specs=pl.BlockSpec((3, length, 128), lambda s, p, w: (0, s, p)),
            scratch_shapes=[low] * 6
            + [
                pltpu.VMEM((8, length), jnp.float32),
                pltpu.VMEM((length, 128), jnp.float32),
                pltpu.VMEM((length, 128), jnp.float32),
            ],
        ),
        out_shape=jax.ShapeDtypeStruct((3, seqs * length, width), jnp.bfloat16),
        compiler_params=pltpu.CompilerParams(vmem_limit_bytes=48 << 20),
        cost_estimate=pl.CostEstimate(flops=10 * seqs * length * length * width, bytes_accessed=14 * seqs * length * width, transcendentals=0),
        name="attend_back",
    )(win, projected, projected, projected, query_side, key_side, grad, mixed, lse)


def swap(piece, axis, mask):
    count = lax.axis_size(axis)
    return lax.ppermute(piece, axis, [(i, i ^ mask) for i in range(count)])


def bits_of(axis):
    return lax.axis_size(axis).bit_length() - 1


def all_bits():
    return [("band", bit) for bit in reversed(range(bits_of("band")))] + [
        ("dp", bit) for bit in reversed(range(bits_of("dp")))
    ]


def scatter_sum(term, order):
    dims = all_bits()
    rows = term.shape[0] // (2 ** len(dims))
    parts = [term.reshape((2,) * len(dims) + (rows,) + term.shape[1:])]
    for axis, bit in order:
        dim = dims.index((axis, bit))
        dims.pop(dim)
        mine = (lax.axis_index(axis) >> bit) & 1
        send = sum(
            lax.dynamic_index_in_dim(part, 1 - mine, dim, False).astype(jnp.float32)
            for part in parts
        ).astype(jnp.bfloat16)
        parts = [lax.dynamic_index_in_dim(part, mine, dim, False) for part in parts]
        parts.append(swap(send, axis, 1 << bit))
    return sum(part.astype(jnp.float32) for part in parts)


def exchange(pieces, axis):
    count = lax.axis_size(axis)
    shape = pieces.shape
    held = pieces
    for bit in range(bits_of(axis)):
        view = held.reshape((count >> (bit + 1), 2, 1 << bit) + shape[1:])
        got = swap(view[:, 1], axis, 1 << bit)
        held = jnp.stack([view[:, 0], got], axis=1).reshape(shape)
    return held


def gather_xor(piece, axis):
    held = piece[None]
    for bit in range(bits_of(axis)):
        held = jnp.concatenate([held, swap(held, axis, 1 << bit)], axis=0)
    return held


def in_order(held, axis):
    place = lax.axis_index(axis)
    return jnp.stack(
        [
            lax.dynamic_index_in_dim(held, place ^ i, 0, False)
            for i in range(held.shape[0])
        ]
    )


def shards(
    pixels,
    band_ids,
    band_mask,
    sensor_tags,
    segment_ids,
    wave_table,
    gen_w1,
    gen_w2,
    sensor_table,
    ln1_gain,
    qkv_weight,
    proj_weight,
    ln2_gain,
    fc1_weight,
    fc2_weight,
    out_grad,
):
    band_place = lax.axis_index("band")
    dp_place = lax.axis_index("dp")
    band_count = lax.axis_size("band")
    dp_count = lax.axis_size("dp")
    slots_dev = pixels.shape[0]
    slots = band_ids.shape[1]
    tok_dev = out_grad.shape[0]
    model_width = qkv_weight.shape[0]
    patch_pixels = pixels.shape[2]
    wave_count = wave_table.shape[0]
    sensors = sensor_table.shape[0]
    code_width = wave_table.shape[1]
    part_rows = slots_dev * patch_pixels

    own_pixels = pixels.transpose(0, 2, 1).reshape(part_rows, -1)
    token_pixels = jnp.zeros((band_count * part_rows, tok_dev), pixels.dtype)
    for mask in range(band_count):
        other = band_place ^ mask
        piece = lax.dynamic_slice_in_dim(own_pixels, other * tok_dev, tok_dev, 1)
        if mask:
            piece = swap(piece, "band", mask)
        token_pixels = lax.dynamic_update_slice_in_dim(
            token_pixels, piece, other * part_rows, 0
        )

    numbers = jnp.concatenate([band_ids[0], band_mask[0], sensor_tags])
    all_numbers = in_order(gather_xor(numbers, "dp"), "dp")
    all_ids = all_numbers[:, :slots].reshape(-1)
    all_masks = all_numbers[:, slots : 2 * slots].reshape(-1)
    all_tags = all_numbers[:, 2 * slots]

    select = (all_ids[:, None] == jnp.arange(wave_count, dtype=jnp.int32)[None, :]).astype(
        jnp.float32
    )
    table_exact = wave_table.astype(jnp.float32)
    gen_w1_exact = gen_w1.astype(jnp.float32)

    def lookup_generate(table, weight):
        return generate_exact(jnp.dot(select, table, precision=highest), weight)

    hidden_all, gen_pull = jax.vjp(lookup_generate, table_exact, gen_w1_exact)
    hidden_all_low = hidden_all.astype(jnp.bfloat16)

    select_own = (band_ids[0][:, None] == jnp.arange(wave_count, dtype=jnp.int32)[None, :]).astype(
        jnp.bfloat16
    )
    wave_rows = jnp.dot(select_own, wave_table, preferred_element_type=jnp.float32)
    hidden_low = generate(wave_rows, gen_w1).astype(jnp.bfloat16)
    kernel_flat = jnp.dot(hidden_low, gen_w2, preferred_element_type=jnp.float32).astype(
        jnp.bfloat16
    )
    mask_low = band_mask[0].astype(jnp.bfloat16)
    kernel = (kernel_flat * mask_low[:, None]).reshape(slots * patch_pixels, model_width)
    sensor_pick = (sensor_tags[0] == jnp.arange(sensors, dtype=jnp.int32)).astype(jnp.float32)
    sensor_row = jnp.dot(sensor_pick, sensor_table.astype(jnp.float32), precision=highest)
    start_rows = (
        jnp.einsum("st,sd->td", token_pixels, kernel, preferred_element_type=jnp.float32)
        + sensor_row[None, :]
    )
    normed1, unit1, inverse1 = layer_norm(start_rows, ln1_gain)
    normed1_low = normed1.astype(jnp.bfloat16)
    projected = jnp.dot(normed1_low, qkv_weight, preferred_element_type=jnp.float32).astype(
        jnp.bfloat16
    )
    window = windows(segment_ids)
    query_side, key_side = features(segment_ids)
    attended, totals = attend_forward(projected, segment_ids, window, query_side, key_side)
    after = start_rows + jnp.dot(attended, proj_weight, preferred_element_type=jnp.float32)
    normed2, unit2, inverse2 = layer_norm(after, ln2_gain)
    normed2_low = normed2.astype(jnp.bfloat16)
    up_rows = jnp.dot(normed2_low, fc1_weight, preferred_element_type=jnp.float32)
    act_low = jax.nn.gelu(up_rows).astype(jnp.bfloat16)
    encoded = after + jnp.dot(act_low, fc2_weight, preferred_element_type=jnp.float32)
    grad_act = jnp.dot(out_grad, fc2_weight.T, preferred_element_type=jnp.float32)
    fc2_term = jnp.dot(act_low.T, out_grad, preferred_element_type=jnp.float32).astype(jnp.bfloat16)
    gelu_out, gelu_pull = jax.vjp(jax.nn.gelu, up_rows)
    grad_up = gelu_pull(grad_act)[0].astype(jnp.bfloat16)
    fc1_term = jnp.dot(grad_up.T, normed2_low, preferred_element_type=jnp.float32).astype(
        jnp.bfloat16
    )
    grad_normed2 = jnp.dot(grad_up, fc1_weight.T, preferred_element_type=jnp.float32)
    grad_after_norm, ln2_term = norm_back(grad_normed2, unit2, inverse2, ln2_gain)
    grad_after = out_grad.astype(jnp.float32) + grad_after_norm
    grad_attn = grad_after.astype(jnp.bfloat16)
    proj_term = jnp.dot(grad_attn.T, attended, preferred_element_type=jnp.float32).astype(
        jnp.bfloat16
    )
    grad_attended = jnp.dot(grad_attn, proj_weight.T, preferred_element_type=jnp.float32).astype(
        jnp.bfloat16
    )

    grad_projected = attend_back(
        projected, segment_ids, window, query_side, key_side, grad_attended, attended, totals
    )
    qkv_term = lax.dot_general(
        grad_projected, normed1_low, (((1,), (0,)), ((), ())), preferred_element_type=jnp.float32
    )
    qkv_term = qkv_term.astype(jnp.bfloat16).reshape(-1, model_width)
    grad_normed1 = lax.dot_general(
        grad_projected,
        qkv_weight.reshape(model_width, 3, model_width),
        (((0, 2), (1, 2)), ((), ())),
        preferred_element_type=jnp.float32,
    )
    grad_start_norm, ln1_term = norm_back(grad_normed1, unit1, inverse1, ln1_gain)
    grad_start = grad_after + grad_start_norm
    sensor_term = jnp.sum(grad_start, axis=0)
    grad_embed = grad_start.astype(jnp.bfloat16)

    kernel_term = jnp.dot(token_pixels, grad_embed, preferred_element_type=jnp.float32)
    kernel_parts = [
        kernel_term.astype(jnp.bfloat16).reshape(
            (slots,) + (2,) * bits_of("band") + (patch_pixels // band_count, model_width)
        )
    ]
    for bit in range(bits_of("band")):
        mine = (band_place >> bit) & 1
        dim = bits_of("band") - bit
        send = sum(
            lax.dynamic_index_in_dim(part, 1 - mine, dim, False).astype(jnp.float32)
            for part in kernel_parts
        ).astype(jnp.bfloat16)
        kernel_parts = [lax.dynamic_index_in_dim(part, mine, dim, False) for part in kernel_parts]
        kernel_parts.append(swap(send, "band", 1 << bit))
    kernel_sum = sum(part.astype(jnp.float32) for part in kernel_parts).reshape(slots, -1)
    grad_kernel_low = (kernel_sum * band_mask[0].astype(jnp.float32)[:, None]).astype(jnp.bfloat16)
    range_width = grad_kernel_low.shape[1]
    hidden_term = lax.dot_general(
        grad_kernel_low,
        lax.dynamic_slice_in_dim(gen_w2, band_place * range_width, range_width, 1),
        (((1,), (1,)), ((), ())),
        preferred_element_type=jnp.float32,
    )
    share = range_width // dp_count
    kernel_shares = jnp.stack(
        [
            lax.dynamic_slice_in_dim(grad_kernel_low, (dp_place ^ i) * share, share, 1)
            for i in range(dp_count)
        ]
    )
    kernel_rows = in_order(exchange(kernel_shares, "dp"), "dp").reshape(-1, share)
    gen_w2_grad = lax.dot_general(
        hidden_all_low,
        kernel_rows,
        (((0,), (0,)), ((), ())),
        preferred_element_type=jnp.float32,
    )

    small = jnp.concatenate([hidden_term.reshape(-1), ln1_term, ln2_term, sensor_term])
    for bit in range(bits_of("band")):
        small = small + swap(small, "band", 1 << bit)
    all_small = in_order(gather_xor(small, "dp"), "dp")
    hidden_size = slots * code_width
    grad_hidden = all_small[:, :hidden_size].reshape(-1, code_width)
    sums = jnp.sum(all_small[:, hidden_size:], axis=0)
    ln1_gain_grad = sums[:model_width]
    ln2_gain_grad = sums[model_width : 2 * model_width]
    sensor_each = all_small[:, hidden_size + 2 * model_width :]
    all_pick = (all_tags[None, :] == jnp.arange(sensors, dtype=jnp.int32)[:, None]).astype(
        jnp.float32
    )
    sensor_grad = jnp.dot(all_pick, sensor_each, precision=highest)
    wave_table_grad, gen_w1_grad = gen_pull(grad_hidden)

    pixel_terms = lax.dot_general(
        kernel,
        grad_embed,
        (((1,), (1,)), ((), ())),
        preferred_element_type=jnp.float32,
    )
    grad_pixels = jnp.zeros((part_rows, band_count * tok_dev), jnp.float32)
    for mask in range(band_count):
        other = band_place ^ mask
        piece = lax.dynamic_slice_in_dim(pixel_terms, other * part_rows, part_rows, 0)
        if mask:
            piece = swap(piece.astype(jnp.bfloat16), "band", mask).astype(jnp.float32)
        grad_pixels = lax.dynamic_update_slice_in_dim(grad_pixels, piece, other * tok_dev, 1)
    grad_pixels = grad_pixels.reshape(slots_dev, patch_pixels, -1).transpose(0, 2, 1)

    dims = all_bits()
    core_first = [("band", 0)]
    rest = [item for item in dims if item not in core_first]
    fc2_grad = scatter_sum(fc2_term, core_first + rest)
    turned = core_first + rest[len(rest) // 2 :] + rest[: len(rest) // 2]
    fc1_grad = scatter_sum(fc1_term, turned).T
    proj_grad = scatter_sum(proj_term, core_first + rest).T
    qkv_grad = scatter_sum(qkv_term, core_first + rest).T
    return (
        encoded,
        grad_pixels,
        wave_table_grad,
        gen_w1_grad,
        gen_w2_grad,
        sensor_grad,
        ln1_gain_grad,
        qkv_grad,
        proj_grad,
        ln2_gain_grad,
        fc1_grad,
        fc2_grad,
    )


def solution(mesh):
    return jax.shard_map(
        shards,
        mesh=mesh,
        in_specs=(
            P("band", "dp", None),
            P("dp", None),
            P("dp", None),
            P("dp"),
            P(("dp", "band"), None),
            P(),
            P(),
            P(),
            P(),
            P(),
            P(),
            P(),
            P(),
            P(),
            P(),
            P(("dp", "band"), None),
        ),
        out_specs=(
            P(("dp", "band"), None),
            P("band", "dp", None),
            P(),
            P(),
            P(None, ("band", "dp")),
            P(),
            P(),
            P(None, ("band", "dp")),
            P(None, ("band", "dp")),
            P(),
            P(None, ("band", "dp")),
            P(("band", "dp"), None),
        ),
        check_vma=False,
    )
```

```python
import functools

import jax
import jax.numpy as jnp
from jax import lax
from jax.experimental import pallas as pl
from jax.experimental.pallas import tpu as pltpu
from jax.sharding import PartitionSpec as P

highest = lax.Precision.HIGHEST
UNIT = 96
PARTS = 3
VA = 58
VM = 56
low = jnp.bfloat16
MIB = 1 << 20

BLOCK = 256
STEP = 128
FAR = 2.0**30
LANES = (((1,), (1,)), ((), ()))
ROWS = (((0,), (0,)), ((), ()))


def dot32(left, right, dims):
    return lax.dot_general(left, right, dims, preferred_element_type=jnp.float32)


def windows(segment_ids):
    length = segment_ids.shape[1]
    first = segment_ids[:, ::BLOCK]
    last = segment_ids[:, BLOCK - 1 :: BLOCK]
    begin = jnp.sum(segment_ids[:, None, :] < first[:, :, None], axis=-1)
    end = jnp.sum(segment_ids[:, None, :] <= last[:, :, None], axis=-1)
    low = begin // STEP
    count = (end + STEP - 1) // STEP - low
    return jnp.stack([low, count - 1], axis=-1).astype(jnp.int32).reshape(-1)


def features(segment_ids):
    lane = jnp.arange(128, dtype=jnp.int32)
    code = segment_ids.reshape(-1, 1)
    same = (code == (lane % 64)[None, :])
    used = (lane % 64 < 4)[None, :]
    query_side = jnp.where(same & used, 1.0, 0.0)
    key_side = jnp.where(used & ~same, -FAR, 0.0)
    return query_side.astype(jnp.bfloat16), key_side.astype(jnp.bfloat16)


def head_masks():
    lane = lax.broadcasted_iota(jnp.int32, (1, 128), 1)
    low = jnp.where(lane < 64, 1.0, 0.0)
    return low.astype(jnp.bfloat16), (1.0 - low).astype(jnp.bfloat16)


def forward_kernel(win, q_ref, k_ref, v_ref, qf_ref, kf_ref, o_ref, lse_ref, qa, ka, va):
    length = q_ref.shape[0]
    blocks = length // BLOCK
    base = pl.program_id(0) * blocks * 2
    for h, mask in enumerate(head_masks()):
        other = jnp.bfloat16(1.0) - mask
        qa[h] = q_ref[...] * (mask * jnp.bfloat16(0.125)) + qf_ref[...] * other
        ka[h] = k_ref[...] * mask + kf_ref[...] * other
        va[h] = v_ref[...] * mask + other

    def one_block(block, carry):
        rows = pl.ds(pl.multiple_of(block * BLOCK, BLOCK), BLOCK)
        low = pl.multiple_of(win[base + 2 * block] * STEP, STEP)

        def run(width):
            keys = pl.ds(low, width)
            mixes, peaks = [], []
            for h in range(2):
                scores = dot32(qa[h, rows, :], ka[h, keys, :], LANES)
                peak = jnp.max(scores, axis=1, keepdims=True)
                probs = jnp.exp(scores - peak).astype(jnp.bfloat16)
                mixes.append(jnp.dot(probs, va[h, keys, :], preferred_element_type=jnp.float32))
                peaks.append(peak)
            low_lanes = lax.broadcasted_iota(jnp.int32, (1, 128), 1) < 64
            mixed = jnp.where(low_lanes, mixes[0], mixes[1])
            total = pltpu.roll(jnp.where(low_lanes, mixes[1], mixes[0]), 64, 1)
            o_ref[rows, :] = (mixed / total).astype(jnp.bfloat16)
            both = (jnp.where(low_lanes, peaks[0], peaks[1]) + jnp.log(total)).T
            lse_ref[0, 0, 0:1, rows] = both[0:1]
            lse_ref[0, 0, 1:2, rows] = both[64:65]

        count = win[base + 2 * block + 1]
        for size in range(length // STEP):
            pl.when(count == size)(functools.partial(run, (size + 1) * STEP))
        return carry

    lax.fori_loop(0, blocks, one_block, 0)


def back_kernel(win, q_ref, k_ref, v_ref, qf_ref, kf_ref, g_ref, o_ref, lse_ref, out_ref, qa, ka, qh, kh, vh, gh, delta, dk, dv):
    length = q_ref.shape[0]
    blocks = length // BLOCK
    base = pl.program_id(0) * blocks * 2
    masks = head_masks()
    for h, mask in enumerate(masks):
        other = jnp.bfloat16(1.0) - mask
        scaled = q_ref[...] * (mask * jnp.bfloat16(0.125))
        qh[h] = scaled
        qa[h] = scaled + qf_ref[...] * other
        own = k_ref[...] * mask
        kh[h] = own
        ka[h] = own + kf_ref[...] * other
        vh[h] = v_ref[...] * mask
        gh[h] = g_ref[...] * mask
    product = g_ref[...].astype(jnp.float32) * o_ref[...].astype(jnp.float32)
    turned = product.T
    delta[0:1, :] = jnp.sum(turned[:64], axis=0, keepdims=True)
    delta[1:2, :] = jnp.sum(turned[64:], axis=0, keepdims=True)
    dk[...] = jnp.zeros_like(dk)
    dv[...] = jnp.zeros_like(dv)

    def one_block(block, carry):
        rows = pl.ds(pl.multiple_of(block * BLOCK, BLOCK), BLOCK)
        low = pl.multiple_of(win[base + 2 * block] * STEP, STEP)

        def run(width):
            keys = pl.ds(low, width)
            turned_grad = None
            for h in range(2):
                scores = dot32(ka[h, keys, :], qa[h, rows, :], LANES)
                probs = jnp.exp(scores - lse_ref[0, 0, h : h + 1, rows])
                grad_probs = dot32(vh[h, keys, :], gh[h, rows, :], LANES)
                grad_scores = (probs * (grad_probs - delta[h : h + 1, rows])).astype(jnp.bfloat16)
                dv[keys, :] += jnp.dot(probs.astype(jnp.bfloat16), gh[h, rows, :], preferred_element_type=jnp.float32)
                dk[keys, :] += jnp.dot(grad_scores, qh[h, rows, :], preferred_element_type=jnp.float32)
                term = dot32(grad_scores, kh[h, keys, :], ROWS)
                turned_grad = term if h == 0 else turned_grad + term
            out_ref[0, rows, :] = (turned_grad * 0.125).astype(jnp.bfloat16)

        count = win[base + 2 * block + 1]
        for size in range(length // STEP):
            pl.when(count == size)(functools.partial(run, (size + 1) * STEP))
        return carry

    lax.fori_loop(0, blocks, one_block, 0)
    out_ref[1] = dk[...].astype(jnp.bfloat16)
    out_ref[2] = dv[...].astype(jnp.bfloat16)


def attend_forward(projected, segment_ids, win, query_side, key_side):
    seqs, length = segment_ids.shape
    width = projected.shape[1] // 3
    pairs = width // 128

    def columns(offset):
        return pl.BlockSpec((length, 128), lambda s, p, w: (s, p + offset))

    fixed = pl.BlockSpec((length, 128), lambda s, p, w: (s, 0))
    return call(
        forward_kernel,
        "attend_forward",
        (seqs, pairs),
        [columns(0), columns(pairs), columns(2 * pairs), fixed, fixed],
        [columns(0), pl.BlockSpec((1, 1, 8, length), lambda s, p, w: (s, p, 0, 0))],
        [
            shape_of(seqs * length, width, dtype=low),
            shape_of(seqs, pairs, 8, length),
        ],
        4 * seqs * length * length * width,
        8 * seqs * length * width,
        [pltpu.VMEM((2, length, 128), low)] * 3,
        vmem=VA,
    )(win, projected, projected, projected, query_side, key_side)


def attend_back(projected, segment_ids, win, query_side, key_side, grad, mixed, lse, part, behind):
    seqs, length = segment_ids.shape
    width = projected.shape[1] // 3
    pairs = width // 128
    run = pairs // PARTS
    begin = part * run

    def columns(offset):
        return pl.BlockSpec((length, 128), lambda s, p, w: (s, p + offset + begin))

    fixed = pl.BlockSpec((length, 128), lambda s, p, w: (s, 0))
    pair_low = pltpu.VMEM((2, length, 128), low)
    return call(
        back_kernel,
        "attend_back",
        (seqs, run),
        [
            columns(0),
            columns(pairs),
            columns(2 * pairs),
            fixed,
            fixed,
            columns(0),
            columns(0),
            pl.BlockSpec((1, 1, 8, length), lambda s, p, w: (s, p + begin, 0, 0)),
        ],
        pl.BlockSpec((3, length, 128), lambda s, p, w: (0, s, p)),
        shape_of(3, seqs * length, run * 128, dtype=low),
        10 * seqs * length * length * run * 128,
        14 * seqs * length * run * 128,
        [pair_low] * 6
        + [
            pltpu.VMEM((8, length), jnp.float32),
            pltpu.VMEM((length, 128), jnp.float32),
            pltpu.VMEM((length, 128), jnp.float32),
        ],
        vmem=VA,
        behind=behind,
    )(win, projected, projected, projected, query_side, key_side, grad, mixed, lse)


def whole(shape):
    return pl.BlockSpec(shape, lambda *_: (0,) * len(shape))


def call(
    kernel,
    name,
    grid,
    in_specs,
    out_specs,
    out_shape,
    flops,
    moved,
    scratch=(),
    prefetch=1,
    vmem=40,
    behind=(),
):
    first = prefetch + len(in_specs)

    def body(*refs):
        kernel(*refs[:first], *refs[first + len(behind) :])

    run = pl.pallas_call(
        body,
        grid_spec=pltpu.PrefetchScalarGridSpec(
            num_scalar_prefetch=prefetch,
            grid=grid,
            in_specs=list(in_specs) + [pl.BlockSpec(memory_space=pl.ANY)] * len(behind),
            out_specs=out_specs,
            scratch_shapes=list(scratch),
        ),
        out_shape=out_shape,
        compiler_params=pltpu.CompilerParams(vmem_limit_bytes=vmem * MIB),
        cost_estimate=pl.CostEstimate(flops=flops, bytes_accessed=moved, transcendentals=0),
        name=name,
    )
    return lambda *args: run(*args, *behind)


def shape_of(*shape, dtype=jnp.float32):
    return jax.ShapeDtypeStruct(shape, dtype)


def units(rows):
    center = rows - jnp.mean(rows, axis=-1, keepdims=True)
    inverse = lax.rsqrt(jnp.mean(center * center, axis=-1, keepdims=True) + 1e-05)
    return center * inverse, inverse


def norm_back(grad_rows, unit_rows, inverse, gain):
    scaled = grad_rows * gain
    inner = jnp.mean(scaled * unit_rows, axis=-1, keepdims=True)
    return inverse * (scaled - jnp.mean(scaled, axis=-1, keepdims=True) - unit_rows * inner)


def gelu_both(rows):
    root = 0.7978845608028654
    square = rows * rows
    curve = jnp.tanh(rows * (root + (root * 0.044715) * square))
    half = 0.5 + 0.5 * curve
    slope = half + (0.5 * rows) * (1.0 - curve * curve) * (root + (3.0 * root * 0.044715) * square)
    return rows * half, slope


def code_rows(ids, table, weight):
    lane = lax.broadcasted_iota(jnp.int32, (ids.shape[0], table.shape[0]), 1)
    select = jnp.where(ids == lane, 1.0, 0.0)
    rows = jnp.dot(select.astype(low), table, preferred_element_type=jnp.float32)
    raw = jnp.dot(rows.astype(low), weight, preferred_element_type=jnp.float32)
    value, slope = gelu_both(raw)
    return select, rows, rows + value, slope


def generate_kernel(ids_ref, mask_ref, table_ref, w1_ref, w2_ref, out_ref, hidden, lines):
    slots, pixels, width = out_ref.shape

    @pl.when(pl.program_id(0) == 0)
    def _():
        hidden[...] = code_rows(ids_ref[...], table_ref[...], w1_ref[...])[2].astype(low)

    for p in range(pixels):
        made = jnp.dot(
            hidden[...], w2_ref[:, p * width : (p + 1) * width], preferred_element_type=jnp.float32
        )
        for c in range(0, width, 128):
            lines[c // 128, pl.ds(p, slots, stride=pixels), :] = (
                made[:, c : c + 128] * mask_ref[...]
            )
    for c in range(0, width, 128):
        out_ref[:, :, c : c + 128] = lines[c // 128].reshape(slots, pixels, 128).astype(low)


def generate_kernels(band_ids, band_mask, wave_table, gen_w1, gen_w2, width):
    slots = band_ids.shape[1]
    pixels = gen_w2.shape[1] // width
    part = 16
    return call(
        generate_kernel,
        "generate",
        (pixels // part,),
        [
            whole((slots, 1)),
            whole((slots, 1)),
            whole(wave_table.shape),
            whole(gen_w1.shape),
            pl.BlockSpec((gen_w2.shape[0], part * width), lambda i: (0, i)),
        ],
        pl.BlockSpec((slots, part, width), lambda i: (0, i, 0)),
        shape_of(slots, pixels, width, dtype=low),
        2 * 128 * slots * gen_w2.shape[1],
        2 * gen_w2.size,
        [
            pltpu.VMEM((slots, gen_w1.shape[0]), low),
            pltpu.VMEM((width // 128, slots * part, 128), jnp.float32),
        ],
        prefetch=0,
    )(band_ids.reshape(slots, 1), band_mask.reshape(slots, 1).astype(jnp.float32), wave_table, gen_w1, gen_w2)


def embed_kernel(count, place, kernel_ref, table_ref, gain_ref, weight_ref, *refs):
    pieces, (start_ref, normed_ref, out_ref) = refs[:count], refs[count:]
    rows = pieces[0].shape[0]
    sensor = lax.broadcasted_iota(jnp.int32, table_ref.shape, 0) == place[1]
    start = jnp.sum(
        jnp.where(sensor, table_ref[...].astype(jnp.float32), 0.0), axis=0, keepdims=True
    )
    for m, piece in enumerate(pieces):
        first = pl.multiple_of((place[0] ^ m) * rows, rows)
        start = start + dot32(piece[...], kernel_ref[pl.ds(first, rows), :], ROWS)
    start_ref[...] = start
    normed = (units(start)[0] * gain_ref[...]).astype(low)
    normed_ref[...] = normed
    out_ref[...] = jnp.dot(normed, weight_ref[...], preferred_element_type=jnp.float32).astype(low)


def embed(place, kernel, sensor_table, gain, weight, pieces):
    rows, tokens = pieces[0].shape
    width = weight.shape[0]
    return call(
        functools.partial(embed_kernel, len(pieces)),
        "embed",
        (tokens // BLOCK,),
        [whole(kernel.shape), whole(sensor_table.shape), whole((1, width)), whole(weight.shape)]
        + [pl.BlockSpec((rows, BLOCK), lambda i, s: (0, i))] * len(pieces),
        [
            pl.BlockSpec((BLOCK, width), lambda i, s: (i, 0)),
            pl.BlockSpec((BLOCK, width), lambda i, s: (i, 0)),
            pl.BlockSpec((BLOCK, 3 * width), lambda i, s: (i, 0)),
        ],
        [
            shape_of(tokens, width),
            shape_of(tokens, width, dtype=low),
            shape_of(tokens, 3 * width, dtype=low),
        ],
        2 * tokens * width * (kernel.shape[0] + 3 * width),
        14 * tokens * width + 2 * weight.size,
    )(place, kernel, sensor_table, gain.reshape(1, width), weight, *pieces)


def turn(step, groups, place):
    half = groups // 2
    core = place[0] % 2
    return (step % half) * 2 + jnp.where(step < half, 1 - core, core)


def split_units(term, total, groups, place, keep_ref, send_ref):
    each = total // groups // UNIT
    for unit in range(total // UNIT):
        group = unit // each
        first = ((group // 2) * each + unit % each) * UNIT
        mine = place[0] % 2 == group % 2
        part = term[unit * UNIT : (unit + 1) * UNIT]

        @pl.when(mine)
        def _():
            keep_ref[first : first + UNIT, :] = part

        @pl.when(jnp.logical_not(mine))
        def _():
            send_ref[first : first + UNIT, :] = part


def by_rows(tokens, work):
    def one(i, carry):
        work(pl.ds(pl.multiple_of(i * BLOCK, BLOCK), BLOCK))
        return carry

    lax.fori_loop(0, tokens // BLOCK, one, 0, unroll=True)


def mlp_kernel(
    blocks,
    groups,
    place,
    start_ref,
    mixed_ref,
    grad_ref,
    proj_ref,
    gain_ref,
    w1_ref,
    w2_ref,
    encoded_ref,
    out_ref,
    mixed_out_ref,
    sum_ref,
    send2_ref,
    keep2_ref,
    send1_ref,
    keep1_ref,
    send_ref,
    keep_ref,
    afters,
    totals,
    mixes,
    norms,
    act,
    hidden,
    back,
    sem,
):
    step = pl.program_id(0)
    tokens, width = afters.shape
    half = groups // 2
    last = blocks + groups
    write = pltpu.make_async_copy(totals, encoded_ref, sem)

    @pl.when(step < blocks)
    def _():
        rows = pl.ds(pl.multiple_of(step * BLOCK, BLOCK), BLOCK)
        mixed = mixed_ref[...]
        mixes[rows, :] = mixed
        after = start_ref[...] + jnp.dot(mixed, proj_ref[...], preferred_element_type=jnp.float32)
        afters[rows, :] = after
        totals[rows, :] = after
        norms[rows, :] = (units(after)[0] * gain_ref[...]).astype(low)
        back[rows, :] = jnp.zeros_like(after)

    @pl.when(jnp.logical_and(step >= blocks, step < last))
    def _():
        def work(rows):
            up = jnp.dot(norms[rows, :], w1_ref[...], preferred_element_type=jnp.float32)
            value, slope = gelu_both(up)
            value = value.astype(low)
            act[rows, :] = value
            totals[rows, :] += jnp.dot(value, w2_ref[...], preferred_element_type=jnp.float32)
            grad = (slope * dot32(grad_ref[rows, :], w2_ref[...], LANES)).astype(low)
            hidden[rows, :] = grad
            back[rows, :] += dot32(grad, w1_ref[...], LANES)

        by_rows(tokens, work)
        term2 = dot32(act[...], grad_ref[...], ROWS).astype(low)
        term1 = dot32(hidden[...], norms[...], ROWS).astype(low)

        @pl.when(step < blocks + half)
        def _():
            send2_ref[...] = term2
            send1_ref[...] = term1

        @pl.when(step >= blocks + half)
        def _():
            keep2_ref[...] = term2
            keep1_ref[...] = term1

    @pl.when(step == last)
    def _():
        write.start()
        sum_ref[...] = jnp.zeros_like(sum_ref)

    @pl.when(jnp.logical_and(step >= last, step < last + blocks))
    def _():
        rows = pl.ds(pl.multiple_of((step - last) * BLOCK, BLOCK), BLOCK)
        unit, inverse = units(afters[rows, :])
        grad_rows = back[rows, :]
        grad = grad_ref[rows, :].astype(jnp.float32) + norm_back(
            grad_rows, unit, inverse, gain_ref[...]
        )
        out_ref[...] = grad
        grad_low = grad.astype(low)
        norms[rows, :] = grad_low
        mixed_out_ref[...] = dot32(grad_low, proj_ref[...], LANES).astype(low)
        sum_ref[0:1, :] += jnp.sum(grad_rows * unit, axis=0, keepdims=True)

    @pl.when(step == last + blocks)
    def _():
        term = dot32(norms[...], mixes[...], ROWS).astype(low)
        split_units(term, width, groups, place, keep_ref, send_ref)
        write.wait()


def mlp_pass(place, start, mixed, out_grad, proj, gain, fc1, fc2, groups):
    tokens, width = start.shape
    wide = fc1.shape[1]
    size = wide // groups
    half = groups // 2
    blocks = tokens // BLOCK

    def once(shape):
        return pl.BlockSpec(shape, lambda *_: (0,) * len(shape), pipeline_mode=pl.Buffered(1))

    def chunk(i, s):
        return turn(jnp.clip(i - blocks, 0, groups - 1), groups, s)

    def part(first):
        return pl.BlockSpec(
            (size, width), lambda i, s: (jnp.clip(i - blocks - first, 0, half - 1), 0)
        )

    def rows_from(first):
        return pl.BlockSpec((BLOCK, width), lambda i, s: (jnp.clip(i - first, 0, blocks - 1), 0))

    halves = shape_of(wide // 2, width, dtype=low)
    small = (width // 2, width)
    full_low, full = (pltpu.VMEM((tokens, width), kind) for kind in (low, jnp.float32))
    return call(
        functools.partial(mlp_kernel, blocks, groups),
        "mlp_pass",
        (2 * blocks + groups + 1,),
        [rows_from(0), rows_from(0), once((tokens, width)), once(proj.shape), once((1, width))]
        + [
            pl.BlockSpec((width, size), lambda i, s: (0, chunk(i, s))),
            pl.BlockSpec((size, width), lambda i, s: (chunk(i, s), 0)),
        ],
        [pl.BlockSpec(memory_space=pl.ANY)]
        + [rows_from(blocks + groups), rows_from(blocks + groups), once((8, width))]
        + [part(0), part(half), part(0), part(half)]
        + [once(small), once(small)],
        [
            shape_of(tokens, width),
            shape_of(tokens, width),
            shape_of(tokens, width, dtype=low),
            shape_of(8, width),
        ]
        + [halves] * 4
        + [shape_of(*small, dtype=low)] * 2,
        2 * tokens * width * (3 * width + 6 * wide),
        20 * tokens * width + 8 * fc1.size,
        [full, full, full_low, full_low]
        + [pltpu.VMEM((tokens, size), low)] * 2
        + [full, pltpu.SemaphoreType.DMA],
        vmem=VM,
    )(place, start, mixed, out_grad, proj, gain.reshape(1, width), fc1, fc2)


def start_kernel(blocks, count, slots, place, *refs):
    back_refs, refs = refs[:PARTS], refs[PARTS:]
    weight_ref, start_ref, gain_ref, grad_ref, kernel_ref = refs[:5]
    pieces, refs = refs[5 : 5 + count], refs[5 + count :]
    sum_ref, keep_ref, send_ref, all_ref, pixel_ref, grads, lines = refs
    step = pl.program_id(0)
    width = start_ref.shape[1]

    @pl.when(step == 0)
    def _():
        sum_ref[...] = jnp.zeros_like(sum_ref)

    @pl.when(step < blocks)
    def _():
        back = 0.0
        for i, back_ref in enumerate(back_refs):
            some = back_ref.shape[2]
            for j in range(3):
                first = j * width + i * some
                back = back + dot32(back_ref[j], weight_ref[:, first : first + some], LANES)
        unit, inverse = units(start_ref[...])
        grad = grad_ref[...] + norm_back(back, unit, inverse, gain_ref[...])
        grads[pl.ds(pl.multiple_of(step * BLOCK, BLOCK), BLOCK), :] = grad.astype(low)
        sum_ref[0:1, :] += jnp.sum(back * unit, axis=0, keepdims=True)
        sum_ref[1:2, :] += jnp.sum(grad, axis=0, keepdims=True)

    @pl.when(step == blocks)
    def _():
        patch_terms(place, slots, grads, pieces, keep_ref, send_ref, all_ref, lines)

    @pl.when(step >= blocks)
    def _():
        pixel_ref[0] = dot32(kernel_ref[...], grads[...], LANES).astype(low)


def patch_terms(place, slots, grads, pieces, keep_ref, send_ref, all_ref, lines):
    count = len(pieces)
    rows = pieces[0].shape[0]
    per = slots // count
    pixels = rows // per
    width = grads.shape[1]
    for m, piece in enumerate(pieces):
        term = jnp.dot(piece[...], grads[...], preferred_element_type=jnp.float32)
        for s in range(per):
            slot = (place[0] ^ m) * per + s
            for c in range(0, width, 128):
                lines[c // 128, pl.ds(slot, pixels, stride=slots), :] = term[
                    s * pixels : (s + 1) * pixels, c : c + 128
                ]
    span = pixels * slots // count
    for j in range(count):
        mine = (place[0] & 1) == j % 2
        for c in range(0, width, 128):
            part = lines[c // 128, j * span : (j + 1) * span, :].astype(low)
            all_ref[j, :, c : c + 128] = part

        @pl.when(mine)
        def _():
            keep_ref[j // 2] = all_ref[j]

        @pl.when(jnp.logical_not(mine))
        def _():
            send_ref[j // 2] = all_ref[j]


def start_pass(place, backs, weight, start, gain, grad_after, kernel, pieces, slots, behind):
    tokens, width = start.shape
    count = len(pieces)
    rows = pieces[0].shape[0]
    blocks = tokens // BLOCK

    def row_block(i):
        return jnp.minimum(i, blocks - 1)

    def turned(i):
        return jnp.maximum(i - blocks, 0)

    block = pl.BlockSpec((BLOCK, width), lambda i, s: (row_block(i), 0))
    return call(
        functools.partial(start_kernel, blocks, count, slots),
        "start_pass",
        (blocks + count,),
        [pl.BlockSpec((3, BLOCK, width // PARTS), lambda i, s: (0, row_block(i), 0))] * PARTS
        + [whole(weight.shape), block, whole((1, width)), block]
        + [pl.BlockSpec((rows, width), lambda i, s: (s[0] ^ turned(i), 0))]
        + [whole(pieces[0].shape)] * count,
        [
            whole((8, width)),
            whole((count // 2, rows, width)),
            whole((count // 2, rows, width)),
            whole((count, rows, width)),
            pl.BlockSpec((1, rows, tokens), lambda i, s: (turned(i), 0, 0)),
        ],
        [
            shape_of(8, width),
            shape_of(count // 2, rows, width, dtype=low),
            shape_of(count // 2, rows, width, dtype=low),
            shape_of(count, rows, width, dtype=low),
            shape_of(count, rows, tokens, dtype=low),
        ],
        2 * tokens * width * (3 * width + 2 * rows * count),
        16 * tokens * width + 2 * weight.size,
        [
            pltpu.VMEM((tokens, width), low),
            pltpu.VMEM((width // 128, rows * count, 128), jnp.float32),
        ],
        behind=behind,
    )(place, *backs, weight, start, gain.reshape(1, width), grad_after, kernel, *pieces)


def term_kernel(groups, total, place, *refs):
    lefts, (right_ref, keep_ref, send_ref) = refs[:-3], refs[-3:]
    tokens, width = right_ref.shape
    if len(lefts) == 1:
        left = lefts[0][...]
    else:
        left = jnp.concatenate([ref[0] for ref in lefts], axis=1)
    term = dot32(left, right_ref[...], ROWS).astype(low)
    each = total // groups // UNIT
    for u in range(width // UNIT):
        unit = pl.program_id(0) * (width // UNIT) + u
        group = unit // each
        first = pl.multiple_of(((group // 2) * each + unit % each) * UNIT, UNIT)
        mine = group % 2 == place[0] % 2
        part = term[u * UNIT : (u + 1) * UNIT]

        @pl.when(mine)
        def _():
            keep_ref[pl.ds(first, UNIT), :] = part

        @pl.when(jnp.logical_not(mine))
        def _():
            send_ref[pl.ds(first, UNIT), :] = part


def weight_term(place, lefts, right, groups, name, behind=()):
    tokens, width = right.shape
    if len(lefts) > 1:
        total = lefts[0].shape[0] * width
        blocks = [
            pl.BlockSpec((1, tokens, left.shape[2]), lambda i, s: (i, 0, 0)) for left in lefts
        ]
    else:
        total = lefts[0].shape[1]
        blocks = [pl.BlockSpec((tokens, width), lambda i, s: (0, i))]
    half = (total // 2, width)
    return call(
        functools.partial(term_kernel, groups, total),
        name,
        (total // width,),
        blocks + [whole(right.shape)],
        [whole(half), whole(half)],
        [shape_of(*half, dtype=low)] * 2,
        2 * tokens * total * width,
        2 * (tokens * total + right.size + total * width),
        behind=behind,
    )(place, *lefts, right)


def hidden_kernel(slots, term_ref, w2_ref, out_ref):
    width = term_ref.shape[1]

    @pl.when(pl.program_id(0) == 0)
    def _():
        out_ref[...] = jnp.zeros_like(out_ref)

    total = out_ref[...]
    for p in range(term_ref.shape[0] // slots):
        total = total + dot32(
            term_ref[p * slots : (p + 1) * slots, :], w2_ref[:, p * width : (p + 1) * width], LANES
        )
    out_ref[...] = total


def hidden_term(term, gen_w2, slots, behind=()):
    rows, width = term.shape
    part = 16
    pixels = rows // slots
    codes = gen_w2.shape[0]
    return call(
        functools.partial(hidden_kernel, slots),
        "hidden_term",
        (pixels // part,),
        [
            pl.BlockSpec((part * slots, width), lambda i: (i, 0)),
            pl.BlockSpec((codes, part * width), lambda i: (0, i)),
        ],
        whole((slots, codes)),
        shape_of(slots, codes),
        2 * rows * width * codes,
        2 * gen_w2.size,
        prefetch=0,
        behind=behind,
    )(term, gen_w2)


def join_kernel(place, *refs):
    out_ref = refs[-1]
    for m, piece in enumerate(refs[:-1]):

        @pl.when(pl.program_id(0) == m)
        def _():
            out_ref[...] = piece[...].astype(jnp.float32)


def join_pixels(place, pieces, behind):
    rows, tokens = pieces[0].shape
    count = len(pieces)
    return call(
        join_kernel,
        "join_pixels",
        (count,),
        [whole(pieces[0].shape)] * count,
        pl.BlockSpec((rows, tokens), lambda i, s: (0, s[0] ^ i)),
        shape_of(rows, count * tokens),
        0,
        6 * rows * count * tokens,
        behind=behind,
    )(place, *pieces)


def finish_kernel(slots, sensors, place, small_ref, rows_ref, table_ref, w1_ref, wave_ref, gen1_ref, gen2_ref, sensor_ref, norm_ref):
    groups = small_ref.shape[0]
    bands = wave_ref.shape[0]
    table, weight = table_ref[...], w1_ref[...]
    lines = norm_ref.shape[1]
    ids = [small_ref[q, slots : 2 * slots, :bands].astype(jnp.int32) for q in range(groups)]
    hidden = code_rows(jnp.concatenate(ids, axis=0), table, weight)[2].astype(low)
    for i in range(rows_ref.shape[0]):
        wide = rows_ref.shape[2]
        gen2_ref[:, i * wide : (i + 1) * wide] = dot32(hidden, rows_ref[i], ROWS)

    in_order = [place[2] ^ g for g in range(groups)]
    ids = [small_ref[q, slots : 2 * slots, :bands].astype(jnp.int32) for q in in_order]
    select, rows, _, slope = code_rows(jnp.concatenate(ids, axis=0), table, weight)
    grad = jnp.concatenate([small_ref[q, :slots, :] for q in in_order], axis=0)
    scaled = slope * grad
    gen1_ref[...] = lax.dot_general(
        rows, scaled, ROWS, precision=highest, preferred_element_type=jnp.float32
    )
    row_grad = grad + lax.dot_general(
        scaled,
        weight.astype(jnp.float32),
        LANES,
        precision=highest,
        preferred_element_type=jnp.float32,
    )
    wave_ref[...] = lax.dot_general(
        select, row_grad, ROWS, precision=highest, preferred_element_type=jnp.float32
    )
    first = 2 * slots
    norms = [jnp.zeros((lines, 128), jnp.float32)] * 2
    each = [jnp.zeros((lines, 128), jnp.float32)] * sensors
    for q in in_order:
        for n in range(2):
            norms[n] = norms[n] + small_ref[q, first + n * lines : first + (n + 1) * lines, :]
        line = small_ref[q, first + 2 * lines : first + 3 * lines, :]
        tag = small_ref[q, first + 3 * lines : first + 3 * lines + 1, :]
        for s in range(sensors):
            each[s] = each[s] + jnp.where(tag == float(s), line, 0.0)
    for n in range(2):
        norm_ref[n] = norms[n]
    for s in range(sensors):
        sensor_ref[s] = each[s]


def finish(place, small, rows, wave_table, gen_w1, slots, sensors, width):
    lines = width // 128
    codes = wave_table.shape[1]
    shapes = [
        wave_table.shape,
        gen_w1.shape,
        (codes, rows.shape[0] * rows.shape[2]),
        (sensors, lines, 128),
        (2, lines, 128),
    ]
    return call(
        functools.partial(finish_kernel, slots, sensors),
        "finish",
        (1,),
        [whole(small.shape), whole(rows.shape), whole(wave_table.shape), whole(gen_w1.shape)],
        [whole(shape) for shape in shapes],
        [shape_of(*shape) for shape in shapes],
        2 * rows.size * codes,
        4 * rows.size,
    )(place, small, rows, wave_table, gen_w1)


def swap(piece, axis, mask):
    count = lax.axis_size(axis)
    return lax.ppermute(piece, axis, [(i, i ^ mask) for i in range(count)])


def bits_of(axis):
    return lax.axis_size(axis).bit_length() - 1


class Scatter:
    def __init__(self, keep, send):
        self.dims = [("band", bit) for bit in reversed(range(1, bits_of("band")))] + [
            ("dp", bit) for bit in reversed(range(bits_of("dp")))
        ]
        rows = keep.shape[0] >> len(self.dims)
        shape = (2,) * len(self.dims) + (rows, keep.shape[1])
        got = swap(send, "band", 1)
        self.last = got
        self.parts = [keep.reshape(shape), got.reshape(shape)]

    def columns(self, first, last):
        some = object.__new__(Scatter)
        some.dims = list(self.dims)
        some.last = self.last
        some.parts = [part[..., first:last] for part in self.parts]
        return some

    def result(self):
        return sum(part.astype(jnp.float32) for part in self.parts)


def halve(sums, axis, bit, when=()):
    mine = (lax.axis_index(axis) >> bit) & 1
    mine, _ = lax.optimization_barrier((mine, when))
    sends = []
    for one in sums:
        dim = one.dims.index((axis, bit))
        one.dims.pop(dim)
        send = sum(
            lax.dynamic_index_in_dim(part, 1 - mine, dim, False).astype(jnp.float32)
            for part in one.parts
        )
        sends.append(send.astype(low))
        one.parts = [lax.dynamic_index_in_dim(part, mine, dim, False) for part in one.parts]
    send = sends[0] if len(sends) == 1 else jnp.concatenate(sends, axis=-2)
    got = swap(send, axis, 1 << bit)
    first = 0
    for one, each in zip(sums, sends):
        rows = each.shape[-2]
        one.parts.append(lax.slice_in_dim(got, first, first + rows, axis=got.ndim - 2))
        one.last = got
        first += rows
    return send


def exchange(pieces, axis):
    count = lax.axis_size(axis)
    shape = pieces.shape
    held = pieces
    for bit in range(bits_of(axis)):
        view = held.reshape((count >> (bit + 1), 2, 1 << bit) + shape[1:])
        got = swap(view[:, 1], axis, 1 << bit)
        held = jnp.stack([view[:, 0], got], axis=1).reshape(shape)
    return held


def gather_xor(piece, axis):
    held = piece[None]
    for bit in range(bits_of(axis)):
        held = jnp.concatenate([held, swap(held, axis, 1 << bit)], axis=0)
    return held


def shards(
    pixels,
    band_ids,
    band_mask,
    sensor_tags,
    segment_ids,
    wave_table,
    gen_w1,
    gen_w2,
    sensor_table,
    ln1_gain,
    qkv_weight,
    proj_weight,
    ln2_gain,
    fc1_weight,
    fc2_weight,
    out_grad,
):
    band_place = lax.axis_index("band")
    dp_place = lax.axis_index("dp")
    band_count = lax.axis_size("band")
    dp_count = lax.axis_size("dp")
    slots_dev = pixels.shape[0]
    slots = band_ids.shape[1]
    tok_dev, model_width = out_grad.shape
    patch_pixels = pixels.shape[2]
    sensors = sensor_table.shape[0]
    code_width = wave_table.shape[1]
    part_rows = slots_dev * patch_pixels
    lines = model_width // 128
    place = jnp.stack([band_place, sensor_tags[0], dp_place]).astype(jnp.int32)

    own_pixels = pixels.transpose(0, 2, 1).reshape(part_rows, -1)
    pieces = []
    for mask in range(band_count):
        piece = lax.dynamic_slice_in_dim(own_pixels, (band_place ^ mask) * tok_dev, tok_dev, 1)
        pieces.append(swap(piece, "band", mask) if mask else piece)

    kernel = generate_kernels(band_ids, band_mask, wave_table, gen_w1, gen_w2, model_width)
    kernel = kernel.reshape(slots * patch_pixels, model_width)
    start_rows, normed1, projected = embed(
        place, kernel, sensor_table, ln1_gain, qkv_weight, pieces
    )
    window = windows(segment_ids)
    query_side, key_side = features(segment_ids)
    attended, totals = attend_forward(projected, segment_ids, window, query_side, key_side)
    encoded, grad_after, grad_attended, norm2_sums, *halves = mlp_pass(
        place,
        start_rows,
        attended,
        out_grad,
        proj_weight,
        ln2_gain,
        fc1_weight,
        fc2_weight,
        band_count,
    )
    band_rest = [("band", bit) for bit in range(1, bits_of("band"))]
    dp_rest = [("dp", bit) for bit in range(bits_of("dp"))]
    fc2_sum, fc1_sum, proj_sum = [
        Scatter(keep, send) for send, keep in zip(halves[0::2], halves[1::2])
    ]
    sent = [halve([fc2_sum], *band_rest[0])]
    for item in band_rest[1:]:
        sent.append(halve([fc2_sum], *item))
    sent.append(halve([fc1_sum, proj_sum], *dp_rest[0]))
    backs = []

    def back_part(behind):
        backs.append(
            attend_back(
                projected,
                segment_ids,
                window,
                query_side,
                key_side,
                grad_attended,
                attended,
                totals,
                len(backs),
                behind,
            )
        )

    back_part(sent)
    sent = [fc2_sum.last, fc1_sum.last]
    sent.append(halve([fc2_sum], *dp_rest[0], backs[-1]))
    for item in band_rest:
        sent.append(halve([fc1_sum, proj_sum], *item, backs[-1]))
    back_part(sent)
    sent = [fc2_sum.last, fc1_sum.last]
    sent.append(halve([fc2_sum, fc1_sum, proj_sum], *dp_rest[1], backs[-1]))
    back_part(sent)
    sent = [fc2_sum.last]
    sent.append(halve([fc2_sum, fc1_sum, proj_sum], *dp_rest[2], backs[-1]))
    norm1_sums, keep, send, patch_all, pixel_parts = start_pass(
        place,
        backs,
        qkv_weight,
        start_rows,
        ln1_gain,
        grad_after,
        kernel,
        pieces,
        slots,
        sent,
    )

    patch_parts = [keep, swap(send, "band", 1)]
    for item in dp_rest[3:]:
        halve([fc2_sum, fc1_sum, proj_sum], *item)
    qkv_sum = Scatter(
        *weight_term(place, backs, normed1, band_count, "qkv_term", [keep, fc2_sum.last])
    )
    qkv_halves = [
        qkv_sum.columns(0, model_width // 2),
        qkv_sum.columns(model_width // 2, model_width),
    ]
    for bit in range(1, bits_of("band")):
        mine = (band_place >> bit) & 1
        patch_parts = [
            part.reshape((part.shape[0] // 2, 2) + part.shape[1:])
            for part in patch_parts
        ]
        sent = sum(
            lax.dynamic_index_in_dim(part, 1 - mine, 1, False).astype(jnp.float32)
            for part in patch_parts
        ).astype(low)
        patch_parts = [lax.dynamic_index_in_dim(part, mine, 1, False) for part in patch_parts]
        patch_parts.append(swap(sent, "band", 1 << bit))
    sent = [halve(qkv_halves[:1], *dp_rest[0]), halve(qkv_halves[1:], *band_rest[0])]
    for item in band_rest[1:]:
        halve(qkv_halves[1:], *item)
    hidden_grad = hidden_term(
        patch_all.reshape(-1, model_width), gen_w2, slots, sent + [patch_parts[-1]]
    ) * band_mask[0].astype(jnp.float32)[:, None]
    span = patch_pixels // band_count
    patch_sum = sum(part.astype(jnp.float32) for part in patch_parts).reshape(
        span, slots, model_width
    )
    patch_low = (patch_sum * band_mask[0].astype(jnp.float32)[None, :, None]).astype(low)
    cuts = max(1, dp_count // span)
    share = model_width // cuts
    if cuts > 1:
        patch_low = patch_low.reshape(span, slots, cuts, share).transpose(0, 2, 1, 3)
    patch_low = patch_low.reshape(dp_count, -1, slots, share)
    patch_low = jnp.stack(
        [lax.dynamic_index_in_dim(patch_low, dp_place ^ i, 0, False) for i in range(dp_count)]
    )
    kernel_rows = exchange(patch_low, "dp").transpose(1, 0, 2, 3)
    kernel_rows = kernel_rows.reshape(kernel_rows.shape[0], dp_count * slots, share)

    first = (band_place == 0).astype(jnp.float32)
    ids_wide = jnp.broadcast_to(band_ids[0].astype(jnp.float32)[:, None], (slots, code_width))
    tag_wide = jnp.broadcast_to(sensor_tags.astype(jnp.float32)[:, None], (1, code_width))
    small = jnp.concatenate(
        [
            hidden_grad,
            ids_wide * first,
            norm1_sums[0].reshape(lines, 128),
            norm2_sums[0].reshape(lines, 128),
            norm1_sums[1].reshape(lines, 128),
            tag_wide * first,
        ]
    )
    small = jnp.pad(small, ((0, -small.shape[0] % 8), (0, 0)))
    for bit in range(bits_of("band")):
        small = small + swap(small, "band", 1 << bit)
    all_small = gather_xor(small, "dp")
    wave_table_grad, gen_w1_grad, gen_w2_grad, sensor_grad, norm_grads = finish(
        place, all_small, kernel_rows, wave_table, gen_w1, slots, sensors, model_width
    )

    sent = [halve(qkv_halves[1:], *dp_rest[0])]
    for item in band_rest:
        sent.append(halve(qkv_halves[:1], *item))
    for item in dp_rest[1:]:
        halve(qkv_halves, *item)
    grad_pixels = join_pixels(
        place,
        [
            swap(pixel_parts[mask], "band", mask) if mask else pixel_parts[0]
            for mask in range(band_count)
        ],
        sent,
    )
    grad_pixels = grad_pixels.reshape(slots_dev, patch_pixels, -1).transpose(0, 2, 1)

    qkv_grad = jnp.concatenate([half.result() for half in qkv_halves], axis=1)
    fc2_grad, fc1_grad, proj_grad = fc2_sum.result(), fc1_sum.result(), proj_sum.result()
    return (
        encoded,
        grad_pixels,
        wave_table_grad,
        gen_w1_grad,
        gen_w2_grad,
        sensor_grad.reshape(sensors, model_width),
        norm_grads[0].reshape(model_width),
        qkv_grad.T,
        proj_grad.T,
        norm_grads[1].reshape(model_width),
        fc1_grad.T,
        fc2_grad,
    )


def solution(mesh):
    return jax.shard_map(
        shards,
        mesh=mesh,
        in_specs=(
            P("band", "dp", None),
            P("dp", None),
            P("dp", None),
            P("dp"),
            P(("dp", "band"), None),
            P(),
            P(),
            P(),
            P(),
            P(),
            P(),
            P(),
            P(),
            P(),
            P(),
            P(("dp", "band"), None),
        ),
        out_specs=(
            P(("dp", "band"), None),
            P("band", "dp", None),
            P(),
            P(),
            P(None, ("band", "dp")),
            P(),
            P(),
            P(None, ("band", "dp")),
            P(None, ("band", "dp")),
            P(),
            P(None, ("band", "dp")),
            P(("band", "dp"), None),
        ),
        check_vma=False,
    )
```

```python
import functools

import jax
import jax.numpy as jnp
from jax import lax
from jax.experimental import pallas as pl
from jax.experimental.pallas import tpu as pltpu
from jax.sharding import PartitionSpec as P

highest = lax.Precision.HIGHEST
UNIT = 96
PARTS = 3
VA = 58
CUTS = 32
VM = 56
low = jnp.bfloat16
MIB = 1 << 20

BLOCK = 256
STEP = 128
FAR = 2.0**30
LANES = (((1,), (1,)), ((), ()))
ROWS = (((0,), (0,)), ((), ()))


def dot32(left, right, dims):
    return lax.dot_general(left, right, dims, preferred_element_type=jnp.float32)


def windows(segment_ids):
    length = segment_ids.shape[1]
    first = segment_ids[:, ::BLOCK]
    last = segment_ids[:, BLOCK - 1 :: BLOCK]
    begin = jnp.sum(segment_ids[:, None, :] < first[:, :, None], axis=-1)
    end = jnp.sum(segment_ids[:, None, :] <= last[:, :, None], axis=-1)
    low = begin // STEP
    count = (end + STEP - 1) // STEP - low
    return jnp.stack([low, count - 1], axis=-1).astype(jnp.int32).reshape(-1)


def features(segment_ids):
    lane = jnp.arange(128, dtype=jnp.int32)
    code = segment_ids.reshape(-1, 1)
    same = (code == (lane % 64)[None, :])
    used = (lane % 64 < 4)[None, :]
    query_side = jnp.where(same & used, 1.0, 0.0)
    key_side = jnp.where(used & ~same, -FAR, 0.0)
    return query_side.astype(jnp.bfloat16), key_side.astype(jnp.bfloat16)


def head_masks():
    lane = lax.broadcasted_iota(jnp.int32, (1, 128), 1)
    low = jnp.where(lane < 64, 1.0, 0.0)
    return low.astype(jnp.bfloat16), (1.0 - low).astype(jnp.bfloat16)


def forward_kernel(win, q_ref, k_ref, v_ref, qf_ref, kf_ref, o_ref, lse_ref, qa, ka, va):
    length = q_ref.shape[0]
    blocks = length // BLOCK
    base = pl.program_id(0) * blocks * 2
    for h, mask in enumerate(head_masks()):
        other = jnp.bfloat16(1.0) - mask
        qa[h] = q_ref[...] * (mask * jnp.bfloat16(0.125)) + qf_ref[...] * other
        ka[h] = k_ref[...] * mask + kf_ref[...] * other
        va[h] = v_ref[...] * mask + other

    def one_block(block, carry):
        rows = pl.ds(pl.multiple_of(block * BLOCK, BLOCK), BLOCK)
        low = pl.multiple_of(win[base + 2 * block] * STEP, STEP)

        def run(width):
            keys = pl.ds(low, width)
            mixes, peaks = [], []
            for h in range(2):
                scores = dot32(qa[h, rows, :], ka[h, keys, :], LANES)
                peak = jnp.max(scores, axis=1, keepdims=True)
                probs = jnp.exp(scores - peak).astype(jnp.bfloat16)
                mixes.append(jnp.dot(probs, va[h, keys, :], preferred_element_type=jnp.float32))
                peaks.append(peak)
            low_lanes = lax.broadcasted_iota(jnp.int32, (1, 128), 1) < 64
            mixed = jnp.where(low_lanes, mixes[0], mixes[1])
            total = pltpu.roll(jnp.where(low_lanes, mixes[1], mixes[0]), 64, 1)
            o_ref[rows, :] = (mixed / total).astype(jnp.bfloat16)
            both = (jnp.where(low_lanes, peaks[0], peaks[1]) + jnp.log(total)).T
            lse_ref[0, 0, 0:1, rows] = both[0:1]
            lse_ref[0, 0, 1:2, rows] = both[64:65]

        count = win[base + 2 * block + 1]
        for size in range(length // STEP):
            pl.when(count == size)(functools.partial(run, (size + 1) * STEP))
        return carry

    lax.fori_loop(0, blocks, one_block, 0)


def back_kernel(win, q_ref, k_ref, v_ref, qf_ref, kf_ref, g_ref, o_ref, lse_ref, out_ref, qa, ka, qh, kh, vh, gh, delta, dk, dv):
    length = q_ref.shape[0]
    blocks = length // BLOCK
    base = pl.program_id(0) * blocks * 2
    masks = head_masks()
    for h, mask in enumerate(masks):
        other = jnp.bfloat16(1.0) - mask
        scaled = q_ref[...] * (mask * jnp.bfloat16(0.125))
        qh[h] = scaled
        qa[h] = scaled + qf_ref[...] * other
        own = k_ref[...] * mask
        kh[h] = own
        ka[h] = own + kf_ref[...] * other
        vh[h] = v_ref[...] * mask
        gh[h] = g_ref[...] * mask
    product = g_ref[...].astype(jnp.float32) * o_ref[...].astype(jnp.float32)
    turned = product.T
    delta[0:1, :] = jnp.sum(turned[:64], axis=0, keepdims=True)
    delta[1:2, :] = jnp.sum(turned[64:], axis=0, keepdims=True)
    dk[...] = jnp.zeros_like(dk)
    dv[...] = jnp.zeros_like(dv)

    def one_block(block, carry):
        rows = pl.ds(pl.multiple_of(block * BLOCK, BLOCK), BLOCK)
        low = pl.multiple_of(win[base + 2 * block] * STEP, STEP)

        def run(width):
            keys = pl.ds(low, width)
            turned_grad = None
            for h in range(2):
                scores = dot32(ka[h, keys, :], qa[h, rows, :], LANES)
                probs = jnp.exp(scores - lse_ref[0, 0, h : h + 1, rows])
                grad_probs = dot32(vh[h, keys, :], gh[h, rows, :], LANES)
                grad_scores = (probs * (grad_probs - delta[h : h + 1, rows])).astype(jnp.bfloat16)
                dv[keys, :] += jnp.dot(probs.astype(jnp.bfloat16), gh[h, rows, :], preferred_element_type=jnp.float32)
                dk[keys, :] += jnp.dot(grad_scores, qh[h, rows, :], preferred_element_type=jnp.float32)
                term = dot32(grad_scores, kh[h, keys, :], ROWS)
                turned_grad = term if h == 0 else turned_grad + term
            out_ref[0, rows, :] = (turned_grad * 0.125).astype(jnp.bfloat16)

        count = win[base + 2 * block + 1]
        for size in range(length // STEP):
            pl.when(count == size)(functools.partial(run, (size + 1) * STEP))
        return carry

    lax.fori_loop(0, blocks, one_block, 0)
    out_ref[1] = dk[...].astype(jnp.bfloat16)
    out_ref[2] = dv[...].astype(jnp.bfloat16)


def attend_forward(projected, segment_ids, win, query_side, key_side):
    seqs, length = segment_ids.shape
    width = projected.shape[1] // 3
    pairs = width // 128

    def columns(offset):
        return pl.BlockSpec((length, 128), lambda s, p, w: (s, p + offset))

    fixed = pl.BlockSpec((length, 128), lambda s, p, w: (s, 0))
    return call(
        forward_kernel,
        "attend_forward",
        (seqs, pairs),
        [columns(0), columns(pairs), columns(2 * pairs), fixed, fixed],
        [columns(0), pl.BlockSpec((1, 1, 8, length), lambda s, p, w: (s, p, 0, 0))],
        [
            shape_of(seqs * length, width, dtype=low),
            shape_of(seqs, pairs, 8, length),
        ],
        4 * seqs * length * length * width,
        8 * seqs * length * width,
        [pltpu.VMEM((2, length, 128), low)] * 3,
        vmem=VA,
    )(win, projected, projected, projected, query_side, key_side)


def attend_back(projected, segment_ids, win, query_side, key_side, grad, mixed, lse, part, behind):
    seqs, length = segment_ids.shape
    width = projected.shape[1] // 3
    pairs = width // 128
    run = pairs // PARTS
    begin = part * run

    def columns(offset):
        return pl.BlockSpec((length, 128), lambda s, p, w: (s, p + offset + begin))

    fixed = pl.BlockSpec((length, 128), lambda s, p, w: (s, 0))
    pair_low = pltpu.VMEM((2, length, 128), low)
    return call(
        back_kernel,
        "attend_back",
        (seqs, run),
        [
            columns(0),
            columns(pairs),
            columns(2 * pairs),
            fixed,
            fixed,
            columns(0),
            columns(0),
            pl.BlockSpec((1, 1, 8, length), lambda s, p, w: (s, p + begin, 0, 0)),
        ],
        pl.BlockSpec((3, length, 128), lambda s, p, w: (0, s, p)),
        shape_of(3, seqs * length, run * 128, dtype=low),
        10 * seqs * length * length * run * 128,
        14 * seqs * length * run * 128,
        [pair_low] * 6
        + [
            pltpu.VMEM((8, length), jnp.float32),
            pltpu.VMEM((length, 128), jnp.float32),
            pltpu.VMEM((length, 128), jnp.float32),
        ],
        vmem=VA,
        behind=behind,
    )(win, projected, projected, projected, query_side, key_side, grad, mixed, lse)


def whole(shape):
    return pl.BlockSpec(shape, lambda *_: (0,) * len(shape))


def call(
    kernel,
    name,
    grid,
    in_specs,
    out_specs,
    out_shape,
    flops,
    moved,
    scratch=(),
    prefetch=1,
    vmem=40,
    behind=(),
):
    first = prefetch + len(in_specs)

    def body(*refs):
        kernel(*refs[:first], *refs[first + len(behind) :])

    run = pl.pallas_call(
        body,
        grid_spec=pltpu.PrefetchScalarGridSpec(
            num_scalar_prefetch=prefetch,
            grid=grid,
            in_specs=list(in_specs) + [pl.BlockSpec(memory_space=pl.ANY)] * len(behind),
            out_specs=out_specs,
            scratch_shapes=list(scratch),
        ),
        out_shape=out_shape,
        compiler_params=pltpu.CompilerParams(vmem_limit_bytes=vmem * MIB),
        cost_estimate=pl.CostEstimate(flops=flops, bytes_accessed=moved, transcendentals=0),
        name=name,
    )
    return lambda *args: run(*args, *behind)


def shape_of(*shape, dtype=jnp.float32):
    return jax.ShapeDtypeStruct(shape, dtype)


def units(rows):
    center = rows - jnp.mean(rows, axis=-1, keepdims=True)
    inverse = lax.rsqrt(jnp.mean(center * center, axis=-1, keepdims=True) + 1e-05)
    return center * inverse, inverse


def norm_back(grad_rows, unit_rows, inverse, gain):
    scaled = grad_rows * gain
    inner = jnp.mean(scaled * unit_rows, axis=-1, keepdims=True)
    return inverse * (scaled - jnp.mean(scaled, axis=-1, keepdims=True) - unit_rows * inner)


def gelu_both(rows):
    root = 0.7978845608028654
    square = rows * rows
    curve = jnp.tanh(rows * (root + (root * 0.044715) * square))
    half = 0.5 + 0.5 * curve
    slope = half + (0.5 * rows) * (1.0 - curve * curve) * (root + (3.0 * root * 0.044715) * square)
    return rows * half, slope


def code_rows(ids, table, weight):
    lane = lax.broadcasted_iota(jnp.int32, (ids.shape[0], table.shape[0]), 1)
    select = jnp.where(ids == lane, 1.0, 0.0)
    rows = jnp.dot(select.astype(low), table, preferred_element_type=jnp.float32)
    raw = jnp.dot(rows.astype(low), weight, preferred_element_type=jnp.float32)
    value, slope = gelu_both(raw)
    return select, rows, rows + value, slope


def generate_kernel(ids_ref, mask_ref, table_ref, w1_ref, w2_ref, out_ref, hidden, lines):
    slots, pixels, width = out_ref.shape

    @pl.when(pl.program_id(0) == 0)
    def _():
        hidden[...] = code_rows(ids_ref[...], table_ref[...], w1_ref[...])[2].astype(low)

    for p in range(pixels):
        made = jnp.dot(
            hidden[...], w2_ref[:, p * width : (p + 1) * width], preferred_element_type=jnp.float32
        )
        for c in range(0, width, 128):
            lines[c // 128, pl.ds(p, slots, stride=pixels), :] = (
                made[:, c : c + 128] * mask_ref[...]
            )
    for c in range(0, width, 128):
        out_ref[:, :, c : c + 128] = lines[c // 128].reshape(slots, pixels, 128).astype(low)


def generate_kernels(band_ids, band_mask, wave_table, gen_w1, gen_w2, width):
    slots = band_ids.shape[1]
    pixels = gen_w2.shape[1] // width
    part = 16
    return call(
        generate_kernel,
        "generate",
        (pixels // part,),
        [
            whole((slots, 1)),
            whole((slots, 1)),
            whole(wave_table.shape),
            whole(gen_w1.shape),
            pl.BlockSpec((gen_w2.shape[0], part * width), lambda i: (0, i)),
        ],
        pl.BlockSpec((slots, part, width), lambda i: (0, i, 0)),
        shape_of(slots, pixels, width, dtype=low),
        2 * 128 * slots * gen_w2.shape[1],
        2 * gen_w2.size,
        [
            pltpu.VMEM((slots, gen_w1.shape[0]), low),
            pltpu.VMEM((width // 128, slots * part, 128), jnp.float32),
        ],
        prefetch=0,
    )(band_ids.reshape(slots, 1), band_mask.reshape(slots, 1).astype(jnp.float32), wave_table, gen_w1, gen_w2)


def embed_kernel(count, place, kernel_ref, table_ref, gain_ref, weight_ref, *refs):
    pieces, (start_ref, normed_ref, out_ref) = refs[:count], refs[count:]
    rows = pieces[0].shape[0]
    sensor = lax.broadcasted_iota(jnp.int32, table_ref.shape, 0) == place[1]
    start = jnp.sum(
        jnp.where(sensor, table_ref[...].astype(jnp.float32), 0.0), axis=0, keepdims=True
    )
    for m, piece in enumerate(pieces):
        first = pl.multiple_of((place[0] ^ m) * rows, rows)
        start = start + dot32(piece[...], kernel_ref[pl.ds(first, rows), :], ROWS)
    start_ref[...] = start
    normed = (units(start)[0] * gain_ref[...]).astype(low)
    normed_ref[...] = normed
    out_ref[...] = jnp.dot(normed, weight_ref[...], preferred_element_type=jnp.float32).astype(low)


def embed(place, kernel, sensor_table, gain, weight, pieces):
    rows, tokens = pieces[0].shape
    width = weight.shape[0]
    return call(
        functools.partial(embed_kernel, len(pieces)),
        "embed",
        (tokens // BLOCK,),
        [whole(kernel.shape), whole(sensor_table.shape), whole((1, width)), whole(weight.shape)]
        + [pl.BlockSpec((rows, BLOCK), lambda i, s: (0, i))] * len(pieces),
        [
            pl.BlockSpec((BLOCK, width), lambda i, s: (i, 0)),
            pl.BlockSpec((BLOCK, width), lambda i, s: (i, 0)),
            pl.BlockSpec((BLOCK, 3 * width), lambda i, s: (i, 0)),
        ],
        [
            shape_of(tokens, width),
            shape_of(tokens, width, dtype=low),
            shape_of(tokens, 3 * width, dtype=low),
        ],
        2 * tokens * width * (kernel.shape[0] + 3 * width),
        14 * tokens * width + 2 * weight.size,
    )(place, kernel, sensor_table, gain.reshape(1, width), weight, *pieces)


def turn(step, groups, place):
    half = groups // 2
    core = place[0] % 2
    return (step % half) * 2 + jnp.where(step < half, 1 - core, core)


def by_rows(tokens, work):
    def one(i, carry):
        work(pl.ds(pl.multiple_of(i * BLOCK, BLOCK), BLOCK))
        return carry

    lax.fori_loop(0, tokens // BLOCK, one, 0, unroll=True)


def mlp_kernel(
    blocks,
    groups,
    place,
    start_ref,
    mixed_ref,
    grad_ref,
    proj_ref,
    gain_ref,
    w1_ref,
    w2_ref,
    encoded_ref,
    out_ref,
    mixed_out_ref,
    sum_ref,
    send2_ref,
    keep2_ref,
    send1_ref,
    keep1_ref,
    afters,
    totals,
    mixes,
    norms,
    act,
    hidden,
    back,
    sem,
):
    step = pl.program_id(0)
    tokens, width = afters.shape
    half = groups // 2
    last = blocks + groups
    write = pltpu.make_async_copy(totals, encoded_ref, sem)

    @pl.when(step < blocks)
    def _():
        rows = pl.ds(pl.multiple_of(step * BLOCK, BLOCK), BLOCK)
        mixed = mixed_ref[...]
        mixes[rows, :] = mixed
        after = start_ref[...] + jnp.dot(mixed, proj_ref[...], preferred_element_type=jnp.float32)
        afters[rows, :] = after
        totals[rows, :] = after
        norms[rows, :] = (units(after)[0] * gain_ref[...]).astype(low)
        back[rows, :] = jnp.zeros_like(after)

    @pl.when(jnp.logical_and(step >= blocks, step < last))
    def _():
        def work(rows):
            up = jnp.dot(norms[rows, :], w1_ref[...], preferred_element_type=jnp.float32)
            value, slope = gelu_both(up)
            value = value.astype(low)
            act[rows, :] = value
            totals[rows, :] += jnp.dot(value, w2_ref[...], preferred_element_type=jnp.float32)
            grad = (slope * dot32(grad_ref[rows, :], w2_ref[...], LANES)).astype(low)
            hidden[rows, :] = grad
            back[rows, :] += dot32(grad, w1_ref[...], LANES)

        by_rows(tokens, work)
        term2 = dot32(act[...], grad_ref[...], ROWS).astype(low)
        term1 = dot32(hidden[...], norms[...], ROWS)
        many = CUTS // groups
        rows = term1.shape[0] // many
        term1 = term1.reshape(many, rows, width).astype(low)
        first = (step - blocks) % half * many

        @pl.when(step < blocks + half)
        def _():
            send2_ref[...] = term2
            send1_ref[pl.ds(first, many), :rows, :] = term1

        @pl.when(step >= blocks + half)
        def _():
            keep2_ref[...] = term2
            keep1_ref[pl.ds(first, many), :rows, :] = term1

    @pl.when(step == last)
    def _():
        write.start()
        sum_ref[...] = jnp.zeros_like(sum_ref)

    @pl.when(jnp.logical_and(step >= last, step < last + blocks))
    def _():
        rows = pl.ds(pl.multiple_of((step - last) * BLOCK, BLOCK), BLOCK)
        unit, inverse = units(afters[rows, :])
        grad_rows = back[rows, :]
        grad = grad_ref[rows, :].astype(jnp.float32) + norm_back(
            grad_rows, unit, inverse, gain_ref[...]
        )
        out_ref[...] = grad
        grad_low = grad.astype(low)
        norms[rows, :] = grad_low
        mixed_out_ref[...] = dot32(grad_low, proj_ref[...], LANES).astype(low)
        sum_ref[0:1, :] += jnp.sum(grad_rows * unit, axis=0, keepdims=True)

    @pl.when(step == last + blocks)
    def _():
        many = CUTS // groups
        term = dot32(norms[...], mixes[...], ROWS)
        term = term.reshape(groups, many, width // CUTS, width).astype(low)
        rows = send1_ref.shape[1] - width // CUTS
        for group in range(groups):
            mine = place[0] % 2 == group % 2
            spot = slice(group // 2 * many, (group // 2 + 1) * many)

            @pl.when(mine)
            def _():
                keep1_ref[spot, rows:, :] = term[group]

            @pl.when(jnp.logical_not(mine))
            def _():
                send1_ref[spot, rows:, :] = term[group]

        write.wait()


def mlp_pass(place, start, mixed, out_grad, proj, gain, fc1, fc2, groups):
    tokens, width = start.shape
    wide = fc1.shape[1]
    size = wide // groups
    half = groups // 2
    blocks = tokens // BLOCK

    def once(shape):
        return pl.BlockSpec(shape, lambda *_: (0,) * len(shape), pipeline_mode=pl.Buffered(1))

    def chunk(i, s):
        return turn(jnp.clip(i - blocks, 0, groups - 1), groups, s)

    def part(first):
        return pl.BlockSpec(
            (size, width), lambda i, s: (jnp.clip(i - blocks - first, 0, half - 1), 0)
        )

    def rows_from(first):
        return pl.BlockSpec((BLOCK, width), lambda i, s: (jnp.clip(i - first, 0, blocks - 1), 0))

    halves = shape_of(wide // 2, width, dtype=low)
    joint = (CUTS // 2, (wide + width) // CUTS, width)
    full_low, full = (pltpu.VMEM((tokens, width), kind) for kind in (low, jnp.float32))
    return call(
        functools.partial(mlp_kernel, blocks, groups),
        "mlp_pass",
        (2 * blocks + groups + 1,),
        [rows_from(0), rows_from(0), once((tokens, width)), once(proj.shape), once((1, width))]
        + [
            pl.BlockSpec((width, size), lambda i, s: (0, chunk(i, s))),
            pl.BlockSpec((size, width), lambda i, s: (chunk(i, s), 0)),
        ],
        [pl.BlockSpec(memory_space=pl.ANY)]
        + [rows_from(blocks + groups), rows_from(blocks + groups), once((8, width))]
        + [part(0), part(half), once(joint), once(joint)],
        [
            shape_of(tokens, width),
            shape_of(tokens, width),
            shape_of(tokens, width, dtype=low),
            shape_of(8, width),
        ]
        + [halves, halves] + [shape_of(*joint, dtype=low)] * 2,
        2 * tokens * width * (3 * width + 6 * wide),
        20 * tokens * width + 8 * fc1.size,
        [full, full, full_low, full_low]
        + [pltpu.VMEM((tokens, size), low)] * 2
        + [full, pltpu.SemaphoreType.DMA],
        vmem=VM,
    )(place, start, mixed, out_grad, proj, gain.reshape(1, width), fc1, fc2)


def start_kernel(blocks, groups, place, *refs):
    back_refs, left_refs, refs = refs[:PARTS], refs[PARTS : 2 * PARTS], refs[2 * PARTS :]
    weight_ref, start_ref, gain_ref, grad_ref, normed_ref = refs[:5]
    out_ref, sum_ref, keep_ref, send_ref = refs[5:]
    step = pl.program_id(0)
    width = start_ref.shape[1]

    @pl.when(step == 0)
    def _():
        sum_ref[...] = jnp.zeros_like(sum_ref)

    @pl.when(step < blocks)
    def _():
        back = 0.0
        for i, back_ref in enumerate(back_refs):
            some = back_ref.shape[2]
            for j in range(3):
                first = j * width + i * some
                back = back + dot32(back_ref[j], weight_ref[:, first : first + some], LANES)
        unit, inverse = units(start_ref[...])
        grad = grad_ref[...] + norm_back(back, unit, inverse, gain_ref[...])
        out_ref[...] = grad.astype(low)
        sum_ref[0:1, :] += jnp.sum(back * unit, axis=0, keepdims=True)
        sum_ref[1:2, :] += jnp.sum(grad, axis=0, keepdims=True)

    @pl.when(step >= blocks)
    def _():
        left = jnp.concatenate([ref[0] for ref in left_refs], axis=1)
        term = dot32(left, normed_ref[...], ROWS).astype(low)
        each = 3 * width // groups // UNIT
        for u in range(width // UNIT):
            unit = (step - blocks) * (width // UNIT) + u
            group = unit // each
            first = pl.multiple_of(((group // 2) * each + unit % each) * UNIT, UNIT)
            mine = group % 2 == place[0] % 2
            part = term[u * UNIT : (u + 1) * UNIT]

            @pl.when(mine)
            def _():
                keep_ref[pl.ds(first, UNIT), :] = part

            @pl.when(jnp.logical_not(mine))
            def _():
                send_ref[pl.ds(first, UNIT), :] = part


def start_pass(place, backs, weight, start, gain, grad_after, normed, groups, behind):
    tokens, width = start.shape
    blocks = tokens // BLOCK

    def row_block(i):
        return jnp.minimum(i, blocks - 1)

    block = pl.BlockSpec((BLOCK, width), lambda i, s: (row_block(i), 0))
    half = (3 * width // 2, width)
    return call(
        functools.partial(start_kernel, blocks, groups),
        "start_pass",
        (blocks + 3,),
        [pl.BlockSpec((3, BLOCK, width // PARTS), lambda i, s: (0, row_block(i), 0))] * PARTS
        + [
            pl.BlockSpec(
                (1, tokens, width // PARTS), lambda i, s: (jnp.maximum(i - blocks, 0), 0, 0)
            )
        ]
        * PARTS
        + [whole(weight.shape), block, whole((1, width)), block, whole(normed.shape)],
        [block, whole((8, width)), whole(half), whole(half)],
        [
            shape_of(tokens, width, dtype=low),
            shape_of(8, width),
            shape_of(*half, dtype=low),
            shape_of(*half, dtype=low),
        ],
        12 * tokens * width * width,
        24 * tokens * width + 2 * weight.size,
        behind=behind,
    )(place, *backs, *backs, weight, start, gain.reshape(1, width), grad_after, normed)


def patch_kernel(count, slots, place, *refs):
    pieces, refs = refs[:count], refs[count:]
    grad_ref, kernel_ref, w2_ref, sum1_ref, sum2_ref, ids_ref, mask_ref = refs[:7]
    keep_ref, send_ref, small_ref, pixel_ref, lines, both, hidden, small = refs[7:]
    step = pl.program_id(0)
    width = grad_ref.shape[1]
    codes = hidden.shape[1]

    @pl.when(step == 0)
    def _():
        patch_terms(place, slots, grad_ref, pieces, keep_ref, send_ref, both, lines)
        hidden[...] = jnp.zeros_like(hidden)

    @pl.when(step > 0)
    def _():
        pixel_ref[0] = dot32(kernel_ref[...], grad_ref[...], LANES).astype(low)
        total = hidden[...]
        for p in range(both.shape[1] // slots):
            total = total + dot32(
                both[step - 1, p * slots : (p + 1) * slots, :],
                w2_ref[:, p * width : (p + 1) * width],
                LANES,
            )
        hidden[...] = total

    @pl.when(step == count)
    def _():
        first = jnp.where(place[0] == 0, 1.0, 0.0)
        rows = small.shape[0]
        small[...] = jnp.zeros_like(small)
        small[:slots, :codes] = hidden[...] * mask_ref[...]
        small[:slots, codes : 2 * codes] = jnp.broadcast_to(ids_ref[...] * first, (slots, codes))
        small[slots : slots + 2, :] = sum1_ref[0:2, :]
        small[slots + 2 : slots + 3, :] = sum2_ref[0:1, :]
        small[slots + 3 : slots + 4, :] = jnp.full((1, width), place[1].astype(jnp.float32) * first)
        small_low = small[...].astype(low)
        small_ref[...] = small_low
        send_ref[send_ref.shape[0] - rows :, :] = small_low


def patch_terms(place, slots, grads, pieces, keep_ref, send_ref, all_ref, lines):
    count = len(pieces)
    rows = pieces[0].shape[0]
    per = slots // count
    pixels = rows // per
    width = grads.shape[1]
    for m, piece in enumerate(pieces):
        term = jnp.dot(piece[...], grads[...], preferred_element_type=jnp.float32)
        for s in range(per):
            slot = (place[0] ^ m) * per + s
            for c in range(0, width, 128):
                lines[c // 128, pl.ds(slot, pixels, stride=slots), :] = term[
                    s * pixels : (s + 1) * pixels, c : c + 128
                ]
    span = pixels * slots // count
    for j in range(count):
        mine = (place[0] & 1) == j % 2
        for c in range(0, width, 128):
            part = lines[c // 128, j * span : (j + 1) * span, :].astype(low)
            all_ref[j, :, c : c + 128] = part

        @pl.when(mine)
        def _():
            keep_ref[j // 2] = all_ref[j]

        @pl.when(jnp.logical_not(mine))
        def _():
            send_ref[j // 2 * span : (j // 2 + 1) * span, :] = all_ref[j]


def patch_pass(place, pieces, grad_embed, kernel, gen_w2, sum1, sum2, ids_column, mask_column, behind):
    rows, tokens = pieces[0].shape
    count = len(pieces)
    width = grad_embed.shape[1]
    codes = gen_w2.shape[0]
    slots = ids_column.shape[0]
    span = gen_w2.shape[1] // count
    more = -(-(slots + 4) // 16) * 16

    def turned(i):
        return jnp.maximum(i - 1, 0)

    kept = (count // 2, rows, width)
    sent = (count // 2 * rows + more, width)
    return call(
        functools.partial(patch_kernel, count, slots),
        "patch_pass",
        (1 + count,),
        [whole(pieces[0].shape)] * count
        + [
            whole(grad_embed.shape),
            pl.BlockSpec((rows, width), lambda i, s: (s[0] ^ turned(i), 0)),
            pl.BlockSpec((codes, span), lambda i, s: (0, turned(i))),
            whole((8, width)),
            whole((8, width)),
            whole((slots, 1)),
            whole((slots, 1)),
        ],
        [
            whole(kept),
            whole(sent),
            whole((more, width)),
            pl.BlockSpec((1, rows, tokens), lambda i, s: (turned(i), 0, 0)),
        ],
        [
            shape_of(*kept, dtype=low),
            shape_of(*sent, dtype=low),
            shape_of(more, width, dtype=low),
            shape_of(count, rows, tokens, dtype=low),
        ],
        4 * tokens * width * rows * count,
        2 * (tokens * width + gen_w2.size) + 6 * rows * count * (width + tokens),
        [
            pltpu.VMEM((width // 128, rows * count, 128), jnp.float32),
            pltpu.VMEM((count, rows, width), low),
            pltpu.VMEM((slots, codes), jnp.float32),
            pltpu.VMEM((more, width), jnp.float32),
        ],
        behind=behind,
    )(
        place,
        *pieces,
        grad_embed,
        kernel,
        gen_w2,
        sum1,
        sum2,
        ids_column,
        mask_column,
    )


def join_kernel(place, *refs):
    out_ref = refs[-1]
    for m, piece in enumerate(refs[:-1]):

        @pl.when(pl.program_id(0) == m)
        def _():
            out_ref[...] = piece[...].astype(jnp.float32)


def join_pixels(place, pieces, behind):
    rows, tokens = pieces[0].shape
    count = len(pieces)
    return call(
        join_kernel,
        "join_pixels",
        (count,),
        [whole(pieces[0].shape)] * count,
        pl.BlockSpec((rows, tokens), lambda i, s: (0, s[0] ^ i)),
        shape_of(rows, count * tokens),
        0,
        6 * rows * count * tokens,
        behind=behind,
    )(place, *pieces)


def finish_kernel(slots, sensors, place, small_ref, rows_ref, table_ref, w1_ref, wave_ref, gen1_ref, gen2_ref, sensor_ref, norm_ref):
    groups = small_ref.shape[0]
    bands, codes = wave_ref.shape
    table, weight = table_ref[...], w1_ref[...]
    width = norm_ref.shape[1]

    def picked(q):
        return small_ref[q, :slots, codes : codes + bands].astype(jnp.float32).astype(jnp.int32)

    ids = [picked(q) for q in range(groups)]
    hidden = code_rows(jnp.concatenate(ids, axis=0), table, weight)[2].astype(low)
    for i in range(rows_ref.shape[0]):
        wide = rows_ref.shape[2]
        gen2_ref[:, i * wide : (i + 1) * wide] = dot32(hidden, rows_ref[i], ROWS)

    in_order = [place[2] ^ g for g in range(groups)]
    ids = [picked(q) for q in in_order]
    select, rows, _, slope = code_rows(jnp.concatenate(ids, axis=0), table, weight)
    grad = jnp.concatenate(
        [small_ref[q, :slots, :codes].astype(jnp.float32) for q in in_order], axis=0
    )
    scaled = slope * grad
    gen1_ref[...] = lax.dot_general(
        rows, scaled, ROWS, precision=highest, preferred_element_type=jnp.float32
    )
    row_grad = grad + lax.dot_general(
        scaled,
        weight.astype(jnp.float32),
        LANES,
        precision=highest,
        preferred_element_type=jnp.float32,
    )
    wave_ref[...] = lax.dot_general(
        select, row_grad, ROWS, precision=highest, preferred_element_type=jnp.float32
    )
    norms = [jnp.zeros((1, width), jnp.float32)] * 2
    each = [jnp.zeros((1, width), jnp.float32)] * sensors
    for q in in_order:
        lines = small_ref[q, slots : slots + 8, :].astype(jnp.float32)
        norms = [norms[0] + lines[0:1], norms[1] + lines[2:3]]
        for s in range(sensors):
            each[s] = each[s] + jnp.where(lines[3:4] == float(s), lines[1:2], 0.0)
    for n in range(2):
        norm_ref[n : n + 1, :] = norms[n]
    for s in range(sensors):
        sensor_ref[s : s + 1, :] = each[s]


def finish(place, small, rows, wave_table, gen_w1, slots, sensors, width):
    codes = wave_table.shape[1]
    shapes = [
        wave_table.shape,
        gen_w1.shape,
        (codes, rows.shape[0] * rows.shape[2]),
        (sensors, width),
        (2, width),
    ]
    return call(
        functools.partial(finish_kernel, slots, sensors),
        "finish",
        (1,),
        [whole(small.shape), whole(rows.shape), whole(wave_table.shape), whole(gen_w1.shape)],
        [whole(shape) for shape in shapes],
        [shape_of(*shape) for shape in shapes],
        2 * rows.size * codes,
        4 * rows.size,
    )(place, small, rows, wave_table, gen_w1)


def swap(piece, axis, mask):
    count = lax.axis_size(axis)
    return lax.ppermute(piece, axis, [(i, i ^ mask) for i in range(count)])


def bits_of(axis):
    return lax.axis_size(axis).bit_length() - 1


class Scatter:
    def __init__(self, keep, send, bits):
        self.bits = bits
        self.dims = [("band", bit) for bit in reversed(range(1, bits_of("band")))] + [
            ("dp", bit) for bit in reversed(range(bits_of("dp")))
        ]
        rows = keep.shape[0] >> len(self.dims)
        shape = (2,) * len(self.dims) + (rows, keep.shape[1])
        got = swap(send, "band", 1)
        self.last = got
        self.parts = [keep.reshape(shape), got.reshape(shape)]

    def columns(self, first, last):
        some = object.__new__(Scatter)
        some.bits = self.bits
        some.dims = list(self.dims)
        some.last = self.last
        some.parts = [part[..., first:last] for part in self.parts]
        return some

    def result(self):
        return sum(part.astype(jnp.float32) for part in self.parts)


def pick(rows, index, dim):
    return lax.dynamic_index_in_dim(rows, index, dim, False, allow_negative_indices=False)


def halve(sums, axis, bit, when=()):
    (mine, other), _ = lax.optimization_barrier((sums[0].bits[axis, bit], when))
    sends = []
    for one in sums:
        dim = one.dims.index((axis, bit))
        one.dims.pop(dim)
        send = sum(
            pick(part, other, dim).astype(jnp.float32)
            for part in one.parts
        )
        sends.append(send.astype(low))
        one.parts = [pick(part, mine, dim) for part in one.parts]
    send = sends[0] if len(sends) == 1 else jnp.concatenate(sends, axis=-2)
    got = swap(send, axis, 1 << bit)
    first = 0
    for one, each in zip(sums, sends):
        rows = each.shape[-2]
        one.parts.append(lax.slice_in_dim(got, first, first + rows, axis=got.ndim - 2))
        one.last = got
        first += rows
    return send


def rounded(rows):
    return lax.reduce_precision(rows, 8, 7).astype(low)


def shards(
    pixels,
    band_ids,
    band_mask,
    sensor_tags,
    segment_ids,
    wave_table,
    gen_w1,
    gen_w2,
    sensor_table,
    ln1_gain,
    qkv_weight,
    proj_weight,
    ln2_gain,
    fc1_weight,
    fc2_weight,
    out_grad,
):
    band_place = lax.axis_index("band")
    dp_place = lax.axis_index("dp")
    band_count = lax.axis_size("band")
    dp_count = lax.axis_size("dp")
    slots_dev = pixels.shape[0]
    slots = band_ids.shape[1]
    tok_dev, model_width = out_grad.shape
    patch_pixels = pixels.shape[2]
    sensors = sensor_table.shape[0]
    part_rows = slots_dev * patch_pixels
    place = jnp.stack([band_place, sensor_tags[0], dp_place]).astype(jnp.int32)

    own_pixels = pixels.transpose(0, 2, 1).reshape(part_rows, -1)
    pieces = []
    for mask in range(band_count):
        piece = lax.dynamic_slice_in_dim(own_pixels, (band_place ^ mask) * tok_dev, tok_dev, 1)
        pieces.append(swap(piece, "band", mask) if mask else piece)

    kernel = generate_kernels(band_ids, band_mask, wave_table, gen_w1, gen_w2, model_width)
    kernel = kernel.reshape(slots * patch_pixels, model_width)
    start_rows, normed1, projected = embed(
        place, kernel, sensor_table, ln1_gain, qkv_weight, pieces
    )
    window = windows(segment_ids)
    query_side, key_side = features(segment_ids)
    bits = {
        (axis, bit): ((at >> bit) & 1, 1 - ((at >> bit) & 1))
        for axis, at in (("band", band_place), ("dp", dp_place))
        for bit in range(bits_of(axis))
    }
    turned_places = [dp_place ^ i for i in range(dp_count)]
    ids_column = band_ids.reshape(slots, 1).astype(jnp.float32)
    mask_column = band_mask.reshape(slots, 1).astype(jnp.float32)
    projected, window, query_side, key_side, bits, turned_places, ids_column, mask_column = (
        lax.optimization_barrier(
            (
                projected,
                window,
                query_side,
                key_side,
                bits,
                turned_places,
                ids_column,
                mask_column,
            )
        )
    )
    attended, totals = attend_forward(projected, segment_ids, window, query_side, key_side)
    encoded, grad_after, grad_attended, norm2_sums, send2, keep2, send1, keep1 = mlp_pass(
        place,
        start_rows,
        attended,
        out_grad,
        proj_weight,
        ln2_gain,
        fc1_weight,
        fc2_weight,
        band_count,
    )
    band_rest = [("band", bit) for bit in range(1, bits_of("band"))]
    dp_rest = [("dp", bit) for bit in range(bits_of("dp"))]
    devices = band_count * dp_count
    fc1_rows = fc1_weight.shape[1] // devices
    if devices != CUTS:
        first = fc1_weight.shape[1] // CUTS
        send1, keep1 = [
            jnp.concatenate(
                [
                    part.reshape(devices // 2, -1, model_width)
                    for part in (joint[:, :first], joint[:, first:])
                ],
                axis=1,
            )
            for joint in (send1, keep1)
        ]
    fc2_sum = Scatter(keep2, send2, bits)
    fc1_sum = Scatter(*[part.reshape(-1, model_width) for part in (keep1, send1)], bits)
    backs = []

    def back_part(behind):
        backs.append(
            attend_back(
                projected,
                segment_ids,
                window,
                query_side,
                key_side,
                grad_attended,
                attended,
                totals,
                len(backs),
                behind,
            )
        )

    back_part([])
    sent = [
        halve([fc2_sum], *band_rest[0], backs[-1]),
        halve([fc1_sum], *dp_rest[0], backs[-1]),
    ]
    for item in band_rest[1:]:
        sent.append(halve([fc2_sum], *item))
    back_part(sent)
    back_part([backs[-1]])
    sent = [halve([fc2_sum], *dp_rest[0], backs[-1])]
    for item in band_rest:
        sent.append(halve([fc1_sum], *item, backs[-1]))
    grad_embed, norm1_sums, keep, send = start_pass(
        place,
        backs,
        qkv_weight,
        start_rows,
        ln1_gain,
        grad_after,
        normed1,
        band_count,
        sent,
    )
    half = model_width // 2
    qkv_sum = Scatter(keep, send, bits)

    keep, send, small, pixel_parts = patch_pass(
        place,
        pieces,
        grad_embed,
        kernel,
        gen_w2,
        norm1_sums,
        norm2_sums,
        ids_column,
        mask_column,
        [],
    )
    qkv_halves = [qkv_sum.columns(0, half), qkv_sum.columns(half, model_width)]
    for item in dp_rest[1:3]:
        halve([fc2_sum], *item, small)
        halve([fc1_sum], *item, small)
    halve(qkv_halves[:1], *dp_rest[0], small)
    halve(qkv_halves[1:], *band_rest[0], small)
    for item in band_rest[1:]:
        halve(qkv_halves[1:], *item)
    more = small.shape[0]
    got = swap(send, "band", 1)
    patch_parts = [keep, got[:-more].reshape(keep.shape)]
    small = small.astype(jnp.float32) + got[-more:].astype(jnp.float32)
    for bit in range(1, bits_of("band")):
        mine, other = bits["band", bit]
        patch_parts = [
            part.reshape((part.shape[0] // 2, 2) + part.shape[1:]) for part in patch_parts
        ]
        away = sum(
            pick(part, other, 1).astype(jnp.float32)
            for part in patch_parts
        ).astype(low)
        patch_parts = [pick(part, mine, 1) for part in patch_parts]
        small_low = rounded(small)
        got = swap(
            jnp.concatenate([away.reshape(-1, model_width), small_low]), "band", 1 << bit
        )
        patch_parts.append(got[:-more].reshape(away.shape))
        small = small_low.astype(jnp.float32) + got[-more:].astype(jnp.float32)
    pixel_pieces = [
        swap(lax.optimization_barrier((pixel_parts[mask], small))[0], "band", mask)
        if mask
        else pixel_parts[0]
        for mask in range(band_count)
    ]
    span = patch_pixels // band_count
    patch_sum = sum(part.astype(jnp.float32) for part in patch_parts).reshape(
        span, slots, model_width
    )
    patch_low = (patch_sum * mask_column[None]).astype(low)
    cuts = max(1, dp_count // span)
    share = model_width // cuts
    if cuts > 1:
        patch_low = patch_low.reshape(span, slots, cuts, share).transpose(0, 2, 1, 3)
    patch_low = patch_low.reshape(dp_count, -1, slots, share)
    held = jnp.stack(
        [pick(patch_low, turned, 0) for turned in turned_places]
    )
    all_small = rounded(small)[None]

    shape = held.shape
    for n, (axis, bit) in enumerate(dp_rest):
        view = held.reshape((dp_count >> (bit + 1), 2, 1 << bit) + shape[1:])
        away = view[:, 1]
        rows = away.size // model_width
        got = swap(
            jnp.concatenate(
                [away.reshape(rows, model_width), all_small.reshape(-1, model_width)]
            ),
            axis,
            1 << bit,
        )
        if n == 0:
            halve(qkv_halves[1:], *dp_rest[0], all_small)
            for item in band_rest:
                halve(qkv_halves[:1], *item, all_small)
        else:
            halve(qkv_halves, axis, bit)
        if n > 2:
            halve([fc2_sum], axis, bit)
            halve([fc1_sum], axis, bit)
        held = jnp.stack([view[:, 0], got[:rows].reshape(away.shape)], axis=1).reshape(shape)
        all_small = jnp.concatenate([all_small, got[rows:].reshape(all_small.shape)])
    kernel_rows = held.transpose(1, 0, 2, 3).reshape(shape[1], dp_count * slots, share)
    wave_table_grad, gen_w1_grad, gen_w2_grad, sensor_grad, norm_grads = finish(
        place, all_small, kernel_rows, wave_table, gen_w1, slots, sensors, model_width
    )
    grad_pixels = join_pixels(place, pixel_pieces, [])
    grad_pixels = grad_pixels.reshape(slots_dev, patch_pixels, -1).transpose(0, 2, 1)
    qkv_grad = jnp.concatenate([part.result() for part in qkv_halves], axis=1)
    fc2_grad, joint = fc2_sum.result(), fc1_sum.result()
    fc1_grad, proj_grad = joint[:fc1_rows], joint[fc1_rows:]
    return (
        encoded,
        grad_pixels,
        wave_table_grad,
        gen_w1_grad,
        gen_w2_grad,
        sensor_grad,
        norm_grads[0],
        qkv_grad.T,
        proj_grad.T,
        norm_grads[1],
        fc1_grad.T,
        fc2_grad,
    )


def solution(mesh):
    return jax.shard_map(
        shards,
        mesh=mesh,
        in_specs=(
            P("band", "dp", None),
            P("dp", None),
            P("dp", None),
            P("dp"),
            P(("dp", "band"), None),
            P(),
            P(),
            P(),
            P(),
            P(),
            P(),
            P(),
            P(),
            P(),
            P(),
            P(("dp", "band"), None),
        ),
        out_specs=(
            P(("dp", "band"), None),
            P("band", "dp", None),
            P(),
            P(),
            P(None, ("band", "dp")),
            P(),
            P(),
            P(None, ("band", "dp")),
            P(None, ("band", "dp")),
            P(),
            P(None, ("band", "dp")),
            P(("band", "dp"), None),
        ),
        check_vma=False,
    )
```

```python
import functools

import jax
import jax.numpy as jnp
from jax import lax
from jax.experimental import pallas as pl
from jax.experimental.pallas import tpu as pltpu
from jax.sharding import PartitionSpec as P

highest = lax.Precision.HIGHEST
UNIT = 96
PARTS = 3
PAIRS = 3
BACK_PAIRS = 2
VA = 58
CUTS = 32
VM = 56
low = jnp.bfloat16
MIB = 1 << 20

BLOCK = 256
STEP = 256
FAR = 2.0**30
LANES = (((1,), (1,)), ((), ()))
ROWS = (((0,), (0,)), ((), ()))


def dot32(left, right, dims):
    return lax.dot_general(left, right, dims, preferred_element_type=jnp.float32)


def windows(segment_ids):
    length = segment_ids.shape[1]
    first = segment_ids[:, ::BLOCK]
    last = segment_ids[:, BLOCK - 1 :: BLOCK]
    begin = jnp.sum(segment_ids[:, None, :] < first[:, :, None], axis=-1)
    end = jnp.sum(segment_ids[:, None, :] <= last[:, :, None], axis=-1)
    low = begin // STEP
    count = (end + STEP - 1) // STEP - low
    return jnp.stack([low, count - 1], axis=-1).astype(jnp.int32).reshape(-1)


def features(segment_ids):
    lane = jnp.arange(128, dtype=jnp.int32)
    code = segment_ids.reshape(-1, 1)
    same = (code == (lane % 64)[None, :])
    used = (lane % 64 < 4)[None, :]
    query_side = jnp.where(same & used, 1.0, 0.0)
    key_side = jnp.where(used & ~same, -FAR, 0.0)
    return query_side.astype(jnp.bfloat16), key_side.astype(jnp.bfloat16)


def head_masks():
    lane = lax.broadcasted_iota(jnp.int32, (1, 128), 1)
    low = jnp.where(lane < 64, 1.0, 0.0)
    return low.astype(jnp.bfloat16), (1.0 - low).astype(jnp.bfloat16)


def forward_kernel(win, q_ref, k_ref, v_ref, qf_ref, kf_ref, o_ref, lse_ref, qa, ka, va):
    length = q_ref.shape[0]
    blocks = length // BLOCK
    base = pl.program_id(0) * blocks * 2
    masks = head_masks()
    pairs = q_ref.shape[1] // 128
    heads = 2 * pairs
    for n in range(heads):
        mask, cols = masks[n % 2], slice(n // 2 * 128, (n // 2 + 1) * 128)
        other = jnp.bfloat16(1.0) - mask
        qa[n] = q_ref[:, cols] * (mask * jnp.bfloat16(0.125)) + qf_ref[...] * other
        ka[n] = k_ref[:, cols] * mask + kf_ref[...] * other
        va[n] = v_ref[:, cols] * mask + other

    def one_block(block, carry):
        rows = pl.ds(pl.multiple_of(block * BLOCK, BLOCK), BLOCK)
        low = pl.multiple_of(win[base + 2 * block] * STEP, STEP)

        def run(width):
            keys = pl.ds(low, width)
            mixes, peaks = [], []
            for n in range(heads):
                scores = dot32(qa[n, rows, :], ka[n, keys, :], LANES)
                peak = jnp.max(scores, axis=1, keepdims=True)
                probs = jnp.exp(scores - peak).astype(jnp.bfloat16)
                mixes.append(jnp.dot(probs, va[n, keys, :], preferred_element_type=jnp.float32))
                peaks.append(peak)
            low_lanes = lax.broadcasted_iota(jnp.int32, (1, 128), 1) < 64
            for n in range(0, heads, 2):
                mixed = jnp.where(low_lanes, mixes[n], mixes[n + 1])
                total = pltpu.roll(jnp.where(low_lanes, mixes[n + 1], mixes[n]), 64, 1)
                o_ref[rows, n * 64 : n * 64 + 128] = (mixed / total).astype(jnp.bfloat16)
                both = (jnp.where(low_lanes, peaks[n], peaks[n + 1]) + jnp.log(total)).T
                lse_ref[0, n // 2, 0:1, rows] = both[0:1]
                lse_ref[0, n // 2, 1:2, rows] = both[64:65]

        count = win[base + 2 * block + 1]
        for size in range(length // STEP):
            pl.when(count == size)(functools.partial(run, (size + 1) * STEP))
        return carry

    lax.fori_loop(0, blocks, one_block, 0)


def back_kernel(
    win,
    q_ref,
    k_ref,
    v_ref,
    qf_ref,
    kf_ref,
    g_ref,
    o_ref,
    lse_ref,
    out_ref,
    qa,
    ka,
    qh,
    kh,
    vh,
    gh,
    delta,
    dk,
    dv,
):
    length = q_ref.shape[0]
    blocks = length // BLOCK
    base = pl.program_id(0) * blocks * 2
    masks = head_masks()
    pairs = q_ref.shape[1] // 128
    heads = 2 * pairs
    for n in range(heads):
        mask, cols = masks[n % 2], slice(n // 2 * 128, (n // 2 + 1) * 128)
        other = jnp.bfloat16(1.0) - mask
        scaled = q_ref[:, cols] * (mask * jnp.bfloat16(0.125))
        qh[n] = scaled
        qa[n] = scaled + qf_ref[...] * other
        own = k_ref[:, cols] * mask
        kh[n] = own
        ka[n] = own + kf_ref[...] * other
        vh[n] = v_ref[:, cols] * mask
        gh[n] = g_ref[:, cols] * mask
    product = g_ref[...].astype(jnp.float32) * o_ref[...].astype(jnp.float32)
    turned = product.T
    for n in range(heads):
        delta[n : n + 1, :] = jnp.sum(turned[n * 64 : (n + 1) * 64], axis=0, keepdims=True)
    dk[...] = jnp.zeros_like(dk)
    dv[...] = jnp.zeros_like(dv)

    def one_block(block, carry):
        rows = pl.ds(pl.multiple_of(block * BLOCK, BLOCK), BLOCK)
        low = pl.multiple_of(win[base + 2 * block] * STEP, STEP)

        def run(width):
            keys = pl.ds(low, width)
            for p in range(pairs):
                turned_grad = None
                cols = slice(p * 128, (p + 1) * 128)
                for n in (2 * p, 2 * p + 1):
                    scores = dot32(ka[n, keys, :], qa[n, rows, :], LANES)
                    probs = jnp.exp(scores - lse_ref[0, p, n % 2 : n % 2 + 1, rows])
                    grad_probs = dot32(vh[n, keys, :], gh[n, rows, :], LANES)
                    grad_scores = (probs * (grad_probs - delta[n : n + 1, rows])).astype(
                        jnp.bfloat16
                    )
                    dv[keys, cols] += jnp.dot(
                        probs.astype(jnp.bfloat16),
                        gh[n, rows, :],
                        preferred_element_type=jnp.float32,
                    )
                    dk[keys, cols] += jnp.dot(
                        grad_scores, qh[n, rows, :], preferred_element_type=jnp.float32
                    )
                    term = dot32(grad_scores, kh[n, keys, :], ROWS)
                    turned_grad = term if turned_grad is None else turned_grad + term
                out_ref[0, rows, cols] = (turned_grad * 0.125).astype(jnp.bfloat16)

        count = win[base + 2 * block + 1]
        for size in range(length // STEP):
            pl.when(count == size)(functools.partial(run, (size + 1) * STEP))
        return carry

    lax.fori_loop(0, blocks, one_block, 0)
    out_ref[1] = dk[...].astype(jnp.bfloat16)
    out_ref[2] = dv[...].astype(jnp.bfloat16)


def attend_forward(projected, segment_ids, win, query_side, key_side):
    seqs, length = segment_ids.shape
    width = projected.shape[1] // 3
    wide = 128 * PAIRS
    steps = width // wide

    def columns(offset):
        return pl.BlockSpec((length, wide), lambda s, p, w: (s, p + offset))

    fixed = pl.BlockSpec((length, 128), lambda s, p, w: (s, 0))
    return call(
        forward_kernel,
        "attend_forward",
        (seqs, steps),
        [columns(0), columns(steps), columns(2 * steps), fixed, fixed],
        [columns(0), pl.BlockSpec((1, PAIRS, 8, length), lambda s, p, w: (s, p, 0, 0))],
        [
            shape_of(seqs * length, width, dtype=low),
            shape_of(seqs, width // 128, 8, length),
        ],
        4 * seqs * length * length * width,
        8 * seqs * length * width,
        [pltpu.VMEM((2 * PAIRS, length, 128), low)] * 3,
        vmem=VA,
    )(win, projected, projected, projected, query_side, key_side)


def attend_back(projected, segment_ids, win, query_side, key_side, grad, mixed, lse, part, behind):
    seqs, length = segment_ids.shape
    width = projected.shape[1] // 3
    wide = 128 * BACK_PAIRS
    steps = width // wide
    run = steps // PARTS
    begin = part * run

    def columns(offset):
        return pl.BlockSpec((length, wide), lambda s, p, w: (s, p + offset + begin))

    fixed = pl.BlockSpec((length, 128), lambda s, p, w: (s, 0))
    pair_low = pltpu.VMEM((2 * BACK_PAIRS, length, 128), low)
    return call(
        back_kernel,
        "attend_back",
        (seqs, run),
        [
            columns(0),
            columns(steps),
            columns(2 * steps),
            fixed,
            fixed,
            columns(0),
            columns(0),
            pl.BlockSpec((1, BACK_PAIRS, 8, length), lambda s, p, w: (s, p + begin, 0, 0)),
        ],
        pl.BlockSpec((3, length, wide), lambda s, p, w: (0, s, p)),
        shape_of(3, seqs * length, run * wide, dtype=low),
        10 * seqs * length * length * run * wide,
        14 * seqs * length * run * wide,
        [pair_low] * 6
        + [
            pltpu.VMEM((8, length), jnp.float32),
            pltpu.VMEM((length, wide), jnp.float32),
            pltpu.VMEM((length, wide), jnp.float32),
        ],
        vmem=VA,
        behind=behind,
    )(win, projected, projected, projected, query_side, key_side, grad, mixed, lse)


def whole(shape):
    return pl.BlockSpec(shape, lambda *_: (0,) * len(shape))


def call(
    kernel,
    name,
    grid,
    in_specs,
    out_specs,
    out_shape,
    flops,
    moved,
    scratch=(),
    prefetch=1,
    vmem=40,
    behind=(),
):
    first = prefetch + len(in_specs)

    def body(*refs):
        kernel(*refs[:first], *refs[first + len(behind) :])

    run = pl.pallas_call(
        body,
        grid_spec=pltpu.PrefetchScalarGridSpec(
            num_scalar_prefetch=prefetch,
            grid=grid,
            in_specs=list(in_specs) + [pl.BlockSpec(memory_space=pl.ANY)] * len(behind),
            out_specs=out_specs,
            scratch_shapes=list(scratch),
        ),
        out_shape=out_shape,
        compiler_params=pltpu.CompilerParams(vmem_limit_bytes=vmem * MIB),
        cost_estimate=pl.CostEstimate(flops=flops, bytes_accessed=moved, transcendentals=0),
        name=name,
    )
    return lambda *args: run(*args, *behind)


def shape_of(*shape, dtype=jnp.float32):
    return jax.ShapeDtypeStruct(shape, dtype)


def units(rows):
    center = rows - jnp.mean(rows, axis=-1, keepdims=True)
    inverse = lax.rsqrt(jnp.mean(center * center, axis=-1, keepdims=True) + 1e-05)
    return center * inverse, inverse


def norm_back(grad_rows, unit_rows, inverse, gain):
    scaled = grad_rows * gain
    inner = jnp.mean(scaled * unit_rows, axis=-1, keepdims=True)
    return inverse * (scaled - jnp.mean(scaled, axis=-1, keepdims=True) - unit_rows * inner)


def gelu_both(rows):
    root = 0.7978845608028654
    square = rows * rows
    curve = jnp.tanh(rows * (root + (root * 0.044715) * square))
    half = 0.5 + 0.5 * curve
    slope = half + (0.5 * rows) * (1.0 - curve * curve) * (root + (3.0 * root * 0.044715) * square)
    return rows * half, slope


def code_rows(ids, table, weight):
    lane = lax.broadcasted_iota(jnp.int32, (ids.shape[0], table.shape[0]), 1)
    select = jnp.where(ids == lane, 1.0, 0.0)
    rows = jnp.dot(select.astype(low), table, preferred_element_type=jnp.float32)
    raw = jnp.dot(rows.astype(low), weight, preferred_element_type=jnp.float32)
    value, slope = gelu_both(raw)
    return select, rows, rows + value, slope


def generate_kernel(ids_ref, mask_ref, table_ref, w1_ref, w2_ref, out_ref, hidden, lines):
    slots, pixels, width = out_ref.shape

    @pl.when(pl.program_id(0) == 0)
    def _():
        hidden[...] = code_rows(ids_ref[...], table_ref[...], w1_ref[...])[2].astype(low)

    for p in range(pixels):
        made = jnp.dot(
            hidden[...], w2_ref[:, p * width : (p + 1) * width], preferred_element_type=jnp.float32
        )
        for c in range(0, width, 128):
            lines[c // 128, pl.ds(p, slots, stride=pixels), :] = (
                made[:, c : c + 128] * mask_ref[...]
            )
    for c in range(0, width, 128):
        out_ref[:, :, c : c + 128] = lines[c // 128].reshape(slots, pixels, 128).astype(low)


def generate_kernels(band_ids, band_mask, wave_table, gen_w1, gen_w2, width):
    slots = band_ids.shape[1]
    pixels = gen_w2.shape[1] // width
    part = 16
    return call(
        generate_kernel,
        "generate",
        (pixels // part,),
        [
            whole((slots, 1)),
            whole((slots, 1)),
            whole(wave_table.shape),
            whole(gen_w1.shape),
            pl.BlockSpec((gen_w2.shape[0], part * width), lambda i: (0, i)),
        ],
        pl.BlockSpec((slots, part, width), lambda i: (0, i, 0)),
        shape_of(slots, pixels, width, dtype=low),
        2 * 128 * slots * gen_w2.shape[1],
        2 * gen_w2.size,
        [
            pltpu.VMEM((slots, gen_w1.shape[0]), low),
            pltpu.VMEM((width // 128, slots * part, 128), jnp.float32),
        ],
        prefetch=0,
    )(band_ids.reshape(slots, 1), band_mask.reshape(slots, 1).astype(jnp.float32), wave_table, gen_w1, gen_w2)


def embed_kernel(count, place, kernel_ref, table_ref, gain_ref, weight_ref, *refs):
    pieces, (start_ref, normed_ref, out_ref) = refs[:count], refs[count:]
    rows = pieces[0].shape[0]
    sensor = lax.broadcasted_iota(jnp.int32, table_ref.shape, 0) == place[1]
    start = jnp.sum(
        jnp.where(sensor, table_ref[...].astype(jnp.float32), 0.0), axis=0, keepdims=True
    )
    for m, piece in enumerate(pieces):
        first = pl.multiple_of((place[0] ^ m) * rows, rows)
        start = start + dot32(piece[...], kernel_ref[pl.ds(first, rows), :], ROWS)
    start_ref[...] = start
    normed = (units(start)[0] * gain_ref[...]).astype(low)
    normed_ref[...] = normed
    out_ref[...] = jnp.dot(normed, weight_ref[...], preferred_element_type=jnp.float32).astype(low)


def embed(place, kernel, sensor_table, gain, weight, pieces):
    rows, tokens = pieces[0].shape
    width = weight.shape[0]
    return call(
        functools.partial(embed_kernel, len(pieces)),
        "embed",
        (tokens // BLOCK,),
        [whole(kernel.shape), whole(sensor_table.shape), whole((1, width)), whole(weight.shape)]
        + [pl.BlockSpec((rows, BLOCK), lambda i, s: (0, i))] * len(pieces),
        [
            pl.BlockSpec((BLOCK, width), lambda i, s: (i, 0)),
            pl.BlockSpec((BLOCK, width), lambda i, s: (i, 0)),
            pl.BlockSpec((BLOCK, 3 * width), lambda i, s: (i, 0)),
        ],
        [
            shape_of(tokens, width),
            shape_of(tokens, width, dtype=low),
            shape_of(tokens, 3 * width, dtype=low),
        ],
        2 * tokens * width * (kernel.shape[0] + 3 * width),
        14 * tokens * width + 2 * weight.size,
    )(place, kernel, sensor_table, gain.reshape(1, width), weight, *pieces)


def turn(step, groups, place):
    half = groups // 2
    core = place[0] % 2
    return (step % half) * 2 + jnp.where(step < half, 1 - core, core)


def by_rows(tokens, work):
    def one(i, carry):
        work(pl.ds(pl.multiple_of(i * BLOCK, BLOCK), BLOCK))
        return carry

    lax.fori_loop(0, tokens // BLOCK, one, 0, unroll=True)


def mlp_kernel(
    blocks,
    groups,
    place,
    start_ref,
    mixed_ref,
    grad_ref,
    proj_ref,
    gain_ref,
    w1_ref,
    w2_ref,
    encoded_ref,
    out_ref,
    mixed_out_ref,
    sum_ref,
    send2_ref,
    keep2_ref,
    send1_ref,
    keep1_ref,
    afters,
    totals,
    mixes,
    norms,
    act,
    hidden,
    back,
    sem,
):
    step = pl.program_id(0)
    tokens, width = afters.shape
    half = groups // 2
    last = blocks + groups
    write = pltpu.make_async_copy(totals, encoded_ref, sem)

    @pl.when(step < blocks)
    def _():
        rows = pl.ds(pl.multiple_of(step * BLOCK, BLOCK), BLOCK)
        mixed = mixed_ref[...]
        mixes[rows, :] = mixed
        after = start_ref[...] + jnp.dot(mixed, proj_ref[...], preferred_element_type=jnp.float32)
        afters[rows, :] = after
        totals[rows, :] = after
        norms[rows, :] = (units(after)[0] * gain_ref[...]).astype(low)
        back[rows, :] = jnp.zeros_like(after)

    @pl.when(jnp.logical_and(step >= blocks, step < last))
    def _():
        def work(rows):
            up = jnp.dot(norms[rows, :], w1_ref[...], preferred_element_type=jnp.float32)
            value, slope = gelu_both(up)
            value = value.astype(low)
            act[rows, :] = value
            totals[rows, :] += jnp.dot(value, w2_ref[...], preferred_element_type=jnp.float32)
            grad = (slope * dot32(grad_ref[rows, :], w2_ref[...], LANES)).astype(low)
            hidden[rows, :] = grad
            back[rows, :] += dot32(grad, w1_ref[...], LANES)

        by_rows(tokens, work)
        term2 = dot32(act[...], grad_ref[...], ROWS).astype(low)
        term1 = dot32(hidden[...], norms[...], ROWS)
        many = CUTS // groups
        rows = term1.shape[0] // many
        term1 = term1.reshape(many, rows, width).astype(low)
        first = (step - blocks) % half * many

        @pl.when(step < blocks + half)
        def _():
            send2_ref[...] = term2
            send1_ref[pl.ds(first, many), :rows, :] = term1

        @pl.when(step >= blocks + half)
        def _():
            keep2_ref[...] = term2
            keep1_ref[pl.ds(first, many), :rows, :] = term1

    @pl.when(step == last)
    def _():
        write.start()
        sum_ref[...] = jnp.zeros_like(sum_ref)

    @pl.when(jnp.logical_and(step >= last, step < last + blocks))
    def _():
        rows = pl.ds(pl.multiple_of((step - last) * BLOCK, BLOCK), BLOCK)
        unit, inverse = units(afters[rows, :])
        grad_rows = back[rows, :]
        grad = grad_ref[rows, :].astype(jnp.float32) + norm_back(
            grad_rows, unit, inverse, gain_ref[...]
        )
        out_ref[...] = grad
        grad_low = grad.astype(low)
        norms[rows, :] = grad_low
        mixed_out_ref[...] = dot32(grad_low, proj_ref[...], LANES).astype(low)
        sum_ref[0:1, :] += jnp.sum(grad_rows * unit, axis=0, keepdims=True)

    @pl.when(step == last + blocks)
    def _():
        many = CUTS // groups
        term = dot32(norms[...], mixes[...], ROWS)
        term = term.reshape(groups, many, width // CUTS, width).astype(low)
        rows = send1_ref.shape[1] - width // CUTS
        for group in range(groups):
            mine = place[0] % 2 == group % 2
            spot = slice(group // 2 * many, (group // 2 + 1) * many)

            @pl.when(mine)
            def _():
                keep1_ref[spot, rows:, :] = term[group]

            @pl.when(jnp.logical_not(mine))
            def _():
                send1_ref[spot, rows:, :] = term[group]

        write.wait()


def mlp_pass(place, start, mixed, out_grad, proj, gain, fc1, fc2, groups):
    tokens, width = start.shape
    wide = fc1.shape[1]
    size = wide // groups
    half = groups // 2
    blocks = tokens // BLOCK

    def once(shape):
        return pl.BlockSpec(shape, lambda *_: (0,) * len(shape), pipeline_mode=pl.Buffered(1))

    def chunk(i, s):
        return turn(jnp.clip(i - blocks, 0, groups - 1), groups, s)

    def part(first):
        return pl.BlockSpec(
            (size, width), lambda i, s: (jnp.clip(i - blocks - first, 0, half - 1), 0)
        )

    def rows_from(first):
        return pl.BlockSpec((BLOCK, width), lambda i, s: (jnp.clip(i - first, 0, blocks - 1), 0))

    halves = shape_of(wide // 2, width, dtype=low)
    joint = (CUTS // 2, (wide + width) // CUTS, width)
    full_low, full = (pltpu.VMEM((tokens, width), kind) for kind in (low, jnp.float32))
    return call(
        functools.partial(mlp_kernel, blocks, groups),
        "mlp_pass",
        (2 * blocks + groups + 1,),
        [rows_from(0), rows_from(0), once((tokens, width)), once(proj.shape), once((1, width))]
        + [
            pl.BlockSpec((width, size), lambda i, s: (0, chunk(i, s))),
            pl.BlockSpec((size, width), lambda i, s: (chunk(i, s), 0)),
        ],
        [pl.BlockSpec(memory_space=pl.ANY)]
        + [rows_from(blocks + groups), rows_from(blocks + groups), once((8, width))]
        + [part(0), part(half), once(joint), once(joint)],
        [
            shape_of(tokens, width),
            shape_of(tokens, width),
            shape_of(tokens, width, dtype=low),
            shape_of(8, width),
        ]
        + [halves, halves] + [shape_of(*joint, dtype=low)] * 2,
        2 * tokens * width * (3 * width + 6 * wide),
        20 * tokens * width + 8 * fc1.size,
        [full, full, full_low, full_low]
        + [pltpu.VMEM((tokens, size), low)] * 2
        + [full, pltpu.SemaphoreType.DMA],
        vmem=VM,
    )(place, start, mixed, out_grad, proj, gain.reshape(1, width), fc1, fc2)


def start_kernel(blocks, groups, place, *refs):
    back_refs, left_refs, refs = refs[:PARTS], refs[PARTS : 2 * PARTS], refs[2 * PARTS :]
    weight_ref, start_ref, gain_ref, grad_ref, normed_ref = refs[:5]
    out_ref, sum_ref, keep_ref, send_ref = refs[5:]
    step = pl.program_id(0)
    width = start_ref.shape[1]

    @pl.when(step == 0)
    def _():
        sum_ref[...] = jnp.zeros_like(sum_ref)

    @pl.when(step < blocks)
    def _():
        back = 0.0
        for i, back_ref in enumerate(back_refs):
            some = back_ref.shape[2]
            for j in range(3):
                first = j * width + i * some
                back = back + dot32(back_ref[j], weight_ref[:, first : first + some], LANES)
        unit, inverse = units(start_ref[...])
        grad = grad_ref[...] + norm_back(back, unit, inverse, gain_ref[...])
        out_ref[...] = grad.astype(low)
        sum_ref[0:1, :] += jnp.sum(back * unit, axis=0, keepdims=True)
        sum_ref[1:2, :] += jnp.sum(grad, axis=0, keepdims=True)

    @pl.when(step >= blocks)
    def _():
        left = jnp.concatenate([ref[0] for ref in left_refs], axis=1)
        term = dot32(left, normed_ref[...], ROWS).astype(low)
        each = 3 * width // groups // UNIT
        for u in range(width // UNIT):
            unit = (step - blocks) * (width // UNIT) + u
            group = unit // each
            first = pl.multiple_of(((group // 2) * each + unit % each) * UNIT, UNIT)
            mine = group % 2 == place[0] % 2
            part = term[u * UNIT : (u + 1) * UNIT]

            @pl.when(mine)
            def _():
                keep_ref[pl.ds(first, UNIT), :] = part

            @pl.when(jnp.logical_not(mine))
            def _():
                send_ref[pl.ds(first, UNIT), :] = part


def start_pass(place, backs, weight, start, gain, grad_after, normed, groups, behind):
    tokens, width = start.shape
    blocks = tokens // BLOCK

    def row_block(i):
        return jnp.minimum(i, blocks - 1)

    block = pl.BlockSpec((BLOCK, width), lambda i, s: (row_block(i), 0))
    half = (3 * width // 2, width)
    return call(
        functools.partial(start_kernel, blocks, groups),
        "start_pass",
        (blocks + 3,),
        [pl.BlockSpec((3, BLOCK, width // PARTS), lambda i, s: (0, row_block(i), 0))] * PARTS
        + [
            pl.BlockSpec(
                (1, tokens, width // PARTS), lambda i, s: (jnp.maximum(i - blocks, 0), 0, 0)
            )
        ]
        * PARTS
        + [whole(weight.shape), block, whole((1, width)), block, whole(normed.shape)],
        [block, whole((8, width)), whole(half), whole(half)],
        [
            shape_of(tokens, width, dtype=low),
            shape_of(8, width),
            shape_of(*half, dtype=low),
            shape_of(*half, dtype=low),
        ],
        12 * tokens * width * width,
        24 * tokens * width + 2 * weight.size,
        behind=behind,
    )(place, *backs, *backs, weight, start, gain.reshape(1, width), grad_after, normed)


def patch_kernel(count, slots, place, *refs):
    pieces, refs = refs[:count], refs[count:]
    grad_ref, kernel_ref, w2_ref, sum1_ref, sum2_ref, ids_ref, mask_ref = refs[:7]
    keep_ref, send_ref, small_ref, pixel_ref, lines, both, hidden, small = refs[7:]
    step = pl.program_id(0)
    width = grad_ref.shape[1]
    codes = hidden.shape[1]

    @pl.when(step == 0)
    def _():
        patch_terms(place, slots, grad_ref, pieces, keep_ref, send_ref, both, lines)
        hidden[...] = jnp.zeros_like(hidden)

    @pl.when(step > 0)
    def _():
        pixel_ref[0] = dot32(kernel_ref[...], grad_ref[...], LANES).astype(low)
        total = hidden[...]
        for p in range(both.shape[1] // slots):
            total = total + dot32(
                both[step - 1, p * slots : (p + 1) * slots, :],
                w2_ref[:, p * width : (p + 1) * width],
                LANES,
            )
        hidden[...] = total

    @pl.when(step == count)
    def _():
        first = jnp.where(place[0] == 0, 1.0, 0.0)
        rows = small.shape[0]
        small[...] = jnp.zeros_like(small)
        small[:slots, :codes] = hidden[...] * mask_ref[...]
        small[:slots, codes : 2 * codes] = jnp.broadcast_to(ids_ref[...] * first, (slots, codes))
        small[slots : slots + 2, :] = sum1_ref[0:2, :]
        small[slots + 2 : slots + 3, :] = sum2_ref[0:1, :]
        small[slots + 3 : slots + 4, :] = jnp.full((1, width), place[1].astype(jnp.float32) * first)
        small_low = small[...].astype(low)
        small_ref[...] = small_low
        send_ref[send_ref.shape[0] - rows :, :] = small_low


def patch_terms(place, slots, grads, pieces, keep_ref, send_ref, all_ref, lines):
    count = len(pieces)
    rows = pieces[0].shape[0]
    per = slots // count
    pixels = rows // per
    width = grads.shape[1]
    for m, piece in enumerate(pieces):
        term = jnp.dot(piece[...], grads[...], preferred_element_type=jnp.float32)
        for s in range(per):
            slot = (place[0] ^ m) * per + s
            for c in range(0, width, 128):
                lines[c // 128, pl.ds(slot, pixels, stride=slots), :] = term[
                    s * pixels : (s + 1) * pixels, c : c + 128
                ]
    span = pixels * slots // count
    for j in range(count):
        mine = (place[0] & 1) == j % 2
        for c in range(0, width, 128):
            part = lines[c // 128, j * span : (j + 1) * span, :].astype(low)
            all_ref[j, :, c : c + 128] = part

        @pl.when(mine)
        def _():
            keep_ref[j // 2] = all_ref[j]

        @pl.when(jnp.logical_not(mine))
        def _():
            send_ref[j // 2 * span : (j // 2 + 1) * span, :] = all_ref[j]


def patch_pass(place, pieces, grad_embed, kernel, gen_w2, sum1, sum2, ids_column, mask_column, behind):
    rows, tokens = pieces[0].shape
    count = len(pieces)
    width = grad_embed.shape[1]
    codes = gen_w2.shape[0]
    slots = ids_column.shape[0]
    span = gen_w2.shape[1] // count
    more = -(-(slots + 4) // 16) * 16

    def turned(i):
        return jnp.maximum(i - 1, 0)

    kept = (count // 2, rows, width)
    sent = (count // 2 * rows + more, width)
    return call(
        functools.partial(patch_kernel, count, slots),
        "patch_pass",
        (1 + count,),
        [whole(pieces[0].shape)] * count
        + [
            whole(grad_embed.shape),
            pl.BlockSpec((rows, width), lambda i, s: (s[0] ^ turned(i), 0)),
            pl.BlockSpec((codes, span), lambda i, s: (0, turned(i))),
            whole((8, width)),
            whole((8, width)),
            whole((slots, 1)),
            whole((slots, 1)),
        ],
        [
            whole(kept),
            whole(sent),
            whole((more, width)),
            pl.BlockSpec((1, rows, tokens), lambda i, s: (turned(i), 0, 0)),
        ],
        [
            shape_of(*kept, dtype=low),
            shape_of(*sent, dtype=low),
            shape_of(more, width, dtype=low),
            shape_of(count, rows, tokens, dtype=low),
        ],
        4 * tokens * width * rows * count,
        2 * (tokens * width + gen_w2.size) + 6 * rows * count * (width + tokens),
        [
            pltpu.VMEM((width // 128, rows * count, 128), jnp.float32),
            pltpu.VMEM((count, rows, width), low),
            pltpu.VMEM((slots, codes), jnp.float32),
            pltpu.VMEM((more, width), jnp.float32),
        ],
        behind=behind,
    )(
        place,
        *pieces,
        grad_embed,
        kernel,
        gen_w2,
        sum1,
        sum2,
        ids_column,
        mask_column,
    )


def join_kernel(place, *refs):
    out_ref = refs[-1]
    for m, piece in enumerate(refs[:-1]):

        @pl.when(pl.program_id(0) == m)
        def _():
            out_ref[...] = piece[...].astype(jnp.float32)


def join_pixels(place, pieces, behind):
    rows, tokens = pieces[0].shape
    count = len(pieces)
    return call(
        join_kernel,
        "join_pixels",
        (count,),
        [whole(pieces[0].shape)] * count,
        pl.BlockSpec((rows, tokens), lambda i, s: (0, s[0] ^ i)),
        shape_of(rows, count * tokens),
        0,
        6 * rows * count * tokens,
        behind=behind,
    )(place, *pieces)


def finish_kernel(slots, sensors, place, small_ref, rows_ref, table_ref, w1_ref, wave_ref, gen1_ref, gen2_ref, sensor_ref, norm_ref):
    groups = small_ref.shape[0]
    bands, codes = wave_ref.shape
    table, weight = table_ref[...], w1_ref[...]
    width = norm_ref.shape[1]

    def picked(q):
        return small_ref[q, :slots, codes : codes + bands].astype(jnp.float32).astype(jnp.int32)

    ids = [picked(q) for q in range(groups)]
    hidden = code_rows(jnp.concatenate(ids, axis=0), table, weight)[2].astype(low)
    for i in range(rows_ref.shape[0]):
        wide = rows_ref.shape[2]
        gen2_ref[:, i * wide : (i + 1) * wide] = dot32(hidden, rows_ref[i], ROWS)

    in_order = [place[2] ^ g for g in range(groups)]
    ids = [picked(q) for q in in_order]
    select, rows, _, slope = code_rows(jnp.concatenate(ids, axis=0), table, weight)
    grad = jnp.concatenate(
        [small_ref[q, :slots, :codes].astype(jnp.float32) for q in in_order], axis=0
    )
    scaled = slope * grad
    gen1_ref[...] = lax.dot_general(
        rows, scaled, ROWS, precision=highest, preferred_element_type=jnp.float32
    )
    row_grad = grad + lax.dot_general(
        scaled,
        weight.astype(jnp.float32),
        LANES,
        precision=highest,
        preferred_element_type=jnp.float32,
    )
    wave_ref[...] = lax.dot_general(
        select, row_grad, ROWS, precision=highest, preferred_element_type=jnp.float32
    )
    norms = [jnp.zeros((1, width), jnp.float32)] * 2
    each = [jnp.zeros((1, width), jnp.float32)] * sensors
    for q in in_order:
        lines = small_ref[q, slots : slots + 8, :].astype(jnp.float32)
        norms = [norms[0] + lines[0:1], norms[1] + lines[2:3]]
        for s in range(sensors):
            each[s] = each[s] + jnp.where(lines[3:4] == float(s), lines[1:2], 0.0)
    for n in range(2):
        norm_ref[n : n + 1, :] = norms[n]
    for s in range(sensors):
        sensor_ref[s : s + 1, :] = each[s]


def finish(place, small, rows, wave_table, gen_w1, slots, sensors, width):
    codes = wave_table.shape[1]
    shapes = [
        wave_table.shape,
        gen_w1.shape,
        (codes, rows.shape[0] * rows.shape[2]),
        (sensors, width),
        (2, width),
    ]
    return call(
        functools.partial(finish_kernel, slots, sensors),
        "finish",
        (1,),
        [whole(small.shape), whole(rows.shape), whole(wave_table.shape), whole(gen_w1.shape)],
        [whole(shape) for shape in shapes],
        [shape_of(*shape) for shape in shapes],
        2 * rows.size * codes,
        4 * rows.size,
    )(place, small, rows, wave_table, gen_w1)


def swap(piece, axis, mask):
    count = lax.axis_size(axis)
    return lax.ppermute(piece, axis, [(i, i ^ mask) for i in range(count)])


def bits_of(axis):
    return lax.axis_size(axis).bit_length() - 1


class Scatter:
    def __init__(self, keep, send, bits):
        self.bits = bits
        self.dims = [("band", bit) for bit in reversed(range(1, bits_of("band")))] + [
            ("dp", bit) for bit in reversed(range(bits_of("dp")))
        ]
        rows = keep.shape[0] >> len(self.dims)
        shape = (2,) * len(self.dims) + (rows, keep.shape[1])
        got = swap(send, "band", 1)
        self.last = got
        self.parts = [keep.reshape(shape), got.reshape(shape)]

    def columns(self, first, last):
        some = object.__new__(Scatter)
        some.bits = self.bits
        some.dims = list(self.dims)
        some.last = self.last
        some.parts = [part[..., first:last] for part in self.parts]
        return some

    def result(self):
        return sum(part.astype(jnp.float32) for part in self.parts)


def pick(rows, index, dim):
    return lax.dynamic_index_in_dim(rows, index, dim, False, allow_negative_indices=False)


def halve(sums, axis, bit, when=()):
    (mine, other), _ = lax.optimization_barrier((sums[0].bits[axis, bit], when))
    sends = []
    for one in sums:
        dim = one.dims.index((axis, bit))
        one.dims.pop(dim)
        send = sum(
            pick(part, other, dim).astype(jnp.float32)
            for part in one.parts
        )
        sends.append(send.astype(low))
        one.parts = [pick(part, mine, dim) for part in one.parts]
    send = sends[0] if len(sends) == 1 else jnp.concatenate(sends, axis=-2)
    got = swap(send, axis, 1 << bit)
    first = 0
    for one, each in zip(sums, sends):
        rows = each.shape[-2]
        one.parts.append(lax.slice_in_dim(got, first, first + rows, axis=got.ndim - 2))
        one.last = got
        first += rows
    return send


def rounded(rows):
    return lax.reduce_precision(rows, 8, 7).astype(low)


def shards(
    pixels,
    band_ids,
    band_mask,
    sensor_tags,
    segment_ids,
    wave_table,
    gen_w1,
    gen_w2,
    sensor_table,
    ln1_gain,
    qkv_weight,
    proj_weight,
    ln2_gain,
    fc1_weight,
    fc2_weight,
    out_grad,
):
    band_place = lax.axis_index("band")
    dp_place = lax.axis_index("dp")
    band_count = lax.axis_size("band")
    dp_count = lax.axis_size("dp")
    slots_dev = pixels.shape[0]
    slots = band_ids.shape[1]
    tok_dev, model_width = out_grad.shape
    patch_pixels = pixels.shape[2]
    sensors = sensor_table.shape[0]
    part_rows = slots_dev * patch_pixels
    place = jnp.stack([band_place, sensor_tags[0], dp_place]).astype(jnp.int32)

    own_pixels = pixels.transpose(0, 2, 1).reshape(part_rows, -1)
    pieces = []
    for mask in range(band_count):
        piece = lax.dynamic_slice_in_dim(own_pixels, (band_place ^ mask) * tok_dev, tok_dev, 1)
        pieces.append(swap(piece, "band", mask) if mask else piece)

    kernel = generate_kernels(band_ids, band_mask, wave_table, gen_w1, gen_w2, model_width)
    kernel = kernel.reshape(slots * patch_pixels, model_width)
    start_rows, normed1, projected = embed(
        place, kernel, sensor_table, ln1_gain, qkv_weight, pieces
    )
    window = windows(segment_ids)
    query_side, key_side = features(segment_ids)
    bits = {
        (axis, bit): ((at >> bit) & 1, 1 - ((at >> bit) & 1))
        for axis, at in (("band", band_place), ("dp", dp_place))
        for bit in range(bits_of(axis))
    }
    turned_places = [dp_place ^ i for i in range(dp_count)]
    ids_column = band_ids.reshape(slots, 1).astype(jnp.float32)
    mask_column = band_mask.reshape(slots, 1).astype(jnp.float32)
    projected, window, query_side, key_side, bits, turned_places, ids_column, mask_column = (
        lax.optimization_barrier(
            (
                projected,
                window,
                query_side,
                key_side,
                bits,
                turned_places,
                ids_column,
                mask_column,
            )
        )
    )
    attended, totals = attend_forward(projected, segment_ids, window, query_side, key_side)
    encoded, grad_after, grad_attended, norm2_sums, send2, keep2, send1, keep1 = mlp_pass(
        place,
        start_rows,
        attended,
        out_grad,
        proj_weight,
        ln2_gain,
        fc1_weight,
        fc2_weight,
        band_count,
    )
    band_rest = [("band", bit) for bit in range(1, bits_of("band"))]
    dp_rest = [("dp", bit) for bit in range(bits_of("dp"))]
    devices = band_count * dp_count
    fc1_rows = fc1_weight.shape[1] // devices
    if devices != CUTS:
        first = fc1_weight.shape[1] // CUTS
        send1, keep1 = [
            jnp.concatenate(
                [
                    part.reshape(devices // 2, -1, model_width)
                    for part in (joint[:, :first], joint[:, first:])
                ],
                axis=1,
            )
            for joint in (send1, keep1)
        ]
    fc2_sum = Scatter(keep2, send2, bits)
    fc1_sum = Scatter(*[part.reshape(-1, model_width) for part in (keep1, send1)], bits)
    backs = []

    def back_part(behind):
        backs.append(
            attend_back(
                projected,
                segment_ids,
                window,
                query_side,
                key_side,
                grad_attended,
                attended,
                totals,
                len(backs),
                behind,
            )
        )

    back_part([])
    sent = [
        halve([fc2_sum], *band_rest[0], backs[-1]),
        halve([fc1_sum], *dp_rest[0], backs[-1]),
    ]
    for item in band_rest[1:]:
        sent.append(halve([fc2_sum], *item))
    back_part(sent)
    back_part([backs[-1]])
    sent = [halve([fc2_sum], *dp_rest[0], backs[-1])]
    for item in band_rest:
        sent.append(halve([fc1_sum], *item, backs[-1]))
    grad_embed, norm1_sums, keep, send = start_pass(
        place,
        backs,
        qkv_weight,
        start_rows,
        ln1_gain,
        grad_after,
        normed1,
        band_count,
        sent,
    )
    half = model_width // 2
    qkv_sum = Scatter(keep, send, bits)

    keep, send, small, pixel_parts = patch_pass(
        place,
        pieces,
        grad_embed,
        kernel,
        gen_w2,
        norm1_sums,
        norm2_sums,
        ids_column,
        mask_column,
        [],
    )
    qkv_halves = [qkv_sum.columns(0, half), qkv_sum.columns(half, model_width)]
    for item in dp_rest[1:3]:
        halve([fc2_sum], *item, small)
        halve([fc1_sum], *item, small)
    halve(qkv_halves[:1], *dp_rest[0], small)
    halve(qkv_halves[1:], *band_rest[0], small)
    for item in band_rest[1:]:
        halve(qkv_halves[1:], *item)
    more = small.shape[0]
    got = swap(send, "band", 1)
    patch_parts = [keep, got[:-more].reshape(keep.shape)]
    small = small.astype(jnp.float32) + got[-more:].astype(jnp.float32)
    for bit in range(1, bits_of("band")):
        mine, other = bits["band", bit]
        patch_parts = [
            part.reshape((part.shape[0] // 2, 2) + part.shape[1:]) for part in patch_parts
        ]
        away = sum(
            pick(part, other, 1).astype(jnp.float32)
            for part in patch_parts
        ).astype(low)
        patch_parts = [pick(part, mine, 1) for part in patch_parts]
        small_low = rounded(small)
        got = swap(
            jnp.concatenate([away.reshape(-1, model_width), small_low]), "band", 1 << bit
        )
        patch_parts.append(got[:-more].reshape(away.shape))
        small = small_low.astype(jnp.float32) + got[-more:].astype(jnp.float32)
    pixel_pieces = [
        swap(lax.optimization_barrier((pixel_parts[mask], small))[0], "band", mask)
        if mask
        else pixel_parts[0]
        for mask in range(band_count)
    ]
    span = patch_pixels // band_count
    patch_sum = sum(part.astype(jnp.float32) for part in patch_parts).reshape(
        span, slots, model_width
    )
    patch_low = (patch_sum * mask_column[None]).astype(low)
    cuts = max(1, dp_count // span)
    share = model_width // cuts
    if cuts > 1:
        patch_low = patch_low.reshape(span, slots, cuts, share).transpose(0, 2, 1, 3)
    patch_low = patch_low.reshape(dp_count, -1, slots, share)
    held = jnp.stack(
        [pick(patch_low, turned, 0) for turned in turned_places]
    )
    all_small = rounded(small)[None]

    shape = held.shape
    for n, (axis, bit) in enumerate(dp_rest):
        view = held.reshape((dp_count >> (bit + 1), 2, 1 << bit) + shape[1:])
        away = view[:, 1]
        rows = away.size // model_width
        got = swap(
            jnp.concatenate(
                [away.reshape(rows, model_width), all_small.reshape(-1, model_width)]
            ),
            axis,
            1 << bit,
        )
        if n == 0:
            halve(qkv_halves[1:], *dp_rest[0], all_small)
            for item in band_rest:
                halve(qkv_halves[:1], *item, all_small)
        else:
            halve(qkv_halves, axis, bit)
        if n > 2:
            halve([fc2_sum], axis, bit)
            halve([fc1_sum], axis, bit)
        held = jnp.stack([view[:, 0], got[:rows].reshape(away.shape)], axis=1).reshape(shape)
        all_small = jnp.concatenate([all_small, got[rows:].reshape(all_small.shape)])
    kernel_rows = held.transpose(1, 0, 2, 3).reshape(shape[1], dp_count * slots, share)
    wave_table_grad, gen_w1_grad, gen_w2_grad, sensor_grad, norm_grads = finish(
        place, all_small, kernel_rows, wave_table, gen_w1, slots, sensors, model_width
    )
    grad_pixels = join_pixels(place, pixel_pieces, [])
    grad_pixels = grad_pixels.reshape(slots_dev, patch_pixels, -1).transpose(0, 2, 1)
    qkv_grad = jnp.concatenate([part.result() for part in qkv_halves], axis=1)
    fc2_grad, joint = fc2_sum.result(), fc1_sum.result()
    fc1_grad, proj_grad = joint[:fc1_rows], joint[fc1_rows:]
    return (
        encoded,
        grad_pixels,
        wave_table_grad,
        gen_w1_grad,
        gen_w2_grad,
        sensor_grad,
        norm_grads[0],
        qkv_grad.T,
        proj_grad.T,
        norm_grads[1],
        fc1_grad.T,
        fc2_grad,
    )


def solution(mesh):
    return jax.shard_map(
        shards,
        mesh=mesh,
        in_specs=(
            P("band", "dp", None),
            P("dp", None),
            P("dp", None),
            P("dp"),
            P(("dp", "band"), None),
            P(),
            P(),
            P(),
            P(),
            P(),
            P(),
            P(),
            P(),
            P(),
            P(),
            P(("dp", "band"), None),
        ),
        out_specs=(
            P(("dp", "band"), None),
            P("band", "dp", None),
            P(),
            P(),
            P(None, ("band", "dp")),
            P(),
            P(),
            P(None, ("band", "dp")),
            P(None, ("band", "dp")),
            P(),
            P(None, ("band", "dp")),
            P(("band", "dp"), None),
        ),
        check_vma=False,
    )
```

```python
import functools

import jax
import jax.numpy as jnp
from jax import lax
from jax.experimental import pallas as pl
from jax.experimental.pallas import tpu as pltpu
from jax.sharding import PartitionSpec as P

highest = lax.Precision.HIGHEST
UNIT = 96
PARTS = 3
PAIRS = 3
BACK_PAIRS = 2
VA = 58
CUTS = 32
VM = 56
low = jnp.bfloat16
MIB = 1 << 20

BLOCK = 256
STEP = 256
FAR = 2.0**30
LANES = (((1,), (1,)), ((), ()))
ROWS = (((0,), (0,)), ((), ()))


def dot32(left, right, dims):
    return lax.dot_general(left, right, dims, preferred_element_type=jnp.float32)


def windows(segment_ids):
    length = segment_ids.shape[1]
    first = segment_ids[:, ::BLOCK]
    last = segment_ids[:, BLOCK - 1 :: BLOCK]
    begin = jnp.sum(segment_ids[:, None, :] < first[:, :, None], axis=-1)
    end = jnp.sum(segment_ids[:, None, :] <= last[:, :, None], axis=-1)
    low = begin // STEP
    count = (end + STEP - 1) // STEP - low
    return jnp.stack([low, count - 1], axis=-1).astype(jnp.int32).reshape(-1)


def features(segment_ids):
    lane = jnp.arange(128, dtype=jnp.int32)
    code = segment_ids.reshape(-1, 1)
    same = (code == (lane % 64)[None, :])
    used = (lane % 64 < 4)[None, :]
    query_side = jnp.where(same & used, 1.0, 0.0)
    key_side = jnp.where(used & ~same, -FAR, 0.0)
    return query_side.astype(jnp.bfloat16), key_side.astype(jnp.bfloat16)


def head_masks():
    lane = lax.broadcasted_iota(jnp.int32, (1, 128), 1)
    low = jnp.where(lane < 64, 1.0, 0.0)
    return low.astype(jnp.bfloat16), (1.0 - low).astype(jnp.bfloat16)


def forward_kernel(win, q_ref, k_ref, v_ref, qf_ref, kf_ref, o_ref, lse_ref, qa, ka, va):
    length = q_ref.shape[0]
    blocks = length // BLOCK
    base = pl.program_id(0) * blocks * 2
    masks = head_masks()
    pairs = q_ref.shape[1] // 128
    heads = 2 * pairs
    for n in range(heads):
        mask, cols = masks[n % 2], slice(n // 2 * 128, (n // 2 + 1) * 128)
        other = jnp.bfloat16(1.0) - mask
        qa[n] = q_ref[:, cols] * (mask * jnp.bfloat16(0.125)) + qf_ref[...] * other
        ka[n] = k_ref[:, cols] * mask + kf_ref[...] * other
        va[n] = v_ref[:, cols] * mask + other

    def one_block(block, carry):
        rows = pl.ds(pl.multiple_of(block * BLOCK, BLOCK), BLOCK)
        low = pl.multiple_of(win[base + 2 * block] * STEP, STEP)

        def run(width):
            keys = pl.ds(low, width)
            mixes, peaks = [], []
            for n in range(heads):
                scores = dot32(qa[n, rows, :], ka[n, keys, :], LANES)
                peak = jnp.max(scores, axis=1, keepdims=True)
                probs = jnp.exp(scores - peak).astype(jnp.bfloat16)
                mixes.append(jnp.dot(probs, va[n, keys, :], preferred_element_type=jnp.float32))
                peaks.append(peak)
            low_lanes = lax.broadcasted_iota(jnp.int32, (1, 128), 1) < 64
            for n in range(0, heads, 2):
                mixed = jnp.where(low_lanes, mixes[n], mixes[n + 1])
                total = pltpu.roll(jnp.where(low_lanes, mixes[n + 1], mixes[n]), 64, 1)
                o_ref[rows, n * 64 : n * 64 + 128] = (mixed / total).astype(jnp.bfloat16)
                both = (jnp.where(low_lanes, peaks[n], peaks[n + 1]) + jnp.log(total)).T
                lse_ref[0, n // 2, 0:1, rows] = both[0:1]
                lse_ref[0, n // 2, 1:2, rows] = both[64:65]

        count = win[base + 2 * block + 1]
        for size in range(length // STEP):
            pl.when(count == size)(functools.partial(run, (size + 1) * STEP))
        return carry

    lax.fori_loop(0, blocks, one_block, 0)


def back_kernel(
    win,
    q_ref,
    k_ref,
    v_ref,
    qf_ref,
    kf_ref,
    g_ref,
    o_ref,
    lse_ref,
    out_ref,
    qa,
    ka,
    qh,
    kh,
    vh,
    gh,
    delta,
    dk,
    dv,
):
    length = q_ref.shape[0]
    blocks = length // BLOCK
    base = pl.program_id(0) * blocks * 2
    masks = head_masks()
    pairs = q_ref.shape[1] // 128
    heads = 2 * pairs
    for n in range(heads):
        mask, cols = masks[n % 2], slice(n // 2 * 128, (n // 2 + 1) * 128)
        other = jnp.bfloat16(1.0) - mask
        scaled = q_ref[:, cols] * (mask * jnp.bfloat16(0.125))
        qh[n] = scaled
        qa[n] = scaled + qf_ref[...] * other
        own = k_ref[:, cols] * mask
        kh[n] = own
        ka[n] = own + kf_ref[...] * other
        vh[n] = v_ref[:, cols] * mask
        gh[n] = g_ref[:, cols] * mask
    product = g_ref[...].astype(jnp.float32) * o_ref[...].astype(jnp.float32)
    turned = product.T
    for n in range(heads):
        delta[n : n + 1, :] = jnp.sum(turned[n * 64 : (n + 1) * 64], axis=0, keepdims=True)
    dk[...] = jnp.zeros_like(dk)
    dv[...] = jnp.zeros_like(dv)

    def one_block(block, carry):
        rows = pl.ds(pl.multiple_of(block * BLOCK, BLOCK), BLOCK)
        low = pl.multiple_of(win[base + 2 * block] * STEP, STEP)

        def run(width):
            keys = pl.ds(low, width)
            for p in range(pairs):
                turned_grad = None
                cols = slice(p * 128, (p + 1) * 128)
                for n in (2 * p, 2 * p + 1):
                    scores = dot32(ka[n, keys, :], qa[n, rows, :], LANES)
                    probs = jnp.exp(scores - lse_ref[0, p, n % 2 : n % 2 + 1, rows])
                    grad_probs = dot32(vh[n, keys, :], gh[n, rows, :], LANES)
                    grad_scores = (probs * (grad_probs - delta[n : n + 1, rows])).astype(
                        jnp.bfloat16
                    )
                    dv[keys, cols] += jnp.dot(
                        probs.astype(jnp.bfloat16),
                        gh[n, rows, :],
                        preferred_element_type=jnp.float32,
                    )
                    dk[keys, cols] += jnp.dot(
                        grad_scores, qh[n, rows, :], preferred_element_type=jnp.float32
                    )
                    term = dot32(grad_scores, kh[n, keys, :], ROWS)
                    turned_grad = term if turned_grad is None else turned_grad + term
                out_ref[0, rows, cols] = (turned_grad * 0.125).astype(jnp.bfloat16)

        count = win[base + 2 * block + 1]
        for size in range(length // STEP):
            pl.when(count == size)(functools.partial(run, (size + 1) * STEP))
        return carry

    lax.fori_loop(0, blocks, one_block, 0)
    out_ref[1] = dk[...].astype(jnp.bfloat16)
    out_ref[2] = dv[...].astype(jnp.bfloat16)


def attend_forward(projected, segment_ids, win, query_side, key_side):
    seqs, length = segment_ids.shape
    width = projected.shape[1] // 3
    wide = 128 * PAIRS
    steps = width // wide

    def columns(offset):
        return pl.BlockSpec((length, wide), lambda s, p, w: (s, p + offset))

    fixed = pl.BlockSpec((length, 128), lambda s, p, w: (s, 0))
    return call(
        forward_kernel,
        "attend_forward",
        (seqs, steps),
        [columns(0), columns(steps), columns(2 * steps), fixed, fixed],
        [columns(0), pl.BlockSpec((1, PAIRS, 8, length), lambda s, p, w: (s, p, 0, 0))],
        [
            shape_of(seqs * length, width, dtype=low),
            shape_of(seqs, width // 128, 8, length),
        ],
        4 * seqs * length * length * width,
        8 * seqs * length * width,
        [pltpu.VMEM((2 * PAIRS, length, 128), low)] * 3,
        vmem=VA,
    )(win, projected, projected, projected, query_side, key_side)


def attend_back(projected, segment_ids, win, query_side, key_side, grad, mixed, lse, part, behind):
    seqs, length = segment_ids.shape
    width = projected.shape[1] // 3
    wide = 128 * BACK_PAIRS
    steps = width // wide
    run = steps // PARTS
    begin = part * run

    def columns(offset):
        return pl.BlockSpec((length, wide), lambda s, p, w: (s, p + offset + begin))

    fixed = pl.BlockSpec((length, 128), lambda s, p, w: (s, 0))
    pair_low = pltpu.VMEM((2 * BACK_PAIRS, length, 128), low)
    return call(
        back_kernel,
        "attend_back",
        (seqs, run),
        [
            columns(0),
            columns(steps),
            columns(2 * steps),
            fixed,
            fixed,
            columns(0),
            columns(0),
            pl.BlockSpec((1, BACK_PAIRS, 8, length), lambda s, p, w: (s, p + begin, 0, 0)),
        ],
        pl.BlockSpec((3, length, wide), lambda s, p, w: (0, s, p)),
        shape_of(3, seqs * length, run * wide, dtype=low),
        10 * seqs * length * length * run * wide,
        14 * seqs * length * run * wide,
        [pair_low] * 6
        + [
            pltpu.VMEM((8, length), jnp.float32),
            pltpu.VMEM((length, wide), jnp.float32),
            pltpu.VMEM((length, wide), jnp.float32),
        ],
        vmem=VA,
        behind=behind,
    )(win, projected, projected, projected, query_side, key_side, grad, mixed, lse)


def whole(shape):
    return pl.BlockSpec(shape, lambda *_: (0,) * len(shape))


def call(
    kernel,
    name,
    grid,
    in_specs,
    out_specs,
    out_shape,
    flops,
    moved,
    scratch=(),
    prefetch=1,
    vmem=40,
    behind=(),
):
    first = prefetch + len(in_specs)

    def body(*refs):
        kernel(*refs[:first], *refs[first + len(behind) :])

    run = pl.pallas_call(
        body,
        grid_spec=pltpu.PrefetchScalarGridSpec(
            num_scalar_prefetch=prefetch,
            grid=grid,
            in_specs=list(in_specs) + [pl.BlockSpec(memory_space=pl.ANY)] * len(behind),
            out_specs=out_specs,
            scratch_shapes=list(scratch),
        ),
        out_shape=out_shape,
        compiler_params=pltpu.CompilerParams(vmem_limit_bytes=vmem * MIB),
        cost_estimate=pl.CostEstimate(flops=flops, bytes_accessed=moved, transcendentals=0),
        name=name,
    )
    return lambda *args: run(*args, *behind)


def shape_of(*shape, dtype=jnp.float32):
    return jax.ShapeDtypeStruct(shape, dtype)


def units(rows):
    center = rows - jnp.mean(rows, axis=-1, keepdims=True)
    inverse = lax.rsqrt(jnp.mean(center * center, axis=-1, keepdims=True) + 1e-05)
    return center * inverse, inverse


def norm_back(grad_rows, unit_rows, inverse, gain):
    scaled = grad_rows * gain
    inner = jnp.mean(scaled * unit_rows, axis=-1, keepdims=True)
    return inverse * (scaled - jnp.mean(scaled, axis=-1, keepdims=True) - unit_rows * inner)


def gelu_both(rows):
    root = 0.7978845608028654
    square = rows * rows
    curve = jnp.tanh(rows * (root + (root * 0.044715) * square))
    half = 0.5 + 0.5 * curve
    slope = half + (0.5 * rows) * (1.0 - curve * curve) * (root + (3.0 * root * 0.044715) * square)
    return rows * half, slope


def code_rows(ids, table, weight):
    lane = lax.broadcasted_iota(jnp.int32, (ids.shape[0], table.shape[0]), 1)
    select = jnp.where(ids == lane, 1.0, 0.0)
    rows = jnp.dot(select.astype(low), table, preferred_element_type=jnp.float32)
    raw = jnp.dot(rows.astype(low), weight, preferred_element_type=jnp.float32)
    value, slope = gelu_both(raw)
    return select, rows, rows + value, slope


def generate_kernel(ids_ref, mask_ref, table_ref, w1_ref, w2_ref, out_ref, hidden, lines):
    slots, pixels, width = out_ref.shape

    @pl.when(pl.program_id(0) == 0)
    def _():
        hidden[...] = code_rows(ids_ref[...], table_ref[...], w1_ref[...])[2].astype(low)

    for p in range(pixels):
        made = jnp.dot(
            hidden[...], w2_ref[:, p * width : (p + 1) * width], preferred_element_type=jnp.float32
        )
        for c in range(0, width, 128):
            lines[c // 128, pl.ds(p, slots, stride=pixels), :] = (
                made[:, c : c + 128] * mask_ref[...]
            )
    for c in range(0, width, 128):
        out_ref[:, :, c : c + 128] = lines[c // 128, : slots * pixels, :].reshape(slots, pixels, 128).astype(low)


def generate_kernels(band_ids, band_mask, wave_table, gen_w1, gen_w2, width):
    slots = band_ids.shape[1]
    pixels = gen_w2.shape[1] // width
    part = 16
    return call(
        generate_kernel,
        "generate",
        (pixels // part,),
        [
            whole((slots, 1)),
            whole((slots, 1)),
            whole(wave_table.shape),
            whole(gen_w1.shape),
            pl.BlockSpec((gen_w2.shape[0], part * width), lambda i: (0, i)),
        ],
        pl.BlockSpec((slots, part, width), lambda i: (0, i, 0)),
        shape_of(slots, pixels, width, dtype=low),
        2 * 128 * slots * gen_w2.shape[1],
        2 * gen_w2.size,
        [
            pltpu.VMEM((slots, gen_w1.shape[0]), low),
            pltpu.VMEM((width // 128, (slots + 1) * part, 128), jnp.float32),
        ],
        prefetch=0,
    )(band_ids.reshape(slots, 1), band_mask.reshape(slots, 1).astype(jnp.float32), wave_table, gen_w1, gen_w2)


def embed_kernel(count, place, kernel_ref, table_ref, gain_ref, weight_ref, *refs):
    pieces, (start_ref, normed_ref, out_ref) = refs[:count], refs[count:]
    rows = pieces[0].shape[0]
    sensor = lax.broadcasted_iota(jnp.int32, table_ref.shape, 0) == place[1]
    start = jnp.sum(
        jnp.where(sensor, table_ref[...].astype(jnp.float32), 0.0), axis=0, keepdims=True
    )
    for m, piece in enumerate(pieces):
        first = pl.multiple_of((place[0] ^ m) * rows, rows)
        start = start + dot32(piece[...], kernel_ref[pl.ds(first, rows), :], ROWS)
    start_ref[...] = start
    normed = (units(start)[0] * gain_ref[...]).astype(low)
    normed_ref[...] = normed
    out_ref[...] = jnp.dot(normed, weight_ref[...], preferred_element_type=jnp.float32).astype(low)


def embed(place, kernel, sensor_table, gain, weight, pieces):
    rows, tokens = pieces[0].shape
    width = weight.shape[0]
    return call(
        functools.partial(embed_kernel, len(pieces)),
        "embed",
        (tokens // BLOCK,),
        [whole(kernel.shape), whole(sensor_table.shape), whole((1, width)), whole(weight.shape)]
        + [pl.BlockSpec((rows, BLOCK), lambda i, s: (0, i))] * len(pieces),
        [
            pl.BlockSpec((BLOCK, width), lambda i, s: (i, 0)),
            pl.BlockSpec((BLOCK, width), lambda i, s: (i, 0)),
            pl.BlockSpec((BLOCK, 3 * width), lambda i, s: (i, 0)),
        ],
        [
            shape_of(tokens, width),
            shape_of(tokens, width, dtype=low),
            shape_of(tokens, 3 * width, dtype=low),
        ],
        2 * tokens * width * (kernel.shape[0] + 3 * width),
        14 * tokens * width + 2 * weight.size,
    )(place, kernel, sensor_table, gain.reshape(1, width), weight, *pieces)


def turn(step, groups, place):
    half = groups // 2
    core = place[0] % 2
    return (step % half) * 2 + jnp.where(step < half, 1 - core, core)


def by_rows(tokens, work):
    def one(i, carry):
        work(pl.ds(pl.multiple_of(i * BLOCK, BLOCK), BLOCK))
        return carry

    lax.fori_loop(0, tokens // BLOCK, one, 0, unroll=True)


def mlp_kernel(
    blocks,
    groups,
    place,
    start_ref,
    mixed_ref,
    grad_ref,
    proj_ref,
    gain_ref,
    w1_ref,
    w2_ref,
    encoded_ref,
    out_ref,
    mixed_out_ref,
    sum_ref,
    send2_ref,
    keep2_ref,
    send1_ref,
    keep1_ref,
    afters,
    totals,
    mixes,
    norms,
    act,
    hidden,
    back,
    sem,
):
    step = pl.program_id(0)
    tokens, width = afters.shape
    half = groups // 2
    last = blocks + groups
    write = pltpu.make_async_copy(totals, encoded_ref, sem)

    @pl.when(step < blocks)
    def _():
        rows = pl.ds(pl.multiple_of(step * BLOCK, BLOCK), BLOCK)
        mixed = mixed_ref[...]
        mixes[rows, :] = mixed
        after = start_ref[...] + jnp.dot(mixed, proj_ref[...], preferred_element_type=jnp.float32)
        afters[rows, :] = after
        totals[rows, :] = after
        norms[rows, :] = (units(after)[0] * gain_ref[...]).astype(low)
        back[rows, :] = jnp.zeros_like(after)

    @pl.when(jnp.logical_and(step >= blocks, step < last))
    def _():
        def work(rows):
            up = jnp.dot(norms[rows, :], w1_ref[...], preferred_element_type=jnp.float32)
            value, slope = gelu_both(up)
            value = value.astype(low)
            act[rows, :] = value
            totals[rows, :] += jnp.dot(value, w2_ref[...], preferred_element_type=jnp.float32)
            grad = (slope * dot32(grad_ref[rows, :], w2_ref[...], LANES)).astype(low)
            hidden[rows, :] = grad
            back[rows, :] += dot32(grad, w1_ref[...], LANES)

        by_rows(tokens, work)
        term2 = dot32(act[...], grad_ref[...], ROWS).astype(low)
        term1 = dot32(hidden[...], norms[...], ROWS)
        many = CUTS // groups
        rows = term1.shape[0] // many
        term1 = term1.reshape(many, rows, width).astype(low)
        first = (step - blocks) % half * many

        @pl.when(step < blocks + half)
        def _():
            send2_ref[...] = term2
            send1_ref[pl.ds(first, many), :rows, :] = term1

        @pl.when(step >= blocks + half)
        def _():
            keep2_ref[...] = term2
            keep1_ref[pl.ds(first, many), :rows, :] = term1

    @pl.when(step == last)
    def _():
        write.start()
        sum_ref[...] = jnp.zeros_like(sum_ref)

    @pl.when(jnp.logical_and(step >= last, step < last + blocks))
    def _():
        rows = pl.ds(pl.multiple_of((step - last) * BLOCK, BLOCK), BLOCK)
        unit, inverse = units(afters[rows, :])
        grad_rows = back[rows, :]
        grad = grad_ref[rows, :].astype(jnp.float32) + norm_back(
            grad_rows, unit, inverse, gain_ref[...]
        )
        out_ref[...] = grad
        grad_low = grad.astype(low)
        norms[rows, :] = grad_low
        mixed_out_ref[...] = dot32(grad_low, proj_ref[...], LANES).astype(low)
        sum_ref[0:1, :] += jnp.sum(grad_rows * unit, axis=0, keepdims=True)

    @pl.when(step == last + blocks)
    def _():
        many = CUTS // groups
        term = dot32(norms[...], mixes[...], ROWS)
        term = term.reshape(groups, many, width // CUTS, width).astype(low)
        rows = send1_ref.shape[1] - width // CUTS
        for group in range(groups):
            mine = place[0] % 2 == group % 2
            spot = slice(group // 2 * many, (group // 2 + 1) * many)

            @pl.when(mine)
            def _():
                keep1_ref[spot, rows:, :] = term[group]

            @pl.when(jnp.logical_not(mine))
            def _():
                send1_ref[spot, rows:, :] = term[group]

        write.wait()


def mlp_pass(place, start, mixed, out_grad, proj, gain, fc1, fc2, groups):
    tokens, width = start.shape
    wide = fc1.shape[1]
    size = wide // groups
    half = groups // 2
    blocks = tokens // BLOCK

    def once(shape):
        return pl.BlockSpec(shape, lambda *_: (0,) * len(shape), pipeline_mode=pl.Buffered(1))

    def chunk(i, s):
        return turn(jnp.clip(i - blocks, 0, groups - 1), groups, s)

    def part(first):
        return pl.BlockSpec(
            (size, width), lambda i, s: (jnp.clip(i - blocks - first, 0, half - 1), 0)
        )

    def rows_from(first):
        return pl.BlockSpec((BLOCK, width), lambda i, s: (jnp.clip(i - first, 0, blocks - 1), 0))

    halves = shape_of(wide // 2, width, dtype=low)
    joint = (CUTS // 2, (wide + width) // CUTS, width)
    full_low, full = (pltpu.VMEM((tokens, width), kind) for kind in (low, jnp.float32))
    return call(
        functools.partial(mlp_kernel, blocks, groups),
        "mlp_pass",
        (2 * blocks + groups + 1,),
        [rows_from(0), rows_from(0), once((tokens, width)), once(proj.shape), once((1, width))]
        + [
            pl.BlockSpec((width, size), lambda i, s: (0, chunk(i, s))),
            pl.BlockSpec((size, width), lambda i, s: (chunk(i, s), 0)),
        ],
        [pl.BlockSpec(memory_space=pl.ANY)]
        + [rows_from(blocks + groups), rows_from(blocks + groups), once((8, width))]
        + [part(0), part(half), once(joint), once(joint)],
        [
            shape_of(tokens, width),
            shape_of(tokens, width),
            shape_of(tokens, width, dtype=low),
            shape_of(8, width),
        ]
        + [halves, halves] + [shape_of(*joint, dtype=low)] * 2,
        2 * tokens * width * (3 * width + 6 * wide),
        20 * tokens * width + 8 * fc1.size,
        [full, full, full_low, full_low]
        + [pltpu.VMEM((tokens, size), low)] * 2
        + [full, pltpu.SemaphoreType.DMA],
        vmem=VM,
    )(place, start, mixed, out_grad, proj, gain.reshape(1, width), fc1, fc2)


def start_kernel(blocks, groups, place, *refs):
    back_refs, left_refs, refs = refs[:PARTS], refs[PARTS : 2 * PARTS], refs[2 * PARTS :]
    weight_ref, start_ref, gain_ref, grad_ref, normed_ref = refs[:5]
    out_ref, sum_ref, keep_ref, send_ref = refs[5:]
    step = pl.program_id(0)
    width = start_ref.shape[1]

    @pl.when(step == 0)
    def _():
        sum_ref[...] = jnp.zeros_like(sum_ref)

    @pl.when(step < blocks)
    def _():
        back = 0.0
        for i, back_ref in enumerate(back_refs):
            some = back_ref.shape[2]
            for j in range(3):
                first = j * width + i * some
                back = back + dot32(back_ref[j], weight_ref[:, first : first + some], LANES)
        unit, inverse = units(start_ref[...])
        grad = grad_ref[...] + norm_back(back, unit, inverse, gain_ref[...])
        out_ref[...] = grad.astype(low)
        sum_ref[0:1, :] += jnp.sum(back * unit, axis=0, keepdims=True)
        sum_ref[1:2, :] += jnp.sum(grad, axis=0, keepdims=True)

    @pl.when(step >= blocks)
    def _():
        left = jnp.concatenate([ref[0] for ref in left_refs], axis=1)
        term = dot32(left, normed_ref[...], ROWS).astype(low)
        each = 3 * width // groups // UNIT
        for u in range(width // UNIT):
            unit = (step - blocks) * (width // UNIT) + u
            group = unit // each
            first = pl.multiple_of(((group // 2) * each + unit % each) * UNIT, UNIT)
            mine = group % 2 == place[0] % 2
            part = term[u * UNIT : (u + 1) * UNIT]

            @pl.when(mine)
            def _():
                keep_ref[pl.ds(first, UNIT), :] = part

            @pl.when(jnp.logical_not(mine))
            def _():
                send_ref[pl.ds(first, UNIT), :] = part


def start_pass(place, backs, weight, start, gain, grad_after, normed, groups, behind):
    tokens, width = start.shape
    blocks = tokens // BLOCK

    def row_block(i):
        return jnp.minimum(i, blocks - 1)

    block = pl.BlockSpec((BLOCK, width), lambda i, s: (row_block(i), 0))
    half = (3 * width // 2, width)
    return call(
        functools.partial(start_kernel, blocks, groups),
        "start_pass",
        (blocks + 3,),
        [pl.BlockSpec((3, BLOCK, width // PARTS), lambda i, s: (0, row_block(i), 0))] * PARTS
        + [
            pl.BlockSpec(
                (1, tokens, width // PARTS), lambda i, s: (jnp.maximum(i - blocks, 0), 0, 0)
            )
        ]
        * PARTS
        + [whole(weight.shape), block, whole((1, width)), block, whole(normed.shape)],
        [block, whole((8, width)), whole(half), whole(half)],
        [
            shape_of(tokens, width, dtype=low),
            shape_of(8, width),
            shape_of(*half, dtype=low),
            shape_of(*half, dtype=low),
        ],
        12 * tokens * width * width,
        24 * tokens * width + 2 * weight.size,
        behind=behind,
    )(place, *backs, *backs, weight, start, gain.reshape(1, width), grad_after, normed)


def patch_kernel(count, slots, place, *refs):
    pieces, refs = refs[:count], refs[count:]
    grad_ref, kernel_ref, w2_ref, sum1_ref, sum2_ref, ids_ref, mask_ref = refs[:7]
    keep_ref, send_ref, small_ref, pixel_ref, lines, both, hidden, small = refs[7:]
    step = pl.program_id(0)
    width = grad_ref.shape[1]
    codes = hidden.shape[1]

    @pl.when(step == 0)
    def _():
        patch_terms(place, slots, grad_ref, pieces, keep_ref, send_ref, both, lines)
        hidden[...] = jnp.zeros_like(hidden)

    @pl.when(step > 0)
    def _():
        pixel_ref[0] = dot32(kernel_ref[...], grad_ref[...], LANES).astype(low)
        total = hidden[...]
        for p in range(both.shape[1] // slots):
            total = total + dot32(
                both[step - 1, p * slots : (p + 1) * slots, :],
                w2_ref[:, p * width : (p + 1) * width],
                LANES,
            )
        hidden[...] = total

    @pl.when(step == count)
    def _():
        first = jnp.where(place[0] == 0, 1.0, 0.0)
        rows = small.shape[0]
        small[...] = jnp.zeros_like(small)
        small[:slots, :codes] = hidden[...] * mask_ref[...]
        small[:slots, codes : 2 * codes] = jnp.broadcast_to(ids_ref[...] * first, (slots, codes))
        small[slots : slots + 2, :] = sum1_ref[0:2, :]
        small[slots + 2 : slots + 3, :] = sum2_ref[0:1, :]
        small[slots + 3 : slots + 4, :] = jnp.full((1, width), place[1].astype(jnp.float32) * first)
        small_low = small[...].astype(low)
        small_ref[...] = small_low
        send_ref[send_ref.shape[0] - rows :, :] = small_low


def patch_terms(place, slots, grads, pieces, keep_ref, send_ref, all_ref, lines):
    count = len(pieces)
    rows = pieces[0].shape[0]
    per = slots // count
    pixels = rows // per
    width = grads.shape[1]
    for m, piece in enumerate(pieces):
        term = jnp.dot(piece[...], grads[...], preferred_element_type=jnp.float32)
        for s in range(per):
            slot = (place[0] ^ m) * per + s
            for c in range(0, width, 128):
                lines[c // 128, pl.ds(slot, pixels, stride=slots), :] = term[
                    s * pixels : (s + 1) * pixels, c : c + 128
                ]
    span = pixels * slots // count
    for j in range(count):
        mine = (place[0] & 1) == j % 2
        for c in range(0, width, 128):
            part = lines[c // 128, j * span : (j + 1) * span, :].astype(low)
            all_ref[j, :, c : c + 128] = part

        @pl.when(mine)
        def _():
            keep_ref[j // 2] = all_ref[j]

        @pl.when(jnp.logical_not(mine))
        def _():
            send_ref[j // 2 * span : (j // 2 + 1) * span, :] = all_ref[j]


def patch_pass(place, pieces, grad_embed, kernel, gen_w2, sum1, sum2, ids_column, mask_column, behind):
    rows, tokens = pieces[0].shape
    count = len(pieces)
    width = grad_embed.shape[1]
    codes = gen_w2.shape[0]
    slots = ids_column.shape[0]
    span = gen_w2.shape[1] // count
    more = -(-(slots + 4) // 16) * 16

    def turned(i):
        return jnp.maximum(i - 1, 0)

    kept = (count // 2, rows, width)
    sent = (count // 2 * rows + more, width)
    return call(
        functools.partial(patch_kernel, count, slots),
        "patch_pass",
        (1 + count,),
        [whole(pieces[0].shape)] * count
        + [
            whole(grad_embed.shape),
            pl.BlockSpec((rows, width), lambda i, s: (s[0] ^ turned(i), 0)),
            pl.BlockSpec((codes, span), lambda i, s: (0, turned(i))),
            whole((8, width)),
            whole((8, width)),
            whole((slots, 1)),
            whole((slots, 1)),
        ],
        [
            whole(kept),
            whole(sent),
            whole((more, width)),
            pl.BlockSpec((1, rows, tokens), lambda i, s: (turned(i), 0, 0)),
        ],
        [
            shape_of(*kept, dtype=low),
            shape_of(*sent, dtype=low),
            shape_of(more, width, dtype=low),
            shape_of(count, rows, tokens, dtype=low),
        ],
        4 * tokens * width * rows * count,
        2 * (tokens * width + gen_w2.size) + 6 * rows * count * (width + tokens),
        [
            pltpu.VMEM((width // 128, rows * count + slots, 128), jnp.float32),
            pltpu.VMEM((count, rows, width), low),
            pltpu.VMEM((slots, codes), jnp.float32),
            pltpu.VMEM((more, width), jnp.float32),
        ],
        behind=behind,
    )(
        place,
        *pieces,
        grad_embed,
        kernel,
        gen_w2,
        sum1,
        sum2,
        ids_column,
        mask_column,
    )


def join_kernel(place, *refs):
    out_ref = refs[-1]
    for m, piece in enumerate(refs[:-1]):

        @pl.when(pl.program_id(0) == m)
        def _():
            out_ref[...] = piece[...].astype(jnp.float32)


def join_pixels(place, pieces, behind):
    rows, tokens = pieces[0].shape
    count = len(pieces)
    return call(
        join_kernel,
        "join_pixels",
        (count,),
        [whole(pieces[0].shape)] * count,
        pl.BlockSpec((rows, tokens), lambda i, s: (0, s[0] ^ i)),
        shape_of(rows, count * tokens),
        0,
        6 * rows * count * tokens,
        behind=behind,
    )(place, *pieces)


def finish_kernel(slots, sensors, place, small_ref, rows_ref, table_ref, w1_ref, wave_ref, gen1_ref, gen2_ref, sensor_ref, norm_ref):
    groups = small_ref.shape[0]
    bands, codes = wave_ref.shape
    table, weight = table_ref[...], w1_ref[...]
    width = norm_ref.shape[1]

    def picked(q):
        return small_ref[q, :slots, codes : codes + bands].astype(jnp.float32).astype(jnp.int32)

    ids = [picked(q) for q in range(groups)]
    hidden = code_rows(jnp.concatenate(ids, axis=0), table, weight)[2].astype(low)
    for i in range(rows_ref.shape[0]):
        wide = rows_ref.shape[2]
        gen2_ref[:, i * wide : (i + 1) * wide] = dot32(hidden, rows_ref[i], ROWS)

    in_order = [place[2] ^ g for g in range(groups)]
    ids = [picked(q) for q in in_order]
    select, rows, _, slope = code_rows(jnp.concatenate(ids, axis=0), table, weight)
    grad = jnp.concatenate(
        [small_ref[q, :slots, :codes].astype(jnp.float32) for q in in_order], axis=0
    )
    scaled = slope * grad
    gen1_ref[...] = lax.dot_general(
        rows, scaled, ROWS, precision=highest, preferred_element_type=jnp.float32
    )
    row_grad = grad + lax.dot_general(
        scaled,
        weight.astype(jnp.float32),
        LANES,
        precision=highest,
        preferred_element_type=jnp.float32,
    )
    wave_ref[...] = lax.dot_general(
        select, row_grad, ROWS, precision=highest, preferred_element_type=jnp.float32
    )
    norms = [jnp.zeros((1, width), jnp.float32)] * 2
    each = [jnp.zeros((1, width), jnp.float32)] * sensors
    for q in in_order:
        lines = small_ref[q, slots : slots + 8, :].astype(jnp.float32)
        norms = [norms[0] + lines[0:1], norms[1] + lines[2:3]]
        for s in range(sensors):
            each[s] = each[s] + jnp.where(lines[3:4] == float(s), lines[1:2], 0.0)
    for n in range(2):
        norm_ref[n : n + 1, :] = norms[n]
    for s in range(sensors):
        sensor_ref[s : s + 1, :] = each[s]


def finish(place, small, rows, wave_table, gen_w1, slots, sensors, width):
    codes = wave_table.shape[1]
    shapes = [
        wave_table.shape,
        gen_w1.shape,
        (codes, rows.shape[0] * rows.shape[2]),
        (sensors, width),
        (2, width),
    ]
    return call(
        functools.partial(finish_kernel, slots, sensors),
        "finish",
        (1,),
        [whole(small.shape), whole(rows.shape), whole(wave_table.shape), whole(gen_w1.shape)],
        [whole(shape) for shape in shapes],
        [shape_of(*shape) for shape in shapes],
        2 * rows.size * codes,
        4 * rows.size,
    )(place, small, rows, wave_table, gen_w1)


def swap(piece, axis, mask):
    count = lax.axis_size(axis)
    return lax.ppermute(piece, axis, [(i, i ^ mask) for i in range(count)])


def bits_of(axis):
    return lax.axis_size(axis).bit_length() - 1


class Scatter:
    def __init__(self, keep, send, bits):
        self.bits = bits
        self.dims = [("band", bit) for bit in reversed(range(1, bits_of("band")))] + [
            ("dp", bit) for bit in reversed(range(bits_of("dp")))
        ]
        rows = keep.shape[0] >> len(self.dims)
        shape = (2,) * len(self.dims) + (rows, keep.shape[1])
        got = swap(send, "band", 1)
        self.last = got
        self.parts = [keep.reshape(shape), got.reshape(shape)]

    def columns(self, first, last):
        some = object.__new__(Scatter)
        some.bits = self.bits
        some.dims = list(self.dims)
        some.last = self.last
        some.parts = [part[..., first:last] for part in self.parts]
        return some

    def result(self):
        return sum(part.astype(jnp.float32) for part in self.parts)


def pick(rows, index, dim):
    return lax.dynamic_index_in_dim(rows, index, dim, False, allow_negative_indices=False)


def halve(sums, axis, bit, when=()):
    (mine, other), _ = lax.optimization_barrier((sums[0].bits[axis, bit], when))
    sends = []
    for one in sums:
        dim = one.dims.index((axis, bit))
        one.dims.pop(dim)
        send = sum(
            pick(part, other, dim).astype(jnp.float32)
            for part in one.parts
        )
        sends.append(send.astype(low))
        one.parts = [pick(part, mine, dim) for part in one.parts]
    send = sends[0] if len(sends) == 1 else jnp.concatenate(sends, axis=-2)
    got = swap(send, axis, 1 << bit)
    first = 0
    for one, each in zip(sums, sends):
        rows = each.shape[-2]
        one.parts.append(lax.slice_in_dim(got, first, first + rows, axis=got.ndim - 2))
        one.last = got
        first += rows
    return send


def rounded(rows):
    return lax.reduce_precision(rows, 8, 7).astype(low)


def shards(
    pixels,
    band_ids,
    band_mask,
    sensor_tags,
    segment_ids,
    wave_table,
    gen_w1,
    gen_w2,
    sensor_table,
    ln1_gain,
    qkv_weight,
    proj_weight,
    ln2_gain,
    fc1_weight,
    fc2_weight,
    out_grad,
):
    band_place = lax.axis_index("band")
    dp_place = lax.axis_index("dp")
    band_count = lax.axis_size("band")
    dp_count = lax.axis_size("dp")
    slots_dev = pixels.shape[0]
    slots = band_ids.shape[1]
    tok_dev, model_width = out_grad.shape
    patch_pixels = pixels.shape[2]
    sensors = sensor_table.shape[0]
    part_rows = slots_dev * patch_pixels
    place = jnp.stack([band_place, sensor_tags[0], dp_place]).astype(jnp.int32)

    own_pixels = pixels.transpose(0, 2, 1).reshape(part_rows, -1)
    pieces = []
    for mask in range(band_count):
        piece = lax.dynamic_slice_in_dim(own_pixels, (band_place ^ mask) * tok_dev, tok_dev, 1)
        pieces.append(swap(piece, "band", mask) if mask else piece)

    kernel = generate_kernels(band_ids, band_mask, wave_table, gen_w1, gen_w2, model_width)
    kernel = kernel.reshape(slots * patch_pixels, model_width)
    start_rows, normed1, projected = embed(
        place, kernel, sensor_table, ln1_gain, qkv_weight, pieces
    )
    window = windows(segment_ids)
    query_side, key_side = features(segment_ids)
    bits = {
        (axis, bit): ((at >> bit) & 1, 1 - ((at >> bit) & 1))
        for axis, at in (("band", band_place), ("dp", dp_place))
        for bit in range(bits_of(axis))
    }
    turned_places = [dp_place ^ i for i in range(dp_count)]
    ids_column = band_ids.reshape(slots, 1).astype(jnp.float32)
    mask_column = band_mask.reshape(slots, 1).astype(jnp.float32)
    projected, window, query_side, key_side, bits, turned_places, ids_column, mask_column = (
        lax.optimization_barrier(
            (
                projected,
                window,
                query_side,
                key_side,
                bits,
                turned_places,
                ids_column,
                mask_column,
            )
        )
    )
    attended, totals = attend_forward(projected, segment_ids, window, query_side, key_side)
    encoded, grad_after, grad_attended, norm2_sums, send2, keep2, send1, keep1 = mlp_pass(
        place,
        start_rows,
        attended,
        out_grad,
        proj_weight,
        ln2_gain,
        fc1_weight,
        fc2_weight,
        band_count,
    )
    band_rest = [("band", bit) for bit in range(1, bits_of("band"))]
    dp_rest = [("dp", bit) for bit in range(bits_of("dp"))]
    devices = band_count * dp_count
    fc1_rows = fc1_weight.shape[1] // devices
    if devices != CUTS:
        first = fc1_weight.shape[1] // CUTS
        send1, keep1 = [
            jnp.concatenate(
                [
                    part.reshape(devices // 2, -1, model_width)
                    for part in (joint[:, :first], joint[:, first:])
                ],
                axis=1,
            )
            for joint in (send1, keep1)
        ]
    fc2_sum = Scatter(keep2, send2, bits)
    fc1_sum = Scatter(*[part.reshape(-1, model_width) for part in (keep1, send1)], bits)
    backs = []

    def back_part(behind):
        backs.append(
            attend_back(
                projected,
                segment_ids,
                window,
                query_side,
                key_side,
                grad_attended,
                attended,
                totals,
                len(backs),
                behind,
            )
        )

    back_part([])
    sent = [
        halve([fc2_sum], *band_rest[0], backs[-1]),
        halve([fc1_sum], *dp_rest[0], backs[-1]),
    ]
    for item in band_rest[1:]:
        sent.append(halve([fc2_sum], *item))
    back_part(sent)
    back_part([backs[-1]])
    sent = [halve([fc2_sum], *dp_rest[0], backs[-1])]
    for item in band_rest:
        sent.append(halve([fc1_sum], *item, backs[-1]))
    grad_embed, norm1_sums, keep, send = start_pass(
        place,
        backs,
        qkv_weight,
        start_rows,
        ln1_gain,
        grad_after,
        normed1,
        band_count,
        sent,
    )
    half = model_width // 2
    qkv_sum = Scatter(keep, send, bits)

    keep, send, small, pixel_parts = patch_pass(
        place,
        pieces,
        grad_embed,
        kernel,
        gen_w2,
        norm1_sums,
        norm2_sums,
        ids_column,
        mask_column,
        [],
    )
    qkv_halves = [qkv_sum.columns(0, half), qkv_sum.columns(half, model_width)]
    for item in dp_rest[1:3]:
        halve([fc2_sum], *item, small)
        halve([fc1_sum], *item, small)
    halve(qkv_halves[:1], *dp_rest[0], small)
    halve(qkv_halves[1:], *band_rest[0], small)
    for item in band_rest[1:]:
        halve(qkv_halves[1:], *item)
    more = small.shape[0]
    got = swap(send, "band", 1)
    patch_parts = [keep, got[:-more].reshape(keep.shape)]
    small = small.astype(jnp.float32) + got[-more:].astype(jnp.float32)
    for bit in range(1, bits_of("band")):
        mine, other = bits["band", bit]
        patch_parts = [
            part.reshape((part.shape[0] // 2, 2) + part.shape[1:]) for part in patch_parts
        ]
        away = sum(
            pick(part, other, 1).astype(jnp.float32)
            for part in patch_parts
        ).astype(low)
        patch_parts = [pick(part, mine, 1) for part in patch_parts]
        small_low = rounded(small)
        got = swap(
            jnp.concatenate([away.reshape(-1, model_width), small_low]), "band", 1 << bit
        )
        patch_parts.append(got[:-more].reshape(away.shape))
        small = small_low.astype(jnp.float32) + got[-more:].astype(jnp.float32)
    pixel_pieces = [
        swap(lax.optimization_barrier((pixel_parts[mask], small))[0], "band", mask)
        if mask
        else pixel_parts[0]
        for mask in range(band_count)
    ]
    span = patch_pixels // band_count
    patch_sum = sum(part.astype(jnp.float32) for part in patch_parts).reshape(
        span, slots, model_width
    )
    patch_low = (patch_sum * mask_column[None]).astype(low)
    cuts = max(1, dp_count // span)
    share = model_width // cuts
    if cuts > 1:
        patch_low = patch_low.reshape(span, slots, cuts, share).transpose(0, 2, 1, 3)
    patch_low = patch_low.reshape(dp_count, -1, slots, share)
    held = jnp.stack(
        [pick(patch_low, turned, 0) for turned in turned_places]
    )
    all_small = rounded(small)[None]

    shape = held.shape
    for n, (axis, bit) in enumerate(dp_rest):
        view = held.reshape((dp_count >> (bit + 1), 2, 1 << bit) + shape[1:])
        away = view[:, 1]
        rows = away.size // model_width
        got = swap(
            jnp.concatenate(
                [away.reshape(rows, model_width), all_small.reshape(-1, model_width)]
            ),
            axis,
            1 << bit,
        )
        if n == 0:
            halve(qkv_halves[1:], *dp_rest[0], all_small)
            for item in band_rest:
                halve(qkv_halves[:1], *item, all_small)
        else:
            halve(qkv_halves, axis, bit)
        if n > 2:
            halve([fc2_sum], axis, bit)
            halve([fc1_sum], axis, bit)
        held = jnp.stack([view[:, 0], got[:rows].reshape(away.shape)], axis=1).reshape(shape)
        all_small = jnp.concatenate([all_small, got[rows:].reshape(all_small.shape)])
    kernel_rows = held.transpose(1, 0, 2, 3).reshape(shape[1], dp_count * slots, share)
    wave_table_grad, gen_w1_grad, gen_w2_grad, sensor_grad, norm_grads = finish(
        place, all_small, kernel_rows, wave_table, gen_w1, slots, sensors, model_width
    )
    grad_pixels = join_pixels(place, pixel_pieces, [])
    grad_pixels = grad_pixels.reshape(slots_dev, patch_pixels, -1).transpose(0, 2, 1)
    qkv_grad = jnp.concatenate([part.result() for part in qkv_halves], axis=1)
    fc2_grad, joint = fc2_sum.result(), fc1_sum.result()
    fc1_grad, proj_grad = joint[:fc1_rows], joint[fc1_rows:]
    return (
        encoded,
        grad_pixels,
        wave_table_grad,
        gen_w1_grad,
        gen_w2_grad,
        sensor_grad,
        norm_grads[0],
        qkv_grad.T,
        proj_grad.T,
        norm_grads[1],
        fc1_grad.T,
        fc2_grad,
    )


def solution(mesh):
    return jax.shard_map(
        shards,
        mesh=mesh,
        in_specs=(
            P("band", "dp", None),
            P("dp", None),
            P("dp", None),
            P("dp"),
            P(("dp", "band"), None),
            P(),
            P(),
            P(),
            P(),
            P(),
            P(),
            P(),
            P(),
            P(),
            P(),
            P(("dp", "band"), None),
        ),
        out_specs=(
            P(("dp", "band"), None),
            P("band", "dp", None),
            P(),
            P(),
            P(None, ("band", "dp")),
            P(),
            P(),
            P(None, ("band", "dp")),
            P(None, ("band", "dp")),
            P(),
            P(None, ("band", "dp")),
            P(("band", "dp"), None),
        ),
        check_vma=False,
    )
```
